32 devices in a mesh: kv: 4 (over y, x), seq: 8 (over z, core).
Axes of the slice: x: 2, y: 2, z: 4, core: 2. Of those that a mesh axis runs over, the one named last changes fastest.
Arguments:
- queries: bfloat16 [8192, 4096], P('seq', 'kv'), may hold values from -40 to 40
- query_tangent: bfloat16 [8192, 4096], P('seq', 'kv'), may hold values from -6 to 6
- key_value: bfloat16 [8192, 2, 512], P('seq', None, 'kv'), may hold values from -40 to 40
- key_value_tangents: bfloat16 [8192, 2, 512], P('seq', None, 'kv'), may hold values from -6 to 6
- doc_lengths: int32 [64], replicated, may hold values from 1 to 1024, 8192 in all
- out_weight: bfloat16 [4096, 2048], P(('kv', 'seq')), may hold values from -0.5 to 0.5
- weight_tangent: bfloat16 [4096, 2048], P(('kv', 'seq')), may hold values from -0.25 to 0.25
Outputs:
- layer_out: bfloat16 [8192, 2048], P('seq', 'kv')
- out_tangent: bfloat16 [8192, 2048], P('seq', 'kv')
The draws below stay inside these ranges and needn't reach their ends.
Inputs may be any that keep to these rules, and one draw needn't show every extreme that they name: `doc_lengths`: the 64 lengths sum to 8192; the longest is exactly 1024.
All inputs are finite; a program needn't handle non-finite values.
Results may differ from the reference program's by a relative error of at most 0.0057.
Values may be sent and summed in bfloat16 or wider, within the bound.
No kernel may reach another device: no remote copies, remote signals or barrier semaphores. Data moves between devices by JAX's collectives and lax.ppermute only.
A program may use at most 128 MiB of HBM per device.

```python
import math
import jax
import jax.numpy as jnp
import numpy as np
from jax import lax

D = 2048
QUERY_HEADS = 32
KEY_VALUE_HEADS = 4
HEAD_SIZE = 128
STRETCH = 32
WINDOW = 224
DOC_MOST = 1024
TOKEN_POSITIONS = 8192
NDOCS = 64


def shared_pair(key):
    base = jax.random.fold_in(key, 4711)
    query_random_key, key_value_pairs = jax.random.split(base, 2)
    heads_per_group = QUERY_HEADS // KEY_VALUE_HEADS
    query_sample = jax.random.normal(query_random_key, (TOKEN_POSITIONS, KEY_VALUE_HEADS, heads_per_group, HEAD_SIZE), jnp.float32)
    pair_sample = jax.random.normal(key_value_pairs, (TOKEN_POSITIONS, 2, KEY_VALUE_HEADS, HEAD_SIZE), jnp.float32)
    query_sample = jnp.clip(query_sample, -40.0, 40.0)
    pair_sample = jnp.clip(pair_sample, -40.0, 40.0)
    return (query_sample.reshape(TOKEN_POSITIONS, QUERY_HEADS * HEAD_SIZE), pair_sample.reshape(TOKEN_POSITIONS, 2, KEY_VALUE_HEADS * HEAD_SIZE))


def draw_queries(key, part):
    return shared_pair(key)[0].astype(jnp.bfloat16)


def draw_key_value(key, part):
    return shared_pair(key)[1].astype(jnp.bfloat16)


def with_spikes(values, rng, source, target, shards_of, factor):
    owner, partner = [(jnp.arange(values.shape[dim]) // (values.shape[dim] // shards_of)).reshape([-1 if axis == dim else 1 for axis in range(values.ndim)]) for dim in (source, target)]
    chosen = jax.random.permutation(rng, shards_of)[partner]
    strong = (owner == chosen) | (owner == (partner + shards_of // 2) % shards_of)
    return jnp.where(strong, factor * values, values)


def level_of(rng, extent, cuts, smallest, largest):
    factor_of = 1.0
    for dim, blocks in cuts:
        heights = jax.random.uniform(jax.random.fold_in(jax.random.fold_in(rng, 6), dim), (blocks,), jnp.float32, smallest / len(cuts), largest / len(cuts))
        factor_of = factor_of * jnp.repeat(jnp.exp(heights), extent[dim] // blocks).reshape((-1,) + (1,) * (len(extent) - 1 - dim))
    return factor_of


def profile(number_of, total, most, skew):
    loads = [(1 << 20) // math.isqrt(standing ** skew) + 1 for standing in range(2, number_of + 1)]
    spare, holding = total - most - (number_of - 1), [1] * (number_of - 1)
    while spare > 0:
        candidates = [i for i in range(number_of - 1) if holding[i] < most]
        mass, remaining = sum([loads[i] for i in candidates]), spare
        for i in candidates:
            more = min(most - holding[i], max(1, remaining * loads[i] // mass), spare)
            holding[i] = holding[i] + more
            spare = spare - more
    return np.array([most] + holding)


def uneven_parts(key, amount, total, bound, skew):
    if amount == 2:
        one = jax.random.randint(key, (), max(1, total - bound), min(bound, total - 1) + 1)
        return jnp.stack([one, total - one])
    tallies = jnp.asarray(profile(amount, total, bound, skew), jnp.int32)
    pairs = (amount - 1) // 2
    source_of, receiver = tallies[1:1 + 2 * pairs:2], tallies[2:2 + 2 * pairs:2]
    margin = jnp.minimum(source_of - 1, bound - receiver)
    shifted = jax.random.randint(jax.random.fold_in(key, 1), (pairs,), 0, 1 << 20) % (margin + 1)
    tallies = tallies.at[1:1 + 2 * pairs:2].set(source_of - shifted).at[2:2 + 2 * pairs:2].set(receiver + shifted)
    return tallies[jax.random.permutation(jax.random.fold_in(key, 2), amount)]


def normal_values(stream_key, extent, scale, most, cuts=(), held_as=jnp.bfloat16):
    array = scale * jax.random.normal(stream_key, extent, jnp.float32)
    if cuts:
        array = array * level_of(stream_key, extent, cuts, -0.22, 0.18)
    return jnp.clip(array, -most, most).astype(held_as)


def gaussian_with(rng, extent, deviation, reach, cuts, heavy, kind=jnp.bfloat16):
    values = deviation * jax.random.normal(rng, extent, jnp.float32)
    if cuts:
        values = values * level_of(rng, extent, cuts, -0.22, 0.18)
    return jnp.clip(with_spikes(values, jax.random.fold_in(rng, 3), *heavy), -reach, reach).astype(kind)


def setup_inputs(seed: int = 0) -> dict:
    streams_of = jax.random.split(jax.random.key(seed), 8)
    return {
        "queries": draw_queries(jax.random.fold_in(streams_of[7], 71), 0),
        "query_tangent": normal_values(streams_of[1], (TOKEN_POSITIONS, QUERY_HEADS * HEAD_SIZE), 1.0, 6.0, ((0, 8), (1, 4))),
        "key_value": draw_key_value(jax.random.fold_in(streams_of[7], 71), 0),
        "key_value_tangents": normal_values(streams_of[3], (TOKEN_POSITIONS, 2, KEY_VALUE_HEADS * HEAD_SIZE), 1.0, 6.0, ((0, 8), (2, 4))),
        "doc_lengths": uneven_parts(streams_of[4], NDOCS, TOKEN_POSITIONS, DOC_MOST, 2).astype(jnp.int32),
        "out_weight": gaussian_with(streams_of[5], (QUERY_HEADS * HEAD_SIZE, D), (QUERY_HEADS * HEAD_SIZE // 8) ** -0.5, 0.5, ((0, 32),), (0, 1, 32, 2.75)),
        "weight_tangent": normal_values(streams_of[6], (QUERY_HEADS * HEAD_SIZE, D), (QUERY_HEADS * HEAD_SIZE // 8) ** -0.5, 0.25, ((0, 32),)),
    }


masked_score = -1e+30

def attend(query_block, query_tan, key_rows, value_rows, key_tangent, value_tangent, lower_rel):
    head_dim = key_rows.shape[-1]
    score_scale = 1.0 / math.sqrt(head_dim)
    query_full = query_block.astype(jnp.float32)
    keys_full = key_rows.astype(jnp.float32)
    scores = jnp.einsum('bcgh,brh->bgcr', query_full, keys_full) * score_scale
    tangent = (jnp.einsum('bcgh,brh->bgcr', query_tan.astype(jnp.float32), keys_full) + jnp.einsum('bcgh,brh->bgcr', query_full, key_tangent.astype(jnp.float32))) * score_scale
    columns = jnp.arange(key_rows.shape[1]).astype(jnp.float32)[None, None, None, :]
    row_index = jnp.arange(query_block.shape[1]).astype(jnp.float32)[None, None, :, None]
    admitted = (columns >= lower_rel.astype(jnp.float32)[:, None, :, None]) & (columns <= row_index + WINDOW)
    scores = jnp.where(admitted, scores, masked_score)
    row_peak = lax.optimization_barrier(jnp.max(scores, axis=-1, keepdims=True))
    exponent = jnp.where(admitted, jnp.exp(scores - row_peak), 0.0)
    row_total = lax.optimization_barrier(jnp.sum(exponent, axis=-1, keepdims=True))
    probabilities = exponent / row_total
    tangent = jnp.where(admitted, tangent, 0.0)
    mean_tan = lax.optimization_barrier(jnp.sum(probabilities * tangent, axis=-1, keepdims=True))
    prob_tangent = probabilities * (tangent - mean_tan)
    prob_low = lax.optimization_barrier(probabilities.astype(jnp.bfloat16)).astype(jnp.float32)
    tangent_low = lax.optimization_barrier(prob_tangent.astype(jnp.bfloat16)).astype(jnp.float32)
    values_full = value_rows.astype(jnp.float32)
    outputs = jnp.einsum('bgcr,brh->bcgh', prob_low, values_full)
    out_tan = jnp.einsum('bgcr,brh->bcgh', tangent_low, values_full) + jnp.einsum('bgcr,brh->bcgh', prob_low, value_tangent.astype(jnp.float32))
    return (outputs.astype(jnp.bfloat16), out_tan.astype(jnp.bfloat16))

def reference(queries, query_tangent, key_value, key_value_tangents, doc_lengths, out_weight, weight_tangent):
    doc_ends = jnp.cumsum(doc_lengths).astype(jnp.int32)
    doc_starts = (doc_ends - doc_lengths).astype(jnp.int32)
    position = jnp.arange(TOKEN_POSITIONS, dtype=jnp.int32)
    inside = (doc_starts[None, :] <= position[:, None]) & (position[:, None] < doc_ends[None, :])
    doc_first = lax.optimization_barrier(jnp.sum(jnp.where(inside, doc_starts[None, :], 0), axis=1)).astype(jnp.int32)
    lower_bound = jnp.maximum(doc_first, position - WINDOW + 1).astype(jnp.int32)
    stretch_count = TOKEN_POSITIONS // STRETCH
    stretch_start = (jnp.arange(stretch_count, dtype=jnp.int32) * STRETCH)[:, None]
    lower_rel = (lower_bound.reshape(stretch_count, STRETCH) - (stretch_start - WINDOW)).astype(jnp.int32)
    heads_per_group = QUERY_HEADS // KEY_VALUE_HEADS
    span_count = (WINDOW + STRETCH) // STRETCH
    lead_blocks = WINDOW // STRETCH
    per_step = 32
    step_count = stretch_count // per_step
    attention_parts = []
    tangent_parts = []
    for group_number in range(KEY_VALUE_HEADS):
        low = group_number * HEAD_SIZE
        pair_rows = key_value[:, :, low:low + HEAD_SIZE]
        pair_tan = key_value_tangents[:, :, low:low + HEAD_SIZE]
        stacked = jnp.concatenate([pair_rows[:, 0], pair_rows[:, 1], pair_tan[:, 0], pair_tan[:, 1]], axis=1)
        padded = jnp.concatenate([jnp.zeros((WINDOW, 4 * HEAD_SIZE), jnp.bfloat16), stacked], axis=0)
        padded = padded.reshape(lead_blocks + stretch_count, STRETCH, 4 * HEAD_SIZE)
        windows = jnp.concatenate([padded[offset:offset + stretch_count] for offset in range(span_count)], axis=1)
        qlow = group_number * heads_per_group * HEAD_SIZE
        query_group = queries[:, qlow:qlow + heads_per_group * HEAD_SIZE].reshape(step_count, per_step, STRETCH, heads_per_group, HEAD_SIZE)
        tangent_group = query_tangent[:, qlow:qlow + heads_per_group * HEAD_SIZE].reshape(step_count, per_step, STRETCH, heads_per_group, HEAD_SIZE)
        window_group = windows.reshape(step_count, per_step, span_count * STRETCH, 4 * HEAD_SIZE)
        bound_group = lower_rel.reshape(step_count, per_step, STRETCH)

        def one_step(batch_items):
            query_batch, tangent_batch, window_batch, bound_batch = batch_items
            return attend(query_batch, tangent_batch, window_batch[..., :HEAD_SIZE], window_batch[..., HEAD_SIZE:2 * HEAD_SIZE], window_batch[..., 2 * HEAD_SIZE:3 * HEAD_SIZE], window_batch[..., 3 * HEAD_SIZE:], bound_batch)
        result = lax.map(one_step, (query_group, tangent_group, window_group, bound_group))
        attention_parts.append(result[0].reshape(TOKEN_POSITIONS, heads_per_group * HEAD_SIZE))
        tangent_parts.append(result[1].reshape(TOKEN_POSITIONS, heads_per_group * HEAD_SIZE))
    attention = jnp.concatenate(attention_parts, axis=1)
    attention_tan = jnp.concatenate(tangent_parts, axis=1)
    layer_out = jnp.dot(attention, out_weight, preferred_element_type=jnp.float32).astype(jnp.bfloat16)
    out_tangent = (jnp.dot(attention_tan, out_weight, preferred_element_type=jnp.float32) + jnp.dot(attention, weight_tangent, preferred_element_type=jnp.float32)).astype(jnp.bfloat16)
    return (layer_out, out_tangent)
```

```python
import functools
import math

import jax
import jax.numpy as jnp
from jax import lax
from jax.experimental import pallas as pl
from jax.experimental.pallas import tpu as pltpu
from jax.sharding import PartitionSpec as P

STRETCH = 32
WINDOW = 224
CHUNKS = 2
TILE = 128

masked_score = -1e30


def attention_kernel(heads, head_dim, q_ref, qt_ref, ctx_ref, low_ref, out_ref):
    rows = q_ref.shape[0]
    span = WINDOW + STRETCH
    width = heads * head_dim
    score_scale = 1.0 / math.sqrt(head_dim)
    to_log2 = score_scale * math.log2(math.e)
    step = pl.program_id(0)
    transposed = (((1,), (1,)), ((), ()))
    column = lax.broadcasted_iota(jnp.int32, (STRETCH, span), 1)
    row = lax.broadcasted_iota(jnp.int32, (STRETCH, span), 0)
    causal = column <= row + WINDOW
    for part in range(rows // STRETCH):
        here = slice(part * STRETCH, (part + 1) * STRETCH)
        base = pl.multiple_of(step * rows + part * STRETCH, STRETCH)
        keys = ctx_ref[pl.ds(base, span), : 2 * head_dim]
        values = ctx_ref[pl.ds(base, span), 2 * head_dim :]
        low = low_ref[here, :]
        low = jnp.concatenate([low] * (span // low.shape[1]), axis=1)
        admitted = causal & (column >= low)
        q = jnp.concatenate(
            [q_ref[here, h * head_dim : (h + 1) * head_dim] for h in range(heads)], axis=0
        )
        qt = jnp.concatenate(
            [qt_ref[here, h * head_dim : (h + 1) * head_dim] for h in range(heads)], axis=0
        )
        scores = lax.dot_general(
            q, keys[:, :head_dim], transposed, preferred_element_type=jnp.float32
        )
        tangent = lax.dot_general(
            jnp.concatenate([qt, q], axis=1), keys, transposed, preferred_element_type=jnp.float32
        )
        scores = scores.reshape(heads, STRETCH, span)
        tangent = tangent.reshape(heads, STRETCH, span)
        scores = jnp.where(admitted[None], scores, masked_score)
        peak = jnp.max(scores, axis=-1, keepdims=True)
        exponent = jnp.exp2((scores - peak) * to_log2)
        inverse = 1.0 / jnp.sum(exponent, axis=-1, keepdims=True)
        mean = jnp.sum(exponent * tangent, axis=-1, keepdims=True) * inverse
        prob = exponent * inverse
        prob_low = prob.astype(jnp.bfloat16).reshape(heads * STRETCH, span)
        tan_low = (prob * ((tangent - mean) * score_scale)).astype(jnp.bfloat16)
        tan_low = tan_low.reshape(heads * STRETCH, span)
        both = jnp.dot(prob_low, values, preferred_element_type=jnp.float32)
        more = jnp.dot(tan_low, values[:, :head_dim], preferred_element_type=jnp.float32)
        out = both[:, :head_dim].astype(jnp.bfloat16)
        out_tan = (both[:, head_dim:] + more).astype(jnp.bfloat16)
        for h in range(heads):
            of = slice(h * STRETCH, (h + 1) * STRETCH)
            out_ref[here, h * head_dim : (h + 1) * head_dim] = out[of]
            out_ref[here, width + h * head_dim : width + (h + 1) * head_dim] = out_tan[of]


def attention(queries, query_tangent, context, low):
    tokens, width = queries.shape
    head_dim = context.shape[1] // 4
    heads = width // head_dim
    elements = tokens * heads * (WINDOW + STRETCH)
    return pl.pallas_call(
        functools.partial(attention_kernel, heads, head_dim),
        grid=(tokens // TILE,),
        in_specs=[
            pl.BlockSpec((TILE, width), lambda i: (i, 0)),
            pl.BlockSpec((TILE, width), lambda i: (i, 0)),
            pl.BlockSpec(context.shape, lambda i: (0, 0)),
            pl.BlockSpec((TILE, low.shape[1]), lambda i: (i, 0)),
        ],
        out_specs=pl.BlockSpec((TILE, 2 * width), lambda i: (i, 0)),
        out_shape=jax.ShapeDtypeStruct((tokens, 2 * width), jnp.bfloat16),
        compiler_params=pltpu.CompilerParams(vmem_limit_bytes=48 * 1024 * 1024),
        cost_estimate=pl.CostEstimate(
            flops=12 * elements * head_dim, bytes_accessed=10 * tokens * width, transcendentals=elements
        ),
        name="attention",
    )(queries, query_tangent, context, low)


def across(block, flip):
    size = lax.axis_size("kv")
    return lax.ppermute(block, "kv", [(i, i ^ flip) for i in range(size)])


def relative_columns(weight, kv_index):
    size = lax.axis_size("kv")
    blocks = weight.reshape(weight.shape[0], size, -1)
    return [
        lax.dynamic_index_in_dim(blocks, kv_index ^ r, axis=1, keepdims=False) for r in range(size)
    ]


def body(
    queries, query_tangent, key_value, key_value_tangents, doc_lengths, out_weight, weight_tangent
):
    tokens, width = queries.shape
    head_dim = key_value.shape[2]
    seq_index = lax.axis_index("seq")
    kv_index = lax.axis_index("kv")
    seq_size = lax.axis_size("seq")

    value_blocks = relative_columns(out_weight, kv_index)
    tangent_blocks = relative_columns(weight_tangent, kv_index)
    part = value_blocks[0].shape[1] // CHUNKS
    gathered = []
    for chunk in range(CHUNKS):
        of = slice(chunk * part, (chunk + 1) * part)
        mine = jnp.stack(
            [
                jnp.concatenate([blocks[r][:, of] for r in (1, 3, 2, 0)], axis=1)
                for blocks in (tangent_blocks, value_blocks)
            ]
        )
        whole = lax.all_gather(mine, "seq", axis=1, tiled=True)
        gathered.append(whole.reshape(-1, whole.shape[-1]))

    stacked = jnp.concatenate(
        [key_value[:, 0], key_value_tangents[:, 0], key_value[:, 1], key_value_tangents[:, 1]],
        axis=1,
    )
    prior = lax.ppermute(
        stacked[tokens - WINDOW :], "seq", [(i, i + 1) for i in range(seq_size - 1)]
    )
    context = jnp.concatenate([prior, stacked], axis=0)

    doc_ends = jnp.cumsum(doc_lengths)
    doc_starts = doc_ends - doc_lengths
    position = seq_index * tokens + jnp.arange(tokens, dtype=jnp.int32)
    inside = (doc_starts[None, :] <= position[:, None]) & (position[:, None] < doc_ends[None, :])
    doc_first = jnp.sum(jnp.where(inside, doc_starts[None, :], 0), axis=1)
    lower = jnp.maximum(doc_first, position - WINDOW + 1)
    low = lower - (position // STRETCH * STRETCH - WINDOW)
    low = jnp.broadcast_to(low[:, None], (tokens, 128))

    pair = attention(queries, query_tangent, context, low)

    half = tokens // 2
    finished = []
    for weights in gathered:
        col = weights.shape[1] // 4
        rows = weights.shape[0] // 2

        def project(of, columns):
            value = jnp.dot(
                pair[of, :width], weights[rows:, columns], preferred_element_type=jnp.float32
            )
            tangent = jnp.dot(pair[of], weights[:, columns], preferred_element_type=jnp.float32)
            return jnp.stack([value, tangent])

        first, second = slice(0, half), slice(half, tokens)
        partial = project(slice(0, tokens), slice(0, 4 * col))
        send_x = partial[:, first, : 2 * col].astype(jnp.bfloat16)
        send_y = partial[:, second, col : 3 * col].astype(jnp.bfloat16)
        from_x = across(send_x, 1)
        from_y = across(send_y, 2)
        send_y2 = (partial[:, first, 2 * col : 3 * col] + from_x[:, :, col:]).astype(jnp.bfloat16)
        keep_first = partial[:, first, 3 * col :] + from_x[:, :, :col]
        send_x2 = (partial[:, second, :col] + from_y[:, :, :col]).astype(jnp.bfloat16)
        keep_second = partial[:, second, 3 * col :] + from_y[:, :, col:]
        from_y2 = across(send_y2, 2)
        from_x2 = across(send_x2, 1)
        finished.append(
            jnp.concatenate([keep_first + from_y2, keep_second + from_x2], axis=1).astype(
                jnp.bfloat16
            )
        )
    result = jnp.concatenate(finished, axis=2)
    return result[0], result[1]


def solution(mesh):
    in_specs = (
        P("seq", "kv"),
        P("seq", "kv"),
        P("seq", None, "kv"),
        P("seq", None, "kv"),
        P(),
        P(("kv", "seq"), None),
        P(("kv", "seq"), None),
    )
    out_specs = (P("seq", "kv"), P("seq", "kv"))
    return jax.shard_map(body, mesh=mesh, in_specs=in_specs, out_specs=out_specs, check_vma=False)
```

```python
import functools
import math

import jax
import jax.numpy as jnp
from jax import lax
from jax.experimental import pallas as pl
from jax.experimental.pallas import tpu as pltpu
from jax.sharding import PartitionSpec as P

STRETCH = 32
WINDOW = 224
CHUNKS = 4
TILE = 128
CORES = 2
RELATIVE = (1, 3, 2, 0)

masked_score = -1e30
vmem_bytes = 48 * 1024 * 1024


def arrange_kernel(kv_ref, tangent_ref, value_ref, *chunk_refs):
    columns = tangent_ref.shape[1] // len(RELATIVE)
    part = columns // len(chunk_refs)
    for chunk, chunk_ref in enumerate(chunk_refs):
        for place, flip in enumerate(RELATIVE):
            start = pl.multiple_of((kv_ref[0] ^ flip) * columns + chunk * part, part)
            to = slice(place * part, (place + 1) * part)
            chunk_ref[0, :, to] = tangent_ref[:, pl.ds(start, part)]
            chunk_ref[1, :, to] = value_ref[:, pl.ds(start, part)]


def arrange(kv_index, tangent, value):
    rows, columns = value.shape
    shape = jax.ShapeDtypeStruct((2, rows, columns // CHUNKS), value.dtype)
    return pl.pallas_call(
        arrange_kernel,
        in_specs=[
            pl.BlockSpec(memory_space=pltpu.SMEM),
            pl.BlockSpec(memory_space=pltpu.VMEM),
            pl.BlockSpec(memory_space=pltpu.VMEM),
        ],
        out_specs=[pl.BlockSpec(memory_space=pltpu.VMEM)] * CHUNKS,
        out_shape=[shape] * CHUNKS,
        name="arrange",
    )(kv_index.reshape(1), tangent, value)


def attention_kernel(heads, head_dim, offset, order_ref, q_ref, qt_ref, ctx_ref, low_ref, out_ref):
    rows = q_ref.shape[0]
    span = WINDOW + STRETCH
    width = heads * head_dim
    score_scale = 1.0 / math.sqrt(head_dim)
    to_log2 = score_scale * math.log2(math.e)
    step = pl.program_id(0)
    transposed = (((1,), (1,)), ((), ()))
    column = lax.broadcasted_iota(jnp.int32, (STRETCH, span), 1)
    row = lax.broadcasted_iota(jnp.int32, (STRETCH, span), 0)
    causal = column <= row + WINDOW
    starts = [pl.multiple_of(order_ref[h] * head_dim, head_dim) for h in range(heads)]
    for part in range(rows // STRETCH):
        here = slice(part * STRETCH, (part + 1) * STRETCH)
        base = pl.multiple_of(offset + step * rows + part * STRETCH, STRETCH)
        keys = ctx_ref[pl.ds(base, span), : 2 * head_dim]
        values = ctx_ref[pl.ds(base, span), 2 * head_dim :]
        low = low_ref[here, :]
        low = jnp.concatenate([low] * (span // low.shape[1]), axis=1)
        admitted = causal & (column >= low)
        q = jnp.concatenate([q_ref[here, pl.ds(start, head_dim)] for start in starts], axis=0)
        qt = jnp.concatenate([qt_ref[here, pl.ds(start, head_dim)] for start in starts], axis=0)
        scores = lax.dot_general(
            q, keys[:, :head_dim], transposed, preferred_element_type=jnp.float32
        )
        tangent = lax.dot_general(
            jnp.concatenate([qt, q], axis=1), keys, transposed, preferred_element_type=jnp.float32
        )
        scores = scores.reshape(heads, STRETCH, span)
        tangent = tangent.reshape(heads, STRETCH, span)
        scores = jnp.where(admitted[None], scores, masked_score)
        peak = jnp.max(scores, axis=-1, keepdims=True)
        exponent = jnp.exp2((scores - peak) * to_log2)
        inverse = 1.0 / jnp.sum(exponent, axis=-1, keepdims=True)
        mean = jnp.sum(exponent * tangent, axis=-1, keepdims=True) * inverse
        prob = exponent * inverse
        prob_low = prob.astype(jnp.bfloat16).reshape(heads * STRETCH, span)
        tan_low = (prob * ((tangent - mean) * score_scale)).astype(jnp.bfloat16)
        tan_low = tan_low.reshape(heads * STRETCH, span)
        both = jnp.dot(prob_low, values, preferred_element_type=jnp.float32)
        more = jnp.dot(tan_low, values[:, :head_dim], preferred_element_type=jnp.float32)
        out = both[:, :head_dim].astype(jnp.bfloat16)
        out_tan = (both[:, head_dim:] + more).astype(jnp.bfloat16)
        for h in range(heads):
            of = slice(h * STRETCH, (h + 1) * STRETCH)
            out_ref[here, h * head_dim : (h + 1) * head_dim] = out[of]
            out_ref[here, width + h * head_dim : width + (h + 1) * head_dim] = out_tan[of]


def attention(half, order, queries, query_tangent, context, low):
    tokens, width = queries.shape[0] // 2, queries.shape[1]
    head_dim = context.shape[1] // 4
    heads = width // head_dim
    elements = tokens * heads * (WINDOW + STRETCH)
    steps = tokens // TILE
    offset = context.shape[0] - tokens - WINDOW
    return pl.pallas_call(
        functools.partial(attention_kernel, heads, head_dim, offset),
        grid=(steps,),
        in_specs=[
            pl.BlockSpec(memory_space=pltpu.SMEM),
            pl.BlockSpec((TILE, width), lambda i: (half * steps + i, 0)),
            pl.BlockSpec((TILE, width), lambda i: (half * steps + i, 0)),
            pl.BlockSpec(context.shape, lambda i: (0, 0)),
            pl.BlockSpec((TILE, low.shape[1]), lambda i: (half * steps + i, 0)),
        ],
        out_specs=pl.BlockSpec((TILE, 2 * width), lambda i: (i, 0)),
        out_shape=jax.ShapeDtypeStruct((tokens, 2 * width), jnp.bfloat16),
        compiler_params=pltpu.CompilerParams(vmem_limit_bytes=vmem_bytes),
        cost_estimate=pl.CostEstimate(
            flops=elements, bytes_accessed=tokens, transcendentals=0
        ),
        name="attention",
    )(order, queries, query_tangent, context, low)


def project_kernel(sent, kept, pair_ref, near_ref, far_ref, send_ref, keep_ref):
    depth = near_ref.shape[1]
    part = near_ref.shape[2] // len(RELATIVE)
    dot = functools.partial(jnp.dot, preferred_element_type=jnp.float32)
    near, near_tan = pair_ref[:, :depth], pair_ref[:, 2 * depth : 3 * depth]
    far, far_tan = pair_ref[:, depth : 2 * depth], pair_ref[:, 3 * depth :]
    value = dot(near, near_ref[1]) + dot(far, far_ref[1])
    tangent = dot(near, near_ref[0]) + dot(far, far_ref[0])
    tangent = tangent + dot(near_tan, near_ref[1]) + dot(far_tan, far_ref[1])
    for ref, flips in ((send_ref, sent), (keep_ref, kept)):
        for place, flip in enumerate(flips):
            at = RELATIVE.index(flip) * part
            to = slice(place * part, (place + 1) * part)
            ref[0, :, to] = value[:, at : at + part].astype(ref.dtype)
            ref[1, :, to] = tangent[:, at : at + part].astype(ref.dtype)


def project(sent, kept, pair, near, far):
    tokens, width = pair.shape
    tile = min(2 * TILE, tokens)
    steps = tokens // tile
    columns = near.shape[2]
    out = (2, tokens, columns // 2)
    block = pl.BlockSpec((2, tile, columns // 2), lambda i: (0, i, 0))
    return pl.pallas_call(
        functools.partial(project_kernel, sent, kept),
        grid=(steps,),
        in_specs=[
            pl.BlockSpec((tile, width), lambda i: (i, 0)),
            pl.BlockSpec(near.shape, lambda i: (0, 0, 0)),
            pl.BlockSpec(far.shape, lambda i: (0, 0, 0)),
        ],
        out_specs=[block, block],
        out_shape=[
            jax.ShapeDtypeStruct(out, jnp.bfloat16),
            jax.ShapeDtypeStruct(out, jnp.float32),
        ],
        compiler_params=pltpu.CompilerParams(vmem_limit_bytes=vmem_bytes),
        cost_estimate=pl.CostEstimate(
            flops=tokens * columns, bytes_accessed=tokens, transcendentals=0
        ),
        name="project",
    )(pair, near, far)


def across(block, flip):
    size = lax.axis_size("kv")
    return lax.ppermute(block, "kv", [(i, i ^ flip) for i in range(size)])


def along(block, chips):
    size = lax.axis_size("seq")
    return lax.ppermute(block, "seq", [(i, (i + CORES * chips) % size) for i in range(size)])


def other_core(block):
    return lax.ppermute(block, "seq", [(i, i ^ 1) for i in range(lax.axis_size("seq"))])


def hold(block, *until):
    return lax.optimization_barrier((block, *until))[0]


class Gather:
    def __init__(self, mine, chips):
        self.ahead, self.behind = [mine], [mine]
        self.forward, self.backward = chips // 2, (chips - 1) // 2

    def neighbours(self, *until):
        mine = hold(self.ahead[0], *until) if until else self.ahead[0]
        if self.forward:
            self.ahead.append(along(mine, 1))
        if self.backward:
            self.behind.append(along(mine, -1))

    def farther(self, *until):
        for _ in range(self.forward - 1):
            self.ahead.append(along(hold(self.ahead[-1], *until), 1))
        for _ in range(self.backward - 1):
            self.behind.append(along(hold(self.behind[-1], *until), -1))

    def finish(self):
        near = jnp.concatenate(self.ahead + self.behind[:0:-1], axis=1)
        return near, other_core(near)


def body(
    queries, query_tangent, key_value, key_value_tangents, doc_lengths, out_weight, weight_tangent
):
    tokens, width = queries.shape
    head_dim = key_value.shape[2]
    heads = width // head_dim
    half = tokens // 2
    seq_index = lax.axis_index("seq")
    kv_index = lax.axis_index("kv")
    seq_size = lax.axis_size("seq")
    chips = seq_size // CORES

    stacked = jnp.concatenate(
        [key_value[:, 0], key_value_tangents[:, 0], key_value[:, 1], key_value_tangents[:, 1]],
        axis=1,
    )
    prior = lax.ppermute(
        stacked[tokens - WINDOW :], "seq", [(i, i + 1) for i in range(seq_size - 1)]
    )
    context = jnp.concatenate([prior, stacked[:half]], axis=0)

    mine = arrange(kv_index, weight_tangent, out_weight)
    gathers = [Gather(block, chips) for block in mine]
    gathers[0].neighbours()
    gathers[1].neighbours()

    doc_ends = jnp.cumsum(doc_lengths)
    doc_starts = doc_ends - doc_lengths
    position = seq_index * tokens + jnp.arange(tokens, dtype=jnp.int32)
    inside = (doc_starts[None, :] <= position[:, None]) & (position[:, None] < doc_ends[None, :])
    doc_first = jnp.sum(jnp.where(inside, doc_starts[None, :], 0), axis=1)
    lower = jnp.maximum(doc_first, position - WINDOW + 1)
    low = lower - (position // STRETCH * STRETCH - WINDOW)
    low = jnp.broadcast_to(low[:, None], (tokens, 128))

    step = jnp.arange(chips, dtype=jnp.int32)
    chip, core = seq_index // CORES, seq_index % CORES
    owner = (chip - step + chips) % chips * CORES
    order = jnp.concatenate([owner + core, owner + 1 - core])
    whole_heads = order.shape[0] == heads

    def attend(part, context):
        heads_order = order if whole_heads else jnp.arange(heads, dtype=jnp.int32)
        pair = attention(part, heads_order, queries, query_tangent, context, low)
        if not whole_heads:
            pair = jnp.take(pair.reshape(half, 2, seq_size, -1), order, axis=2)
            pair = pair.reshape(half, 2 * width)
        return pair

    pair_second = attend(1, stacked)
    gathers[0].farther(pair_second)
    pair_first = attend(0, hold(context, pair_second))
    gathers[2].neighbours(pair_first)
    gathers[1].farther(pair_first)

    def first_stage(near, far, *until):
        pair = hold(pair_first, *until) if until else pair_first
        send_x, keep_x = project((1, 3), (2, 0), pair, near, far)
        from_x = across(send_x, 1)
        pair = hold(pair_second, send_x)
        send_y, keep_y = project((2, 3), (1, 0), pair, near, far)
        from_y = across(send_y, 2)
        return keep_x, from_x, keep_y, from_y

    def second_stage(keep_x, from_x, keep_y, from_y):
        part = keep_x.shape[2] // 2
        send_y2 = (keep_x[:, :, :part] + from_x[:, :, part:]).astype(jnp.bfloat16)
        from_y2 = across(send_y2, 2)
        send_x2 = (keep_y[:, :, :part] + from_y[:, :, part:]).astype(jnp.bfloat16)
        from_x2 = across(send_x2, 1)
        first = keep_x[:, :, part:] + from_x[:, :, :part] + from_y2
        second = keep_y[:, :, part:] + from_y[:, :, :part] + from_x2
        return jnp.concatenate([first, second], axis=1).astype(jnp.bfloat16)

    staged = []
    for chunk, gathering in enumerate(gathers):
        near, far = gathering.finish()
        now = first_stage(near, far)
        staged.append(now)
        if chunk + 1 < CHUNKS and chunk:
            gathers[chunk + 1].farther(now[0])
        if chunk + 3 < CHUNKS:
            gathers[chunk + 3].neighbours(now[0])
        if chunk:
            last = staged[chunk - 1]
            staged[chunk - 1] = (last[0], hold(last[1], now[0]), last[2], hold(last[3], now[2]))

    finished = [second_stage(*now) for now in staged]
    result = jnp.concatenate(finished, axis=2)
    return result[0], result[1]


def solution(mesh):
    in_specs = (
        P("seq", "kv"),
        P("seq", "kv"),
        P("seq", None, "kv"),
        P("seq", None, "kv"),
        P(),
        P(("kv", "seq"), None),
        P(("kv", "seq"), None),
    )
    out_specs = (P("seq", "kv"), P("seq", "kv"))
    return jax.shard_map(body, mesh=mesh, in_specs=in_specs, out_specs=out_specs, check_vma=False)
```

```python
import functools
import math

import jax
import jax.numpy as jnp
from jax import lax
from jax.experimental import pallas as pl
from jax.experimental.pallas import tpu as pltpu
from jax.sharding import PartitionSpec as P

STRETCH = 32
WINDOW = 224
CHUNKS = 4
TILE = 128
CORES = 2
RELATIVE = (1, 3, 2, 0)

masked_score = -1e30
vmem_bytes = 48 * 1024 * 1024


def arrange_kernel(kv_ref, tangent_ref, value_ref, *chunk_refs):
    columns = tangent_ref.shape[1] // len(RELATIVE)
    part = columns // len(chunk_refs)
    for chunk, chunk_ref in enumerate(chunk_refs):
        for place, flip in enumerate(RELATIVE):
            start = pl.multiple_of((kv_ref[0] ^ flip) * columns + chunk * part, part)
            to = slice(place * part, (place + 1) * part)
            chunk_ref[0, :, to] = tangent_ref[:, pl.ds(start, part)]
            chunk_ref[1, :, to] = value_ref[:, pl.ds(start, part)]


def arrange(kv_index, tangent, value):
    rows, columns = value.shape
    shape = jax.ShapeDtypeStruct((2, rows, columns // CHUNKS), value.dtype)
    return pl.pallas_call(
        arrange_kernel,
        in_specs=[
            pl.BlockSpec(memory_space=pltpu.SMEM),
            pl.BlockSpec(memory_space=pltpu.VMEM),
            pl.BlockSpec(memory_space=pltpu.VMEM),
        ],
        out_specs=[pl.BlockSpec(memory_space=pltpu.VMEM)] * CHUNKS,
        out_shape=[shape] * CHUNKS,
        name="arrange",
    )(kv_index.reshape(1), tangent, value)


def attention_kernel(heads, head_dim, offset, order_ref, q_ref, qt_ref, ctx_ref, low_ref, out_ref):
    rows = q_ref.shape[0]
    span = WINDOW + STRETCH
    width = heads * head_dim
    score_scale = 1.0 / math.sqrt(head_dim)
    to_log2 = score_scale * math.log2(math.e)
    step = pl.program_id(0)
    transposed = (((1,), (1,)), ((), ()))
    column = lax.broadcasted_iota(jnp.int32, (STRETCH, span), 1)
    row = lax.broadcasted_iota(jnp.int32, (STRETCH, span), 0)
    causal = column <= row + WINDOW
    starts = [pl.multiple_of(order_ref[h] * head_dim, head_dim) for h in range(heads)]
    for part in range(rows // STRETCH):
        here = slice(part * STRETCH, (part + 1) * STRETCH)
        base = pl.multiple_of(offset + step * rows + part * STRETCH, STRETCH)
        keys = ctx_ref[pl.ds(base, span), : 2 * head_dim]
        values = ctx_ref[pl.ds(base, span), 2 * head_dim :]
        low = low_ref[here, :]
        low = jnp.concatenate([low] * (span // low.shape[1]), axis=1)
        admitted = causal & (column >= low)
        q = jnp.concatenate([q_ref[here, pl.ds(start, head_dim)] for start in starts], axis=0)
        qt = jnp.concatenate([qt_ref[here, pl.ds(start, head_dim)] for start in starts], axis=0)
        scores = lax.dot_general(
            q, keys[:, :head_dim], transposed, preferred_element_type=jnp.float32
        )
        tangent = lax.dot_general(
            jnp.concatenate([qt, q], axis=1), keys, transposed, preferred_element_type=jnp.float32
        )
        scores = scores.reshape(heads, STRETCH, span)
        tangent = tangent.reshape(heads, STRETCH, span)
        scores = jnp.where(admitted[None], scores, masked_score)
        peak = jnp.max(scores, axis=-1, keepdims=True)
        exponent = jnp.exp2((scores - peak) * to_log2)
        inverse = 1.0 / jnp.sum(exponent, axis=-1, keepdims=True)
        mean = jnp.sum(exponent * tangent, axis=-1, keepdims=True) * inverse
        prob = exponent * inverse
        prob_low = prob.astype(jnp.bfloat16).reshape(heads * STRETCH, span)
        tan_low = (prob * ((tangent - mean) * score_scale)).astype(jnp.bfloat16)
        tan_low = tan_low.reshape(heads * STRETCH, span)
        both = jnp.dot(prob_low, values, preferred_element_type=jnp.float32)
        more = jnp.dot(tan_low, values[:, :head_dim], preferred_element_type=jnp.float32)
        out = both[:, :head_dim].astype(jnp.bfloat16)
        out_tan = (both[:, head_dim:] + more).astype(jnp.bfloat16)
        for h in range(heads):
            of = slice(h * STRETCH, (h + 1) * STRETCH)
            out_ref[here, h * head_dim : (h + 1) * head_dim] = out[of]
            out_ref[here, width + h * head_dim : width + (h + 1) * head_dim] = out_tan[of]


def attention(half, order, queries, query_tangent, context, low):
    tokens, width = queries.shape[0] // 2, queries.shape[1]
    head_dim = context.shape[1] // 4
    heads = width // head_dim
    elements = tokens * heads * (WINDOW + STRETCH)
    steps = tokens // TILE
    offset = context.shape[0] - tokens - WINDOW
    return pl.pallas_call(
        functools.partial(attention_kernel, heads, head_dim, offset),
        grid=(steps,),
        in_specs=[
            pl.BlockSpec(memory_space=pltpu.SMEM),
            pl.BlockSpec((TILE, width), lambda i: (half * steps + i, 0)),
            pl.BlockSpec((TILE, width), lambda i: (half * steps + i, 0)),
            pl.BlockSpec(context.shape, lambda i: (0, 0)),
            pl.BlockSpec((TILE, low.shape[1]), lambda i: (half * steps + i, 0)),
        ],
        out_specs=pl.BlockSpec((TILE, 2 * width), lambda i: (i, 0)),
        out_shape=jax.ShapeDtypeStruct((tokens, 2 * width), jnp.bfloat16),
        compiler_params=pltpu.CompilerParams(vmem_limit_bytes=vmem_bytes),
        cost_estimate=pl.CostEstimate(
            flops=elements, bytes_accessed=tokens, transcendentals=0
        ),
        name="attention",
    )(order, queries, query_tangent, context, low)


def project_kernel(sent, kept, pair_ref, *refs):
    *weight_refs, send_ref, keep_ref = refs
    width = pair_ref.shape[1] // 2
    part = weight_refs[0].shape[2] // len(RELATIVE)
    dot = functools.partial(jnp.dot, preferred_element_type=jnp.float32)
    value, tangent, start = 0.0, 0.0, 0
    for ref in weight_refs:
        end = start + ref.shape[1]
        attended, attended_tan = pair_ref[:, start:end], pair_ref[:, width + start : width + end]
        value += dot(attended, ref[1])
        tangent += dot(attended, ref[0]) + dot(attended_tan, ref[1])
        start = end
    for ref, flips in ((send_ref, sent), (keep_ref, kept)):
        for place, flip in enumerate(flips):
            at = RELATIVE.index(flip) * part
            to = slice(place * part, (place + 1) * part)
            ref[0, :, to] = value[:, at : at + part].astype(ref.dtype)
            ref[1, :, to] = tangent[:, at : at + part].astype(ref.dtype)


def project(sent, kept, pair, weights):
    tokens, width = pair.shape
    tile = min(2 * TILE, tokens)
    columns = weights[0].shape[2]
    out = (2, tokens, columns // 2)
    block = pl.BlockSpec((2, tile, columns // 2), lambda i: (0, i, 0))
    return pl.pallas_call(
        functools.partial(project_kernel, sent, kept),
        grid=(tokens // tile,),
        in_specs=[
            pl.BlockSpec((tile, width), lambda i: (i, 0)),
            *[pl.BlockSpec(piece.shape, lambda i: (0, 0, 0)) for piece in weights],
        ],
        out_specs=[block, block],
        out_shape=[
            jax.ShapeDtypeStruct(out, jnp.bfloat16),
            jax.ShapeDtypeStruct(out, jnp.float32),
        ],
        compiler_params=pltpu.CompilerParams(vmem_limit_bytes=vmem_bytes),
        cost_estimate=pl.CostEstimate(
            flops=tokens * columns, bytes_accessed=tokens, transcendentals=0
        ),
        name="project",
    )(pair, *weights)


def across(block, flip):
    size = lax.axis_size("kv")
    return lax.ppermute(block, "kv", [(i, i ^ flip) for i in range(size)])


def along(block, chips):
    size = lax.axis_size("seq")
    return lax.ppermute(block, "seq", [(i, (i + CORES * chips) % size) for i in range(size)])


def other_core(block):
    return lax.ppermute(block, "seq", [(i, i ^ 1) for i in range(lax.axis_size("seq"))])


def hold(block, *until):
    return lax.optimization_barrier((block, *until))[0]


class Gather:
    def __init__(self, mine, chips):
        self.blocks = {0: mine}
        self.chips = chips
        self.forward, self.backward = chips // 2, (chips - 1) // 2

    def ahead(self):
        if self.forward:
            self.blocks[1] = along(self.blocks[0], 1)

    def behind(self):
        if self.backward:
            self.blocks[self.chips - 1] = along(self.blocks[0], -1)

    def farther(self):
        for step in range(2, self.forward + 1):
            self.blocks[step] = along(self.blocks[step - 1], 1)
        for step in range(2, self.backward + 1):
            self.blocks[self.chips - step] = along(self.blocks[self.chips - step + 1], -1)

    def early(self):
        near = jnp.concatenate([self.blocks[0], self.blocks[1]], axis=1)
        self.first = [near, other_core(near)]

    def late(self):
        near = jnp.concatenate([self.blocks[step] for step in range(2, self.chips)], axis=1)
        return [near, other_core(near)]


def together(*trees):
    return lax.optimization_barrier(trees)


def body(
    queries, query_tangent, key_value, key_value_tangents, doc_lengths, out_weight, weight_tangent
):
    tokens, width = queries.shape
    head_dim = key_value.shape[2]
    heads = width // head_dim
    half = tokens // 2
    seq_index = lax.axis_index("seq")
    kv_index = lax.axis_index("kv")
    seq_size = lax.axis_size("seq")
    chips = seq_size // CORES

    mine = arrange(kv_index, weight_tangent, out_weight)
    gathers = [Gather(block, chips) for block in mine]
    gathers[0].ahead()
    gathers[0].behind()
    gathers[1].ahead()

    key_value, key_value_tangents, _ = lax.optimization_barrier(
        (key_value, key_value_tangents, mine[0])
    )
    stacked = jnp.concatenate(
        [key_value[:, 0], key_value_tangents[:, 0], key_value[:, 1], key_value_tangents[:, 1]],
        axis=1,
    )
    prior = lax.ppermute(
        stacked[tokens - WINDOW :], "seq", [(i, i + 1) for i in range(seq_size - 1)]
    )

    doc_ends = jnp.cumsum(doc_lengths)
    doc_starts = doc_ends - doc_lengths
    position = seq_index * tokens + jnp.arange(tokens, dtype=jnp.int32)
    inside = (doc_starts[None, :] <= position[:, None]) & (position[:, None] < doc_ends[None, :])
    doc_first = jnp.sum(jnp.where(inside, doc_starts[None, :], 0), axis=1)
    lower = jnp.maximum(doc_first, position - WINDOW + 1)
    low = lower - (position // STRETCH * STRETCH - WINDOW)
    low = jnp.broadcast_to(low[:, None], (tokens, 128))

    step = jnp.arange(chips, dtype=jnp.int32)
    chip, core = seq_index // CORES, seq_index % CORES
    owner = (chip - step + chips) % chips * CORES
    near, far = owner + core, owner + 1 - core
    order = jnp.concatenate([near[:2], far[:2], near[2:], far[2:]])
    whole_heads = order.shape[0] == heads

    def attend(part, context):
        heads_order = order if whole_heads else jnp.arange(heads, dtype=jnp.int32)
        pair = attention(part, heads_order, queries, query_tangent, context, low)
        if not whole_heads:
            pair = jnp.take(pair.reshape(half, 2, seq_size, -1), order, axis=2)
            pair = pair.reshape(half, 2 * width)
        return pair

    pair_second = attend(1, stacked)
    pair_second, prior, gathers[0].blocks = together(pair_second, prior, gathers[0].blocks)
    gathers[0].farther()
    pair_first = attend(0, jnp.concatenate([prior, stacked[:half]], axis=0))

    def add_stage(keep, received, place):
        part = keep.shape[2] // 2
        of = slice(place * part, (place + 1) * part)
        return (keep[:, :, :part] + received[:, :, of]).astype(jnp.bfloat16)

    def total(keep, received, place, last):
        part = keep.shape[2] // 2
        of = slice(place * part, (place + 1) * part)
        return (keep[:, :, part:] + received[:, :, of] + last).astype(jnp.bfloat16)

    staged, sums, finished = [None] * CHUNKS, [None] * CHUNKS, []

    def second_stage(chunk):
        keep_x, from_x, keep_y, from_y = staged[chunk]
        send_y = add_stage(keep_x, from_x, 1)
        send_x = add_stage(keep_y, from_y, 1)
        sums[chunk] = (send_y, send_x)

    def finish(chunk, last_y, last_x):
        keep_x, from_x, keep_y, from_y = staged[chunk]
        first = total(keep_x, from_x, 0, last_y)
        second = total(keep_y, from_y, 0, last_x)
        finished.append(jnp.concatenate([first, second], axis=1))

    def last_exchange(chunk):
        send_y, send_x = sums[chunk]
        return across(send_y, 2), across(send_x, 1)

    def take(chunk):
        keep_x, from_x, keep_y, from_y = staged[chunk]
        return (from_x, from_y)

    def put(chunk, from_x, from_y):
        keep_x, _, keep_y, _ = staged[chunk]
        staged[chunk] = (keep_x, from_x, keep_y, from_y)

    gathers[0].early()
    exchanged, send_y = (), ()
    for chunk in range(CHUNKS):
        here = gathers[chunk]
        ahead = gathers[chunk + 1].blocks if chunk + 1 < CHUNKS else {}
        here.blocks, here.first, ahead, pair_first, exchanged, _ = together(
            here.blocks, here.first, ahead, pair_first, exchanged, send_y
        )
        weights = here.first + here.late()
        if chunk + 1 < CHUNKS:
            gathers[chunk + 1].blocks = ahead
            gathers[chunk + 1].behind()
            gathers[chunk + 1].farther()
            gathers[chunk + 1].early()
        if chunk + 2 < CHUNKS:
            gathers[chunk + 2].ahead()
        if chunk >= 2:
            finish(chunk - 2, *exchanged)
        if chunk >= 1:
            received, weights[2] = together(take(chunk - 1), weights[2])
            put(chunk - 1, *received)
            second_stage(chunk - 1)
            sums[chunk - 1], pair_first = together(sums[chunk - 1], pair_first)
            exchanged = last_exchange(chunk - 1)
        send_x, keep_x = project((1, 3), (2, 0), pair_first, weights)
        from_x = across(send_x, 1)
        send_y, keep_y = project((2, 3), (1, 0), hold(pair_second, send_x), weights)
        from_y = across(send_y, 2)
        staged[chunk] = (keep_x, from_x, keep_y, from_y)
    second_stage(CHUNKS - 1)
    last = last_exchange(CHUNKS - 1)
    finish(CHUNKS - 2, *exchanged)
    finish(CHUNKS - 1, *last)
    result = jnp.concatenate(finished, axis=2)
    return result[0], result[1]


def solution(mesh):
    in_specs = (
        P("seq", "kv"),
        P("seq", "kv"),
        P("seq", None, "kv"),
        P("seq", None, "kv"),
        P(),
        P(("kv", "seq"), None),
        P(("kv", "seq"), None),
    )
    out_specs = (P("seq", "kv"), P("seq", "kv"))
    return jax.shard_map(body, mesh=mesh, in_specs=in_specs, out_specs=out_specs, check_vma=False)
```

```python
import functools
import math

import jax
import jax.numpy as jnp
from jax import lax
from jax.experimental import pallas as pl
from jax.experimental.pallas import tpu as pltpu
from jax.sharding import PartitionSpec as P

STRETCH = 32
WINDOW = 224
GROUPS = (2, 2)
TILE = 128
CORES = 2
RELATIVE = (1, 3, 2, 0)

masked_score = -1e30
vmem_bytes = 48 * 1024 * 1024


def arrange_kernel(kv_ref, tangent_ref, value_ref, *group_refs):
    columns = tangent_ref.shape[1] // len(RELATIVE)
    chunk = 0
    for group_ref in group_refs:
        part = group_ref.shape[3] // len(RELATIVE)
        for index in range(group_ref.shape[0]):
            for place, flip in enumerate(RELATIVE):
                start = pl.multiple_of((kv_ref[0] ^ flip) * columns + chunk * part, part)
                to = slice(place * part, (place + 1) * part)
                group_ref[index, 0, :, to] = tangent_ref[:, pl.ds(start, part)]
                group_ref[index, 1, :, to] = value_ref[:, pl.ds(start, part)]
            chunk += 1


def arrange(kv_index, tangent, value):
    rows, columns = value.shape
    shapes = [
        jax.ShapeDtypeStruct((count, 2, rows, columns // sum(GROUPS)), value.dtype)
        for count in GROUPS
    ]
    return pl.pallas_call(
        arrange_kernel,
        in_specs=[
            pl.BlockSpec(memory_space=pltpu.SMEM),
            pl.BlockSpec(memory_space=pltpu.VMEM),
            pl.BlockSpec(memory_space=pltpu.VMEM),
        ],
        out_specs=[pl.BlockSpec(memory_space=pltpu.VMEM)] * len(GROUPS),
        out_shape=shapes,
        name="arrange",
    )(kv_index.reshape(1), tangent, value)


def attention_kernel(heads, head_dim, offset, order_ref, q_ref, qt_ref, ctx_ref, low_ref, out_ref):
    rows = q_ref.shape[0]
    span = WINDOW + STRETCH
    width = heads * head_dim
    score_scale = 1.0 / math.sqrt(head_dim)
    to_log2 = score_scale * math.log2(math.e)
    step = pl.program_id(0)
    transposed = (((1,), (1,)), ((), ()))
    column = lax.broadcasted_iota(jnp.int32, (STRETCH, span), 1)
    row = lax.broadcasted_iota(jnp.int32, (STRETCH, span), 0)
    causal = column <= row + WINDOW
    starts = [pl.multiple_of(order_ref[h] * head_dim, head_dim) for h in range(heads)]

    def window(part):
        return pl.ds(pl.multiple_of(offset + step * rows + part * STRETCH, STRETCH), span)

    def score(part):
        here = slice(part * STRETCH, (part + 1) * STRETCH)
        keys = ctx_ref[window(part), : 2 * head_dim]
        q = jnp.concatenate([q_ref[here, pl.ds(start, head_dim)] for start in starts], axis=0)
        qt = jnp.concatenate([qt_ref[here, pl.ds(start, head_dim)] for start in starts], axis=0)
        scores = lax.dot_general(
            q, keys[:, :head_dim], transposed, preferred_element_type=jnp.float32
        )
        tangent = lax.dot_general(
            jnp.concatenate([qt, q], axis=1), keys, transposed, preferred_element_type=jnp.float32
        )
        return scores.reshape(heads, STRETCH, span), tangent.reshape(heads, STRETCH, span)

    def weigh(part, scores, tangent):
        low = low_ref[part * STRETCH : (part + 1) * STRETCH, :]
        low = jnp.concatenate([low] * (span // low.shape[1]), axis=1)
        admitted = causal & (column >= low)
        scores = jnp.where(admitted[None], scores, masked_score)
        peak = jnp.max(scores, axis=-1, keepdims=True)
        exponent = jnp.exp2((scores - peak) * to_log2)
        inverse = 1.0 / jnp.sum(exponent, axis=-1, keepdims=True)
        mean = jnp.sum(exponent * tangent, axis=-1, keepdims=True) * inverse
        prob = exponent * inverse
        prob_low = prob.astype(jnp.bfloat16).reshape(heads * STRETCH, span)
        tan_low = (prob * ((tangent - mean) * score_scale)).astype(jnp.bfloat16)
        return prob_low, tan_low.reshape(heads * STRETCH, span)

    def gather_values(part, prob_low, tan_low):
        here = slice(part * STRETCH, (part + 1) * STRETCH)
        values = ctx_ref[window(part), 2 * head_dim :]
        both = jnp.dot(prob_low, values, preferred_element_type=jnp.float32)
        more = jnp.dot(tan_low, values[:, :head_dim], preferred_element_type=jnp.float32)
        out = both[:, :head_dim].astype(jnp.bfloat16)
        out_tan = (both[:, head_dim:] + more).astype(jnp.bfloat16)
        for h in range(heads):
            of = slice(h * STRETCH, (h + 1) * STRETCH)
            out_ref[here, h * head_dim : (h + 1) * head_dim] = out[of]
            out_ref[here, width + h * head_dim : width + (h + 1) * head_dim] = out_tan[of]

    parts = rows // STRETCH
    scored, weighed = score(0), None
    for part in range(parts):
        following = score(part + 1) if part + 1 < parts else None
        if weighed is not None:
            gather_values(part - 1, *weighed)
        weighed = weigh(part, *scored)
        scored = following
    gather_values(parts - 1, *weighed)


def attention(half, order, queries, query_tangent, context, low):
    tokens, width = queries.shape[0] // 2, queries.shape[1]
    head_dim = context.shape[1] // 4
    heads = width // head_dim
    elements = tokens * heads * (WINDOW + STRETCH)
    steps = tokens // TILE
    offset = context.shape[0] - tokens - WINDOW
    return pl.pallas_call(
        functools.partial(attention_kernel, heads, head_dim, offset),
        grid=(steps,),
        in_specs=[
            pl.BlockSpec(memory_space=pltpu.SMEM),
            pl.BlockSpec((TILE, width), lambda i: (half * steps + i, 0)),
            pl.BlockSpec((TILE, width), lambda i: (half * steps + i, 0)),
            pl.BlockSpec(context.shape, lambda i: (0, 0)),
            pl.BlockSpec((TILE, low.shape[1]), lambda i: (half * steps + i, 0)),
        ],
        out_specs=pl.BlockSpec((TILE, 2 * width), lambda i: (i, 0)),
        out_shape=jax.ShapeDtypeStruct((tokens, 2 * width), jnp.bfloat16),
        compiler_params=pltpu.CompilerParams(vmem_limit_bytes=vmem_bytes),
        cost_estimate=pl.CostEstimate(
            flops=elements, bytes_accessed=tokens, transcendentals=0
        ),
        name="attention",
    )(order, queries, query_tangent, context, low)


def project_kernel(sent, kept, pair_ref, *refs):
    *weight_refs, send_ref, keep_ref = refs
    width = pair_ref.shape[1] // 2
    rows = weight_refs[0].shape[1]
    part = weight_refs[0].shape[2] // len(RELATIVE)
    dot = functools.partial(jnp.dot, preferred_element_type=jnp.float32)
    value, tangent, start = 0.0, 0.0, 0
    joined = max(1, 256 // rows)
    for first in range(0, len(weight_refs), joined):
        refs = weight_refs[first : first + joined]
        end = start + rows * len(refs)
        tan_weight = jnp.concatenate([ref[0] for ref in refs], axis=0)
        weight = jnp.concatenate([ref[1] for ref in refs], axis=0)
        attended, attended_tan = pair_ref[:, start:end], pair_ref[:, width + start : width + end]
        value += dot(attended, weight)
        tangent += dot(attended, tan_weight) + dot(attended_tan, weight)
        start = end
    for ref, flips in ((send_ref, sent), (keep_ref, kept)):
        for place, flip in enumerate(flips):
            at = RELATIVE.index(flip) * part
            to = slice(place * part, (place + 1) * part)
            ref[0, :, to] = value[:, at : at + part].astype(ref.dtype)
            ref[1, :, to] = tangent[:, at : at + part].astype(ref.dtype)


def project(sent, kept, pair, index, weights):
    tokens, width = pair.shape
    tile = min(2 * TILE, tokens)
    _, _, rows, columns = weights[0].shape
    out = (2, tokens, columns // 2)
    block = pl.BlockSpec((2, tile, columns // 2), lambda i: (0, i, 0))
    piece = pl.BlockSpec((None, 2, rows, columns), lambda i: (index, 0, 0, 0))
    return pl.pallas_call(
        functools.partial(project_kernel, sent, kept),
        grid=(tokens // tile,),
        in_specs=[pl.BlockSpec((tile, width), lambda i: (i, 0))] + [piece] * len(weights),
        out_specs=[block, block],
        out_shape=[
            jax.ShapeDtypeStruct(out, jnp.bfloat16),
            jax.ShapeDtypeStruct(out, jnp.float32),
        ],
        compiler_params=pltpu.CompilerParams(vmem_limit_bytes=vmem_bytes),
        cost_estimate=pl.CostEstimate(
            flops=tokens * columns, bytes_accessed=tokens, transcendentals=0
        ),
        name="project",
    )(pair, *weights)


def finish_kernel(keep_x, from_x, last_y, keep_y, from_y, last_x, *refs):
    value_ref, tangent_ref = refs[-2:]
    half = keep_x.shape[1]
    for mat, ref in enumerate((value_ref, tangent_ref)):
        first = keep_x[mat] + from_x[mat] + last_y[mat]
        second = keep_y[mat] + from_y[mat] + last_x[mat]
        ref[:half, :] = first.astype(ref.dtype)
        ref[half:, :] = second.astype(ref.dtype)


def finish(chunk, chunks, outputs, keep_x, from_x, last_y, keep_y, from_y, last_x):
    half, part = last_y.shape[1:]
    kept = pl.BlockSpec((2, half, part), lambda i: (0, 0, 1))
    received = pl.BlockSpec((2, half, part), lambda i: (0, 0, 0))
    shape = jax.ShapeDtypeStruct((2 * half, part * chunks), jnp.bfloat16)
    return pl.pallas_call(
        finish_kernel,
        grid=(1,),
        in_specs=[kept, received, received] * 2 + [pl.BlockSpec(memory_space=pl.ANY)] * len(outputs),
        out_specs=[pl.BlockSpec((2 * half, part), lambda i: (0, chunk))] * 2,
        out_shape=[shape, shape],
        input_output_aliases={6 + i: i for i in range(len(outputs))},
        compiler_params=pltpu.CompilerParams(vmem_limit_bytes=vmem_bytes),
        name="finish",
    )(keep_x, from_x, last_y, keep_y, from_y, last_x, *outputs)


def across(block, flip):
    size = lax.axis_size("kv")
    return lax.ppermute(block, "kv", [(i, i ^ flip) for i in range(size)])


def along(block, chips):
    size = lax.axis_size("seq")
    return lax.ppermute(block, "seq", [(i, (i + CORES * chips) % size) for i in range(size)])


def other_core(block):
    return lax.ppermute(block, "seq", [(i, i ^ 1) for i in range(lax.axis_size("seq"))])


def together(*trees):
    return lax.optimization_barrier(trees)


class Gather:
    def __init__(self, mine, chips):
        self.blocks = {0: mine}
        self.others = {}
        self.chips = chips
        self.forward, self.backward = chips // 2, (chips - 1) // 2

    def neighbours(self):
        if self.forward:
            self.blocks[1] = along(self.blocks[0], 1)
        if self.backward:
            self.blocks[self.chips - 1] = along(self.blocks[0], -1)

    def farther(self):
        for step in range(2, self.forward + 1):
            self.blocks[step] = along(self.blocks[step - 1], 1)
        for step in range(2, self.backward + 1):
            self.blocks[self.chips - step] = along(self.blocks[self.chips - step + 1], -1)

    def near(self):
        steps = (0, 1, self.chips - 1)
        return {step: self.blocks[step] for step in steps if step in self.blocks}

    def exchange(self, blocks):
        for step, block in blocks.items():
            if step not in self.others:
                self.others[step] = other_core(block)

    def all(self):
        weights = []
        for step in range(self.chips):
            weights += [self.blocks[step], self.others[step]]
        return weights

    def get(self):
        return self.blocks, self.others

    def put(self, state):
        self.blocks, self.others = (dict(part) for part in state)


def body(
    queries, query_tangent, key_value, key_value_tangents, doc_lengths, out_weight, weight_tangent
):
    tokens, width = queries.shape
    head_dim = key_value.shape[2]
    heads = width // head_dim
    half = tokens // 2
    seq_index = lax.axis_index("seq")
    kv_index = lax.axis_index("kv")
    seq_size = lax.axis_size("seq")
    chips = seq_size // CORES

    mine = arrange(kv_index, weight_tangent, out_weight)
    early, late = [Gather(block, chips) for block in mine]
    early.neighbours()

    key_value, key_value_tangents, _ = lax.optimization_barrier(
        (key_value, key_value_tangents, mine[0])
    )
    stacked = jnp.concatenate(
        [key_value[:, 0], key_value_tangents[:, 0], key_value[:, 1], key_value_tangents[:, 1]],
        axis=1,
    )
    prior = lax.ppermute(
        stacked[tokens - WINDOW :], "seq", [(i, i + 1) for i in range(seq_size - 1)]
    )

    doc_ends = jnp.cumsum(doc_lengths)
    doc_starts = doc_ends - doc_lengths
    position = seq_index * tokens + jnp.arange(tokens, dtype=jnp.int32)
    inside = (doc_starts[None, :] <= position[:, None]) & (position[:, None] < doc_ends[None, :])
    doc_first = jnp.sum(jnp.where(inside, doc_starts[None, :], 0), axis=1)
    lower = jnp.maximum(doc_first, position - WINDOW + 1)
    low = lower - (position // STRETCH * STRETCH - WINDOW)
    low = jnp.broadcast_to(low[:, None], (tokens, 128))

    step = jnp.arange(chips, dtype=jnp.int32)
    chip, core = seq_index // CORES, seq_index % CORES
    owner = (chip - step + chips) % chips * CORES
    order = jnp.stack([owner + core, owner + 1 - core], axis=1).reshape(-1)
    whole_heads = order.shape[0] == heads

    def attend(part, context):
        heads_order = order if whole_heads else jnp.arange(heads, dtype=jnp.int32)
        pair = attention(part, heads_order, queries, query_tangent, context, low)
        if not whole_heads:
            pair = jnp.take(pair.reshape(half, 2, seq_size, -1), order, axis=2)
            pair = pair.reshape(half, 2 * width)
        return pair

    def first_stage(gathering, index, pairs):
        weights = gathering.all()
        send_x, keep_x = project((1, 3), (2, 0), pairs[0], index, weights)
        from_x = across(send_x, 1)
        pair, send_x = together(pairs[1], send_x)
        send_y, keep_y = project((2, 3), (1, 0), pair, index, weights)
        from_y = across(send_y, 2)
        return (keep_x, keep_y), (from_x, from_y), send_y

    def second_sums(kept, received):
        part = kept[0].shape[2] // 2
        return [
            (keep[:, :, :part] + block[:, :, part:]).astype(jnp.bfloat16)
            for keep, block in zip(kept, received)
        ]

    def second_stage(sums):
        return across(sums[0], 2), across(sums[1], 1)

    chunks = sum(GROUPS)

    def write(chunk, outputs, kept, received, last):
        return finish(
            chunk, chunks, outputs, kept[0], received[0], last[0], kept[1], received[1], last[1]
        )

    pair_second = attend(1, stacked)
    pair_second, prior, state, held = together(pair_second, prior, early.get(), late.blocks)
    early.put(state)
    late.blocks = dict(held)
    early.farther()
    early.exchange(early.near())
    late.exchange(late.near())
    pair_first = attend(0, jnp.concatenate([prior, stacked[:half]], axis=0))

    pairs, state, held = together((pair_first, pair_second), early.get(), late.get())
    early.put(state)
    late.put(held)
    early.exchange(early.blocks)
    late.neighbours()
    kept0, from0, send = first_stage(early, 0, pairs)
    pairs, send = together(pairs, send)
    kept1, from1, send = first_stage(early, 1, pairs)

    from0, state, pairs, send = together(from0, late.get(), pairs, send)
    late.put(state)
    late.farther()
    sums = second_sums(kept0, from0)
    last0 = second_stage(sums)

    from1, last0, sums, pairs, held = together(from1, last0, sums, pairs, late.near())
    late.blocks.update(held)
    late.exchange(held)
    sums = second_sums(kept1, from1)
    last1 = second_stage(sums)
    outputs = write(0, (), kept0, from0, last0)

    state, sums, pairs = together(late.get(), sums, pairs)
    late.put(state)
    late.exchange(late.blocks)
    state, last1, pairs = together(late.get(), last1, pairs)
    late.put(state)
    kept2, from2, send = first_stage(late, 0, pairs)
    pairs, send = together(pairs, send)
    kept3, from3, send = first_stage(late, 1, pairs)

    from2, send = together(from2, send)
    sums = second_sums(kept2, from2)
    last2 = second_stage(sums)
    outputs = write(1, outputs, kept1, from1, last1)

    from3, sums = together(from3, sums)
    sums = second_sums(kept3, from3)
    last3 = second_stage(sums)
    outputs = write(2, outputs, kept2, from2, last2)
    outputs = write(3, outputs, kept3, from3, last3)
    return tuple(outputs)


def solution(mesh):
    in_specs = (
        P("seq", "kv"),
        P("seq", "kv"),
        P("seq", None, "kv"),
        P("seq", None, "kv"),
        P(),
        P(("kv", "seq"), None),
        P(("kv", "seq"), None),
    )
    out_specs = (P("seq", "kv"), P("seq", "kv"))
    return jax.shard_map(body, mesh=mesh, in_specs=in_specs, out_specs=out_specs, check_vma=False)
```

```python
import functools
import math

import jax
import jax.numpy as jnp
from jax import lax
from jax.experimental import pallas as pl
from jax.experimental.pallas import tpu as pltpu
from jax.sharding import PartitionSpec as P

STRETCH = 32
WINDOW = 224
GROUPS = (1, 1, 2)
TILE = 128
CORES = 2
RELATIVE = (1, 3, 2, 0)

masked_score = -1e30
vmem_bytes = 16 * 1024 * 1024


def arrange_kernel(kv_ref, tangent_ref, value_ref, whole_ref, *group_refs):
    columns = tangent_ref.shape[1] // len(RELATIVE)
    part = whole_ref.shape[3] // len(RELATIVE)
    chunk = 0
    for group_ref in group_refs:
        for index in range(group_ref.shape[0]):
            for place, flip in enumerate(RELATIVE):
                start = pl.multiple_of((kv_ref[0] ^ flip) * columns + chunk * part, part)
                to = slice(place * part, (place + 1) * part)
                for mat, ref in enumerate((tangent_ref, value_ref)):
                    block = ref[:, pl.ds(start, part)]
                    whole_ref[chunk, mat, :, to] = block
                    group_ref[index, mat, :, to] = block
            chunk += 1


def arrange(kv_index, tangent, value):
    rows, columns = value.shape
    shapes = [
        jax.ShapeDtypeStruct((count, 2, rows, columns // sum(GROUPS)), value.dtype)
        for count in (sum(GROUPS), *GROUPS)
    ]
    return pl.pallas_call(
        arrange_kernel,
        in_specs=[
            pl.BlockSpec(memory_space=pltpu.SMEM),
            pl.BlockSpec(memory_space=pltpu.VMEM),
            pl.BlockSpec(memory_space=pltpu.VMEM),
        ],
        out_specs=[pl.BlockSpec(memory_space=pltpu.VMEM)] * len(shapes),
        out_shape=shapes,
        compiler_params=pltpu.CompilerParams(vmem_limit_bytes=vmem_bytes),
        name="arrange",
    )(kv_index.reshape(1), tangent, value)


def attention_kernel(heads, head_dim, offset, order_ref, q_ref, qt_ref, ctx_ref, low_ref, out_ref):
    rows = q_ref.shape[0]
    span = WINDOW + STRETCH
    width = heads * head_dim
    score_scale = 1.0 / math.sqrt(head_dim)
    to_log2 = score_scale * math.log2(math.e)
    step = pl.program_id(0)
    transposed = (((1,), (1,)), ((), ()))
    column = lax.broadcasted_iota(jnp.int32, (STRETCH, span), 1)
    row = lax.broadcasted_iota(jnp.int32, (STRETCH, span), 0)
    causal = column <= row + WINDOW
    starts = [pl.multiple_of(order_ref[h] * head_dim, head_dim) for h in range(heads)]

    def window(part):
        return pl.ds(pl.multiple_of(offset + step * rows + part * STRETCH, STRETCH), span)

    def score(part):
        here = slice(part * STRETCH, (part + 1) * STRETCH)
        keys = ctx_ref[window(part), : 2 * head_dim]
        q = jnp.concatenate([q_ref[here, pl.ds(start, head_dim)] for start in starts], axis=0)
        qt = jnp.concatenate([qt_ref[here, pl.ds(start, head_dim)] for start in starts], axis=0)
        scores = lax.dot_general(
            q, keys[:, :head_dim], transposed, preferred_element_type=jnp.float32
        )
        tangent = lax.dot_general(
            jnp.concatenate([qt, q], axis=1), keys, transposed, preferred_element_type=jnp.float32
        )
        return scores.reshape(heads, STRETCH, span), tangent.reshape(heads, STRETCH, span)

    def weigh(part, scores, tangent):
        low = low_ref[part * STRETCH : (part + 1) * STRETCH, :]
        low = jnp.concatenate([low] * (span // low.shape[1]), axis=1)
        admitted = causal & (column >= low)
        scores = jnp.where(admitted[None], scores, masked_score)
        peak = jnp.max(scores, axis=-1, keepdims=True)
        exponent = jnp.exp2((scores - peak) * to_log2)
        inverse = 1.0 / jnp.sum(exponent, axis=-1, keepdims=True)
        mean = jnp.sum(exponent * tangent, axis=-1, keepdims=True) * inverse
        prob = exponent * inverse
        prob_low = prob.astype(jnp.bfloat16).reshape(heads * STRETCH, span)
        tan_low = (prob * ((tangent - mean) * score_scale)).astype(jnp.bfloat16)
        return prob_low, tan_low.reshape(heads * STRETCH, span)

    def gather_values(part, prob_low, tan_low):
        here = slice(part * STRETCH, (part + 1) * STRETCH)
        values = ctx_ref[window(part), 2 * head_dim :]
        both = jnp.dot(prob_low, values, preferred_element_type=jnp.float32)
        more = jnp.dot(tan_low, values[:, :head_dim], preferred_element_type=jnp.float32)
        out = both[:, :head_dim].astype(jnp.bfloat16)
        out_tan = (both[:, head_dim:] + more).astype(jnp.bfloat16)
        for h in range(heads):
            of = slice(h * STRETCH, (h + 1) * STRETCH)
            out_ref[here, h * head_dim : (h + 1) * head_dim] = out[of]
            out_ref[here, width + h * head_dim : width + (h + 1) * head_dim] = out_tan[of]

    parts = rows // STRETCH
    scored, weighed = score(0), None
    for part in range(parts):
        following = score(part + 1) if part + 1 < parts else None
        if weighed is not None:
            gather_values(part - 1, *weighed)
        weighed = weigh(part, *scored)
        scored = following
    gather_values(parts - 1, *weighed)


def attention(half, order, queries, query_tangent, context, low):
    tokens, width = queries.shape[0] // 2, queries.shape[1]
    head_dim = context.shape[1] // 4
    heads = width // head_dim
    elements = tokens * heads * (WINDOW + STRETCH)
    steps = tokens // TILE
    offset = context.shape[0] - tokens - WINDOW
    return pl.pallas_call(
        functools.partial(attention_kernel, heads, head_dim, offset),
        grid=(steps,),
        in_specs=[
            pl.BlockSpec(memory_space=pltpu.SMEM),
            pl.BlockSpec((TILE, width), lambda i: (half * steps + i, 0)),
            pl.BlockSpec((TILE, width), lambda i: (half * steps + i, 0)),
            pl.BlockSpec(context.shape, lambda i: (0, 0)),
            pl.BlockSpec((TILE, low.shape[1]), lambda i: (half * steps + i, 0)),
        ],
        out_specs=pl.BlockSpec((TILE, 2 * width), lambda i: (i, 0)),
        out_shape=jax.ShapeDtypeStruct((tokens, 2 * width), jnp.bfloat16),
        compiler_params=pltpu.CompilerParams(vmem_limit_bytes=vmem_bytes),
        cost_estimate=pl.CostEstimate(
            flops=elements, bytes_accessed=tokens, transcendentals=0
        ),
        name="attention",
    )(order, queries, query_tangent, context, low)


def project_kernel(places, first_ref, second_ref, *refs):
    count = len(places)
    piece_refs = refs[:count]
    send_x, keep_x, send_y, keep_y, weight_ref, sems = refs[count:]
    step, steps = pl.program_id(0), pl.num_programs(0)
    rows = piece_refs[0].shape[2]
    depth = count * rows
    part = weight_ref.shape[2] // len(RELATIVE)

    @pl.when(step == 0)
    def _():
        copies = []
        for place, (index, ref) in enumerate(zip(places, piece_refs)):
            to = weight_ref.at[:, pl.ds(place * rows, rows), :]
            copies.append(pltpu.make_async_copy(ref.at[index], to, sems.at[place]))
            copies[-1].start()
        for copy in copies:
            copy.wait()

    def run(pair_ref, send_ref, keep_ref, sent, kept):
        dot = functools.partial(jnp.dot, preferred_element_type=jnp.float32)
        value = dot(pair_ref[:, :depth], weight_ref[1])
        tangent = dot(pair_ref[:, :depth], weight_ref[0]) + dot(pair_ref[:, depth:], weight_ref[1])
        for ref, flips in ((send_ref, sent), (keep_ref, kept)):
            for place, flip in enumerate(flips):
                at = RELATIVE.index(flip) * part
                to = slice(place * part, (place + 1) * part)
                ref[0, :, to] = value[:, at : at + part].astype(ref.dtype)
                ref[1, :, to] = tangent[:, at : at + part].astype(ref.dtype)

    @pl.when(step < steps // 2)
    def _():
        run(first_ref, send_x, keep_x, (1, 3), (2, 0))

    @pl.when(step >= steps // 2)
    def _():
        run(second_ref, send_y, keep_y, (2, 3), (1, 0))


def project(pairs, pieces):
    tokens, width = pairs[0].shape
    tile = min(2 * TILE, tokens)
    steps = tokens // tile
    places = [index for index, _ in pieces]
    blocks = [block for _, block in pieces]
    _, _, rows, columns = blocks[0].shape
    early = lambda i: jnp.minimum(i, steps - 1)
    late = lambda i: jnp.maximum(i - steps, 0)
    out = (2, tokens, columns // 2)
    first = pl.BlockSpec((2, tile, columns // 2), lambda i: (0, early(i), 0))
    second = pl.BlockSpec((2, tile, columns // 2), lambda i: (0, late(i), 0))
    send = jax.ShapeDtypeStruct(out, jnp.bfloat16)
    keep = jax.ShapeDtypeStruct(out, jnp.float32)
    return pl.pallas_call(
        functools.partial(project_kernel, places),
        grid=(2 * steps,),
        in_specs=[
            pl.BlockSpec((tile, width), lambda i: (early(i), 0)),
            pl.BlockSpec((tile, width), lambda i: (late(i), 0)),
            *[pl.BlockSpec(memory_space=pl.ANY)] * len(blocks),
        ],
        out_specs=[first, first, second, second],
        out_shape=[send, keep, send, keep],
        scratch_shapes=[
            pltpu.VMEM((2, rows * len(blocks), columns), jnp.bfloat16),
            pltpu.SemaphoreType.DMA((len(blocks),)),
        ],
        compiler_params=pltpu.CompilerParams(vmem_limit_bytes=vmem_bytes),
        cost_estimate=pl.CostEstimate(
            flops=tokens * columns, bytes_accessed=tokens, transcendentals=0
        ),
        name="project",
    )(*pairs, *blocks)


def finish_kernel(keep_x, from_x, last_y, keep_y, from_y, last_x, *refs):
    value_ref, tangent_ref = refs[-2:]
    half = keep_x.shape[1]
    for mat, ref in enumerate((value_ref, tangent_ref)):
        first = keep_x[mat] + from_x[mat] + last_y[mat]
        second = keep_y[mat] + from_y[mat] + last_x[mat]
        ref[:half, :] = first.astype(ref.dtype)
        ref[half:, :] = second.astype(ref.dtype)


def finish(chunk, chunks, outputs, keep_x, from_x, last_y, keep_y, from_y, last_x):
    half, part = last_y.shape[1:]
    kept = pl.BlockSpec((2, half, part), lambda i: (0, 0, 1))
    received = pl.BlockSpec((2, half, part), lambda i: (0, 0, 0))
    shape = jax.ShapeDtypeStruct((2 * half, part * chunks), jnp.bfloat16)
    return pl.pallas_call(
        finish_kernel,
        grid=(1,),
        in_specs=[kept, received, received] * 2 + [pl.BlockSpec(memory_space=pl.ANY)] * len(outputs),
        out_specs=[pl.BlockSpec((2 * half, part), lambda i: (0, chunk))] * 2,
        out_shape=[shape, shape],
        input_output_aliases={6 + i: i for i in range(len(outputs))},
        compiler_params=pltpu.CompilerParams(vmem_limit_bytes=vmem_bytes),
        name="finish",
    )(keep_x, from_x, last_y, keep_y, from_y, last_x, *outputs)


def across(block, flip):
    size = lax.axis_size("kv")
    return lax.ppermute(block, "kv", [(i, i ^ flip) for i in range(size)])


def along(block, chips):
    size = lax.axis_size("seq")
    return lax.ppermute(block, "seq", [(i, (i + CORES * chips) % size) for i in range(size)])


def other_core(block):
    return lax.ppermute(block, "seq", [(i, i ^ 1) for i in range(lax.axis_size("seq"))])


def together(*trees):
    return lax.optimization_barrier(trees)


class Gather:
    def __init__(self, mine, chips):
        self.blocks = {0: mine}
        self.others = {}
        self.chips = chips
        self.forward, self.backward = chips // 2, (chips - 1) // 2

    def ahead(self):
        if self.forward:
            self.blocks[1] = along(self.blocks[0], 1)

    def behind(self):
        if self.backward:
            self.blocks[self.chips - 1] = along(self.blocks[0], -1)

    def farther_ahead(self):
        for step in range(2, self.forward + 1):
            self.blocks[step] = along(self.blocks[step - 1], 1)

    def farther_behind(self):
        for step in range(2, self.backward + 1):
            self.blocks[self.chips - step] = along(self.blocks[self.chips - step + 1], -1)

    def exchange(self, *steps):
        for step in steps or range(1, self.chips):
            if step % self.chips in self.blocks and step % self.chips not in self.others:
                self.others[step % self.chips] = other_core(self.blocks[step % self.chips])

    def get(self):
        return self.blocks, self.others

    def put(self, state):
        self.blocks, self.others = (dict(part) for part in state)

    def pieces(self, index, whole, chunk):
        pieces = [(index, self.blocks[0]), (chunk, whole)]
        for step in range(1, self.chips):
            pieces += [(index, self.blocks[step]), (index, self.others[step])]
        return pieces


def body(
    queries, query_tangent, key_value, key_value_tangents, doc_lengths, out_weight, weight_tangent
):
    tokens, width = queries.shape
    head_dim = key_value.shape[2]
    heads = width // head_dim
    half = tokens // 2
    seq_index = lax.axis_index("seq")
    kv_index = lax.axis_index("kv")
    seq_size = lax.axis_size("seq")
    chips = seq_size // CORES

    whole, *mine = arrange(kv_index, weight_tangent, out_weight)
    one, two, rest = [Gather(block, chips) for block in mine]
    one.ahead()
    one.behind()
    whole = other_core(whole)

    key_value, key_value_tangents, _ = lax.optimization_barrier(
        (key_value, key_value_tangents, mine[0])
    )
    stacked = jnp.concatenate(
        [key_value[:, 0], key_value_tangents[:, 0], key_value[:, 1], key_value_tangents[:, 1]],
        axis=1,
    )
    prior = lax.ppermute(
        stacked[tokens - WINDOW :], "seq", [(i, i + 1) for i in range(seq_size - 1)]
    )

    doc_ends = jnp.cumsum(doc_lengths)
    doc_starts = doc_ends - doc_lengths
    position = seq_index * tokens + jnp.arange(tokens, dtype=jnp.int32)
    inside = (doc_starts[None, :] <= position[:, None]) & (position[:, None] < doc_ends[None, :])
    doc_first = jnp.sum(jnp.where(inside, doc_starts[None, :], 0), axis=1)
    lower = jnp.maximum(doc_first, position - WINDOW + 1)
    low = lower - (position // STRETCH * STRETCH - WINDOW)
    low = jnp.broadcast_to(low[:, None], (tokens, 128))

    step = jnp.arange(chips, dtype=jnp.int32)
    chip, core = seq_index // CORES, seq_index % CORES
    owner = (chip - step + chips) % chips * CORES
    order = jnp.stack([owner + core, owner + 1 - core], axis=1).reshape(-1)
    whole_heads = order.shape[0] == heads

    def attend(part, context):
        heads_order = order if whole_heads else jnp.arange(heads, dtype=jnp.int32)
        pair = attention(part, heads_order, queries, query_tangent, context, low)
        if not whole_heads:
            pair = jnp.take(pair.reshape(half, 2, seq_size, -1), order, axis=2)
            pair = pair.reshape(half, 2 * width)
        return pair

    def first_stage(gathering, index, chunk, pairs, last=()):
        pieces = gathering.pieces(index, whole, chunk)
        send_x, keep_x, send_y, keep_y = project(pairs, pieces)
        send_x, send_y, last = together(send_x, send_y, last)
        return (keep_x, keep_y), (across(send_x, 1), across(send_y, 2)), send_y, last

    def second_sums(kept, received):
        part = kept[0].shape[2] // 2
        return [
            (keep[:, :, :part] + block[:, :, part:]).astype(jnp.bfloat16)
            for keep, block in zip(kept, received)
        ]

    def second_stage(sums):
        return across(sums[0], 2), across(sums[1], 1)

    chunks = sum(GROUPS)

    def write(chunk, outputs, kept, received, last):
        return finish(
            chunk, chunks, outputs, kept[0], received[0], last[0], kept[1], received[1], last[1]
        )

    pair_second = attend(1, stacked)
    pair_second, prior, state, held = together(pair_second, prior, one.get(), two.blocks)
    one.put(state)
    two.blocks = dict(held)
    one.farther_ahead()
    one.farther_behind()
    one.exchange(1, -1)
    two.ahead()
    pair_first = attend(0, jnp.concatenate([prior, stacked[:half]], axis=0))

    pairs, whole, state, held, mine = together(
        (pair_first, pair_second), whole, one.get(), two.get(), rest.blocks
    )
    one.put(state)
    two.put(held)
    rest.blocks = dict(mine)
    one.exchange()
    two.farther_ahead()
    two.behind()
    two.exchange(1)
    kept0, from0, send, _ = first_stage(one, 0, 0, pairs)

    held, pairs, send = together(two.get(), pairs, send)
    two.put(held)
    two.farther_behind()
    two.exchange()
    rest.ahead()
    rest.behind()
    held, from0 = together(two.get(), from0)
    two.put(held)
    sums = second_sums(kept0, from0)
    last0 = second_stage(sums)
    pairs, sums = together(pairs, sums)
    kept1, from1, send, last0 = first_stage(two, 0, 1, pairs, last0)

    state, send = together(rest.get(), send)
    rest.put(state)
    rest.farther_ahead()
    rest.exchange(1, -1)
    rest.farther_behind()
    outputs = write(0, (), kept0, from0, last0)

    from1, pairs, send, outputs = together(from1, pairs, send, outputs)
    sums = second_sums(kept1, from1)
    last1 = second_stage(sums)

    state, sums, pairs = together(rest.get(), sums, pairs)
    rest.put(state)
    rest.exchange()
    kept2, from2, send, last1 = first_stage(rest, 0, 2, pairs, last1)
    pairs, send = together(pairs, send)
    kept3, from3, send, _ = first_stage(rest, 1, 3, pairs)

    from2, send = together(from2, send)
    sums = second_sums(kept2, from2)
    last2 = second_stage(sums)
    outputs = write(1, outputs, kept1, from1, last1)

    from3, sums = together(from3, sums)
    sums = second_sums(kept3, from3)
    last3 = second_stage(sums)
    outputs = write(2, outputs, kept2, from2, last2)
    outputs = write(3, outputs, kept3, from3, last3)
    return tuple(outputs)


def solution(mesh):
    in_specs = (
        P("seq", "kv"),
        P("seq", "kv"),
        P("seq", None, "kv"),
        P("seq", None, "kv"),
        P(),
        P(("kv", "seq"), None),
        P(("kv", "seq"), None),
    )
    out_specs = (P("seq", "kv"), P("seq", "kv"))
    return jax.shard_map(body, mesh=mesh, in_specs=in_specs, out_specs=out_specs, check_vma=False)
```

```python
import functools
import math

import jax
import jax.numpy as jnp
from jax import lax
from jax.experimental import pallas as pl
from jax.experimental.pallas import tpu as pltpu
from jax.sharding import PartitionSpec as P

STRETCH = 32
WINDOW = 224
CHUNKS = 4
TILE = 128
CORES = 2

masked_score = -1e30
vmem_bytes = 16 * 1024 * 1024


def arrange_kernel(owners, tangent_ref, value_ref, whole_ref, *chunk_refs):
    columns = tangent_ref.shape[1] // owners
    part = columns // len(chunk_refs)
    for chunk, chunk_ref in enumerate(chunk_refs):
        for owner in range(owners):
            of = slice(owner * columns + chunk * part, owner * columns + (chunk + 1) * part)
            to = slice(owner * part, (owner + 1) * part)
            for mat, ref in enumerate((tangent_ref, value_ref)):
                whole_ref[chunk, mat, :, to] = ref[:, of]
                chunk_ref[mat, :, to] = ref[:, of]


def arrange(owners, tangent, value):
    rows, columns = value.shape
    chunk = (2, rows, columns // CHUNKS)
    shapes = [jax.ShapeDtypeStruct(shape, value.dtype) for shape in [(CHUNKS, *chunk)] + [chunk] * CHUNKS]
    return pl.pallas_call(
        functools.partial(arrange_kernel, owners),
        in_specs=[pl.BlockSpec(memory_space=pltpu.VMEM)] * 2,
        out_specs=[pl.BlockSpec(memory_space=pltpu.VMEM)] * len(shapes),
        out_shape=shapes,
        compiler_params=pltpu.CompilerParams(vmem_limit_bytes=vmem_bytes),
        name="arrange",
    )(tangent, value)


def attention_kernel(heads, head_dim, offset, order_ref, q_ref, qt_ref, ctx_ref, low_ref, out_ref):
    rows = q_ref.shape[0]
    span = WINDOW + STRETCH
    width = heads * head_dim
    score_scale = 1.0 / math.sqrt(head_dim)
    to_log2 = score_scale * math.log2(math.e)
    step = pl.program_id(0)
    transposed = (((1,), (1,)), ((), ()))
    column = lax.broadcasted_iota(jnp.int32, (STRETCH, span), 1)
    row = lax.broadcasted_iota(jnp.int32, (STRETCH, span), 0)
    causal = column <= row + WINDOW
    starts = [pl.multiple_of(order_ref[h] * head_dim, head_dim) for h in range(heads)]

    def window(part):
        return pl.ds(pl.multiple_of(offset + step * rows + part * STRETCH, STRETCH), span)

    def score(part):
        here = slice(part * STRETCH, (part + 1) * STRETCH)
        keys = ctx_ref[window(part), : 2 * head_dim]
        q = jnp.concatenate([q_ref[here, pl.ds(start, head_dim)] for start in starts], axis=0)
        qt = jnp.concatenate([qt_ref[here, pl.ds(start, head_dim)] for start in starts], axis=0)
        scores = lax.dot_general(
            q, keys[:, :head_dim], transposed, preferred_element_type=jnp.float32
        )
        tangent = lax.dot_general(
            jnp.concatenate([qt, q], axis=1), keys, transposed, preferred_element_type=jnp.float32
        )
        return scores.reshape(heads, STRETCH, span), tangent.reshape(heads, STRETCH, span)

    def weigh(part, scores, tangent):
        low = low_ref[part * STRETCH : (part + 1) * STRETCH, :]
        low = jnp.concatenate([low] * (span // low.shape[1]), axis=1)
        admitted = causal & (column >= low)
        scores = jnp.where(admitted[None], scores, masked_score)
        peak = jnp.max(scores, axis=-1, keepdims=True)
        exponent = jnp.exp2((scores - peak) * to_log2)
        inverse = 1.0 / jnp.sum(exponent, axis=-1, keepdims=True)
        mean = jnp.sum(exponent * tangent, axis=-1, keepdims=True) * inverse
        prob = exponent * inverse
        prob_low = prob.astype(jnp.bfloat16).reshape(heads * STRETCH, span)
        tan_low = (prob * ((tangent - mean) * score_scale)).astype(jnp.bfloat16)
        return prob_low, tan_low.reshape(heads * STRETCH, span)

    def gather_values(part, prob_low, tan_low):
        here = slice(part * STRETCH, (part + 1) * STRETCH)
        values = ctx_ref[window(part), 2 * head_dim :]
        both = jnp.dot(prob_low, values, preferred_element_type=jnp.float32)
        more = jnp.dot(tan_low, values[:, :head_dim], preferred_element_type=jnp.float32)
        out = both[:, :head_dim].astype(jnp.bfloat16)
        out_tan = (both[:, head_dim:] + more).astype(jnp.bfloat16)
        for h in range(heads):
            of = slice(h * STRETCH, (h + 1) * STRETCH)
            out_ref[here, h * head_dim : (h + 1) * head_dim] = out[of]
            out_ref[here, width + h * head_dim : width + (h + 1) * head_dim] = out_tan[of]

    parts = rows // STRETCH
    scored, weighed = score(0), None
    for part in range(parts):
        following = score(part + 1) if part + 1 < parts else None
        if weighed is not None:
            gather_values(part - 1, *weighed)
        weighed = weigh(part, *scored)
        scored = following
    gather_values(parts - 1, *weighed)


def attention(half, order, queries, query_tangent, context, low):
    tokens, width = queries.shape[0] // 2, queries.shape[1]
    head_dim = context.shape[1] // 4
    heads = width // head_dim
    elements = tokens * heads * (WINDOW + STRETCH)
    steps = tokens // TILE
    offset = context.shape[0] - tokens - WINDOW
    return pl.pallas_call(
        functools.partial(attention_kernel, heads, head_dim, offset),
        grid=(steps,),
        in_specs=[
            pl.BlockSpec(memory_space=pltpu.SMEM),
            pl.BlockSpec((TILE, width), lambda i: (half * steps + i, 0)),
            pl.BlockSpec((TILE, width), lambda i: (half * steps + i, 0)),
            pl.BlockSpec(context.shape, lambda i: (0, 0)),
            pl.BlockSpec((TILE, low.shape[1]), lambda i: (half * steps + i, 0)),
        ],
        out_specs=pl.BlockSpec((TILE, 2 * width), lambda i: (i, 0)),
        out_shape=jax.ShapeDtypeStruct((tokens, 2 * width), jnp.bfloat16),
        compiler_params=pltpu.CompilerParams(vmem_limit_bytes=vmem_bytes),
        cost_estimate=pl.CostEstimate(
            flops=elements, bytes_accessed=tokens, transcendentals=0
        ),
        name="attention",
    )(order, queries, query_tangent, context, low)


def project_kernel(chunk, first_ref, second_ref, whole_ref, *refs):
    *piece_refs, send_ref, weight_ref, sems = refs
    step, steps = pl.program_id(0), pl.num_programs(0)
    rows = whole_ref.shape[2]
    depth = weight_ref.shape[1]
    owners, _, _, part = send_ref.shape
    sources = [piece_refs[0], whole_ref.at[chunk], *piece_refs[1:]]

    @pl.when(step == 0)
    def _():
        copies = []
        for place, source in enumerate(sources):
            to = weight_ref.at[:, pl.ds(place * rows, rows), :]
            copies.append(pltpu.make_async_copy(source, to, sems.at[place]))
            copies[-1].start()
        for copy in copies:
            copy.wait()

    def run(pair_ref):
        dot = functools.partial(jnp.dot, preferred_element_type=jnp.float32)
        value = dot(pair_ref[:, :depth], weight_ref[1])
        tangent = dot(pair_ref[:, :depth], weight_ref[0]) + dot(pair_ref[:, depth:], weight_ref[1])
        for owner in range(owners):
            of = slice(owner * part, (owner + 1) * part)
            send_ref[owner, 0] = value[:, of].astype(send_ref.dtype)
            send_ref[owner, 1] = tangent[:, of].astype(send_ref.dtype)

    @pl.when(step < steps // 2)
    def _():
        run(first_ref)

    @pl.when(step >= steps // 2)
    def _():
        run(second_ref)


def project(owners, chunk, pairs, whole, pieces):
    tokens, width = pairs[0].shape
    tile = min(2 * TILE, tokens)
    steps = tokens // tile
    _, rows, columns = pieces[0].shape
    part = columns // owners
    count = len(pieces) + 1
    return pl.pallas_call(
        functools.partial(project_kernel, chunk),
        grid=(2 * steps,),
        in_specs=[
            pl.BlockSpec((tile, width), lambda i: (jnp.minimum(i, steps - 1), 0)),
            pl.BlockSpec((tile, width), lambda i: (jnp.maximum(i - steps, 0), 0)),
            *[pl.BlockSpec(memory_space=pl.ANY)] * count,
        ],
        out_specs=pl.BlockSpec((owners, 2, tile, part), lambda i: (0, 0, i, 0)),
        out_shape=jax.ShapeDtypeStruct((owners, 2, 2 * tokens, part), jnp.bfloat16),
        scratch_shapes=[
            pltpu.VMEM((2, rows * count, columns), jnp.bfloat16),
            pltpu.SemaphoreType.DMA((count,)),
        ],
        compiler_params=pltpu.CompilerParams(vmem_limit_bytes=vmem_bytes),
        cost_estimate=pl.CostEstimate(
            flops=tokens * columns, bytes_accessed=tokens, transcendentals=0
        ),
        name="project",
    )(*pairs, whole, *pieces)


def finish_kernel(parts_ref, *refs):
    for mat, ref in enumerate(refs[-2:]):
        total = parts_ref[0, mat].astype(jnp.float32)
        for owner in range(1, parts_ref.shape[0]):
            total = total + parts_ref[owner, mat]
        ref[...] = total.astype(ref.dtype)


def finish(chunk, outputs, parts):
    owners, _, tokens, part = parts.shape
    shape = jax.ShapeDtypeStruct((tokens, part * CHUNKS), jnp.bfloat16)
    tile = tokens // 2
    return pl.pallas_call(
        finish_kernel,
        grid=(tokens // tile,),
        in_specs=[
            pl.BlockSpec((owners, 2, tile, part), lambda i: (0, 0, i, 0)),
            *[pl.BlockSpec(memory_space=pl.ANY)] * len(outputs),
        ],
        out_specs=[pl.BlockSpec((tile, part), lambda i: (i, chunk))] * 2,
        out_shape=[shape, shape],
        input_output_aliases={1 + i: i for i in range(len(outputs))},
        compiler_params=pltpu.CompilerParams(vmem_limit_bytes=vmem_bytes),
        name="finish",
    )(parts, *outputs)


def along(block, chips):
    size = lax.axis_size("seq")
    return lax.ppermute(block, "seq", [(i, (i + CORES * chips) % size) for i in range(size)])


def other_core(block):
    return lax.ppermute(block, "seq", [(i, i ^ 1) for i in range(lax.axis_size("seq"))])


def together(*trees):
    return lax.optimization_barrier(trees)


class Gather:
    def __init__(self, mine, chips):
        self.blocks = {0: mine}
        self.others = {}
        self.chips = chips
        self.forward, self.backward = chips // 2, (chips - 1) // 2

    def ahead(self):
        if self.forward:
            self.blocks[1] = along(self.blocks[0], 1)

    def behind(self):
        if self.backward:
            self.blocks[self.chips - 1] = along(self.blocks[0], -1)

    def farther_ahead(self):
        for step in range(2, self.forward + 1):
            self.blocks[step] = along(self.blocks[step - 1], 1)

    def farther_behind(self):
        for step in range(2, self.backward + 1):
            self.blocks[self.chips - step] = along(self.blocks[self.chips - step + 1], -1)

    def exchange(self, *steps):
        for step in steps or range(1, self.chips):
            if step % self.chips in self.blocks and step % self.chips not in self.others:
                self.others[step % self.chips] = other_core(self.blocks[step % self.chips])

    def get(self):
        return self.blocks, self.others

    def put(self, state):
        self.blocks, self.others = (dict(part) for part in state)

    def pieces(self):
        pieces = [self.blocks[0]]
        for step in range(1, self.chips):
            pieces += [self.blocks[step], self.others[step]]
        return pieces


def body(
    queries, query_tangent, key_value, key_value_tangents, doc_lengths, out_weight, weight_tangent
):
    tokens, width = queries.shape
    head_dim = key_value.shape[2]
    heads = width // head_dim
    half = tokens // 2
    seq_index = lax.axis_index("seq")
    seq_size = lax.axis_size("seq")
    chips = seq_size // CORES

    owners = lax.axis_size("kv")
    whole, *mine = arrange(owners, weight_tangent, out_weight)
    gathers = [Gather(block, chips) for block in mine]
    gathers[0].behind()
    gathers[0].ahead()
    whole = other_core(whole)

    key_value, key_value_tangents, _ = lax.optimization_barrier(
        (key_value, key_value_tangents, mine[0])
    )
    stacked = jnp.concatenate(
        [key_value[:, 0], key_value_tangents[:, 0], key_value[:, 1], key_value_tangents[:, 1]],
        axis=1,
    )
    prior = lax.ppermute(
        stacked[tokens - WINDOW :], "seq", [(i, i + 1) for i in range(seq_size - 1)]
    )

    doc_ends = jnp.cumsum(doc_lengths)
    doc_starts = doc_ends - doc_lengths
    position = seq_index * tokens + jnp.arange(tokens, dtype=jnp.int32)
    inside = (doc_starts[None, :] <= position[:, None]) & (position[:, None] < doc_ends[None, :])
    doc_first = jnp.sum(jnp.where(inside, doc_starts[None, :], 0), axis=1)
    lower = jnp.maximum(doc_first, position - WINDOW + 1)
    low = lower - (position // STRETCH * STRETCH - WINDOW)
    low = jnp.broadcast_to(low[:, None], (tokens, 128))

    step = jnp.arange(chips, dtype=jnp.int32)
    chip, core = seq_index // CORES, seq_index % CORES
    owner = (chip - step + chips) % chips * CORES
    order = jnp.stack([owner + core, owner + 1 - core], axis=1).reshape(-1)
    whole_heads = order.shape[0] == heads

    def attend(part, context):
        heads_order = order if whole_heads else jnp.arange(heads, dtype=jnp.int32)
        pair = attention(part, heads_order, queries, query_tangent, context, low)
        if not whole_heads:
            pair = jnp.take(pair.reshape(half, 2, seq_size, -1), order, axis=2)
            pair = pair.reshape(half, 2 * width)
        return pair

    pair_second = attend(1, stacked)
    state, held, pair_second, prior = together(
        gathers[0].get(), gathers[1].blocks, pair_second, prior
    )
    gathers[0].put(state)
    gathers[1].blocks = dict(held)
    gathers[0].farther_ahead()
    gathers[0].farther_behind()
    gathers[0].exchange(1, -1)
    gathers[1].ahead()
    pair_first = attend(0, jnp.concatenate([prior, stacked[:half]], axis=0))

    pairs, sent = (pair_first, pair_second), ()
    received, outputs = [], ()
    for chunk in range(CHUNKS):
        states = [gathering.get() for gathering in gathers]
        arrived = received[chunk - 2] if chunk >= 2 else ()
        states, pairs, whole, arrived, sent = together(states, pairs, whole, arrived, sent)
        for gathering, state in zip(gathers, states):
            gathering.put(state)
        if chunk + 1 < CHUNKS:
            gathers[chunk + 1].behind()
            gathers[chunk + 1].farther_ahead()
            gathers[chunk + 1].farther_behind()
            gathers[chunk + 1].exchange(1)
        if chunk + 2 < CHUNKS:
            gathers[chunk + 2].ahead()
        gathers[chunk].exchange()
        sent = project(owners, chunk, pairs, whole, gathers[chunk].pieces())
        received.append(lax.all_to_all(sent, "kv", 0, 0, tiled=True))
        if chunk >= 2:
            outputs = finish(chunk - 2, outputs, arrived)
    for chunk in range(max(CHUNKS - 2, 0), CHUNKS):
        outputs = finish(chunk, outputs, received[chunk])
    return tuple(outputs)


def solution(mesh):
    in_specs = (
        P("seq", "kv"),
        P("seq", "kv"),
        P("seq", None, "kv"),
        P("seq", None, "kv"),
        P(),
        P(("kv", "seq"), None),
        P(("kv", "seq"), None),
    )
    out_specs = (P("seq", "kv"), P("seq", "kv"))
    return jax.shard_map(body, mesh=mesh, in_specs=in_specs, out_specs=out_specs, check_vma=False)
```

```python
import functools
import math

import jax
import jax.numpy as jnp
from jax import lax
from jax.experimental import pallas as pl
from jax.experimental.pallas import tpu as pltpu
from jax.sharding import PartitionSpec as P

STRETCH = 32
WINDOW = 224
CHUNKS = 4
TILE = 128
CORES = 2

masked_score = -1e30
vmem_bytes = 16 * 1024 * 1024


def arrange_kernel(owners, tangent_ref, value_ref, *refs):
    *chunk_refs, sems = refs
    columns = tangent_ref.shape[1] // owners
    part = columns // len(chunk_refs)
    copies = []
    for chunk, chunk_ref in enumerate(chunk_refs):
        for mat, ref in enumerate((tangent_ref, value_ref)):
            for owner in range(owners):
                source = ref.at[:, pl.ds(owner * columns + chunk * part, part)]
                target = chunk_ref.at[0, mat, :, pl.ds(owner * part, part)]
                copies.append(pltpu.make_async_copy(source, target, sems.at[len(copies)]))
                copies[-1].start()
    for copy in copies:
        copy.wait()


def arrange(owners, tangent, value):
    rows, columns = value.shape
    shape = jax.ShapeDtypeStruct((1, 2, rows, columns // CHUNKS), value.dtype)
    return pl.pallas_call(
        functools.partial(arrange_kernel, owners),
        in_specs=[pl.BlockSpec(memory_space=pltpu.HBM)] * 2,
        out_specs=[pl.BlockSpec(memory_space=pl.ANY)] * CHUNKS,
        out_shape=[shape] * CHUNKS,
        scratch_shapes=[pltpu.SemaphoreType.DMA((2 * CHUNKS * owners,))],
        compiler_params=pltpu.CompilerParams(vmem_limit_bytes=vmem_bytes),
        name="arrange",
    )(tangent, value)


def attention_kernel(heads, head_dim, offset, order_ref, q_ref, qt_ref, ctx_ref, low_ref, out_ref):
    rows = q_ref.shape[0]
    span = WINDOW + STRETCH
    width = heads * head_dim
    score_scale = 1.0 / math.sqrt(head_dim)
    to_log2 = score_scale * math.log2(math.e)
    step = pl.program_id(0)
    transposed = (((1,), (1,)), ((), ()))
    column = lax.broadcasted_iota(jnp.int32, (STRETCH, span), 1)
    row = lax.broadcasted_iota(jnp.int32, (STRETCH, span), 0)
    causal = column <= row + WINDOW
    starts = [pl.multiple_of(order_ref[h] * head_dim, head_dim) for h in range(heads)]

    def window(part):
        return pl.ds(pl.multiple_of(offset + step * rows + part * STRETCH, STRETCH), span)

    def score(part):
        here = slice(part * STRETCH, (part + 1) * STRETCH)
        keys = ctx_ref[window(part), : 2 * head_dim]
        q = jnp.concatenate([q_ref[here, pl.ds(start, head_dim)] for start in starts], axis=0)
        qt = jnp.concatenate([qt_ref[here, pl.ds(start, head_dim)] for start in starts], axis=0)
        scores = lax.dot_general(
            q, keys[:, :head_dim], transposed, preferred_element_type=jnp.float32
        )
        tangent = lax.dot_general(
            jnp.concatenate([qt, q], axis=1), keys, transposed, preferred_element_type=jnp.float32
        )
        return scores.reshape(heads, STRETCH, span), tangent.reshape(heads, STRETCH, span)

    def weigh(part, scores, tangent):
        low = low_ref[part * STRETCH : (part + 1) * STRETCH, :]
        low = jnp.concatenate([low] * (span // low.shape[1]), axis=1)
        admitted = causal & (column >= low)
        scores = jnp.where(admitted[None], scores, masked_score)
        peak = jnp.max(scores, axis=-1, keepdims=True)
        exponent = jnp.exp2((scores - peak) * to_log2)
        inverse = 1.0 / jnp.sum(exponent, axis=-1, keepdims=True)
        mean = jnp.sum(exponent * tangent, axis=-1, keepdims=True) * inverse
        prob = exponent * inverse
        prob_low = prob.astype(jnp.bfloat16).reshape(heads * STRETCH, span)
        tan_low = (prob * ((tangent - mean) * score_scale)).astype(jnp.bfloat16)
        return prob_low, tan_low.reshape(heads * STRETCH, span)

    def gather_values(part, prob_low, tan_low):
        here = slice(part * STRETCH, (part + 1) * STRETCH)
        values = ctx_ref[window(part), 2 * head_dim :]
        both = jnp.dot(prob_low, values, preferred_element_type=jnp.float32)
        more = jnp.dot(tan_low, values[:, :head_dim], preferred_element_type=jnp.float32)
        out = both[:, :head_dim].astype(jnp.bfloat16)
        out_tan = (both[:, head_dim:] + more).astype(jnp.bfloat16)
        for h in range(heads):
            of = slice(h * STRETCH, (h + 1) * STRETCH)
            out_ref[here, h * head_dim : (h + 1) * head_dim] = out[of]
            out_ref[here, width + h * head_dim : width + (h + 1) * head_dim] = out_tan[of]

    parts = rows // STRETCH
    scored, weighed = score(0), None
    for part in range(parts):
        following = score(part + 1) if part + 1 < parts else None
        if weighed is not None:
            gather_values(part - 1, *weighed)
        weighed = weigh(part, *scored)
        scored = following
    gather_values(parts - 1, *weighed)


def attention(half, order, queries, query_tangent, context, low):
    tokens, width = queries.shape[0] // 2, queries.shape[1]
    head_dim = context.shape[1] // 4
    heads = width // head_dim
    elements = tokens * heads * (WINDOW + STRETCH)
    steps = tokens // TILE
    offset = context.shape[0] - tokens - WINDOW
    return pl.pallas_call(
        functools.partial(attention_kernel, heads, head_dim, offset),
        grid=(steps,),
        in_specs=[
            pl.BlockSpec(memory_space=pltpu.SMEM),
            pl.BlockSpec((TILE, width), lambda i: (half * steps + i, 0)),
            pl.BlockSpec((TILE, width), lambda i: (half * steps + i, 0)),
            pl.BlockSpec(context.shape, lambda i: (0, 0)),
            pl.BlockSpec((TILE, low.shape[1]), lambda i: (half * steps + i, 0)),
        ],
        out_specs=pl.BlockSpec((TILE, 2 * width), lambda i: (i, 0)),
        out_shape=jax.ShapeDtypeStruct((tokens, 2 * width), jnp.bfloat16),
        compiler_params=pltpu.CompilerParams(vmem_limit_bytes=vmem_bytes),
        cost_estimate=pl.CostEstimate(
            flops=elements, bytes_accessed=tokens, transcendentals=0
        ),
        name="attention",
    )(order, queries, query_tangent, context, low)


def project_kernel(chunk, places, place_ref, first_ref, second_ref, *refs):
    *array_refs, send_ref, keep_ref, weight_ref, sems = refs
    step, steps = pl.program_id(0), pl.num_programs(0)
    depth = weight_ref.shape[1]
    owners = place_ref.shape[0]
    part = weight_ref.shape[2] // owners
    rows = depth // len(places)
    columns = array_refs[0].shape[1] // owners

    @pl.when(step == 0)
    def _():
        copies = []
        for place, (kind, which, index) in enumerate(places):
            for mat in range(2):
                for position in range(owners):
                    owner = place_ref[position]
                    if kind:
                        start = pl.multiple_of(owner * part, part)
                        source = array_refs[which].at[index, mat, :, pl.ds(start, part)]
                    else:
                        start = pl.multiple_of(owner * columns + chunk * part, part)
                        source = array_refs[which + mat].at[:, pl.ds(start, part)]
                    target = weight_ref.at[
                        mat, pl.ds(place * rows, rows), pl.ds(position * part, part)
                    ]
                    copies.append(pltpu.make_async_copy(source, target, sems.at[len(copies)]))
                    copies[-1].start()
        for copy in copies:
            copy.wait()

    def run(pair_ref):
        dot = functools.partial(jnp.dot, preferred_element_type=jnp.float32)
        value = dot(pair_ref[:, :depth], weight_ref[1])
        tangent = dot(pair_ref[:, :depth], weight_ref[0]) + dot(pair_ref[:, depth:], weight_ref[1])
        for mat, result in enumerate((value, tangent)):
            send_ref[mat] = result[:, : 2 * part].astype(send_ref.dtype)
            keep_ref[mat] = result[:, 2 * part :]

    @pl.when(step < steps // 2)
    def _():
        run(first_ref)

    @pl.when(step >= steps // 2)
    def _():
        run(second_ref)


def project(chunk, places, order, pairs, arrays, columns):
    tokens, width = pairs[0].shape
    tile = min(2 * TILE, tokens)
    steps = tokens // tile
    block = pl.BlockSpec((2, tile, columns // 2), lambda i: (0, i, 0))
    out = (2, 2 * tokens, columns // 2)
    return pl.pallas_call(
        functools.partial(project_kernel, chunk, places),
        grid=(2 * steps,),
        in_specs=[
            pl.BlockSpec(memory_space=pltpu.SMEM),
            pl.BlockSpec((tile, width), lambda i: (jnp.minimum(i, steps - 1), 0)),
            pl.BlockSpec((tile, width), lambda i: (jnp.maximum(i - steps, 0), 0)),
            *[pl.BlockSpec(memory_space=pl.ANY)] * len(arrays),
        ],
        out_specs=[block, block],
        out_shape=[jax.ShapeDtypeStruct(out, jnp.bfloat16), jax.ShapeDtypeStruct(out, jnp.float32)],
        scratch_shapes=[
            pltpu.VMEM((2, width // 2, columns), jnp.bfloat16),
            pltpu.SemaphoreType.DMA((2 * len(places) * order.shape[0],)),
        ],
        compiler_params=pltpu.CompilerParams(vmem_limit_bytes=vmem_bytes),
        cost_estimate=pl.CostEstimate(
            flops=tokens * columns, bytes_accessed=tokens, transcendentals=0
        ),
        name="project",
    )(order, *pairs, *arrays)


def finish_kernel(keep_ref, received_ref, last_ref, *refs):
    for mat, ref in enumerate(refs[-2:]):
        ref[...] = (keep_ref[mat] + received_ref[mat] + last_ref[mat]).astype(ref.dtype)


def finish(chunk, outputs, keep, received, last):
    _, tokens, part = last.shape
    shape = jax.ShapeDtypeStruct((tokens, part * CHUNKS), jnp.bfloat16)
    tile = tokens // 2
    return pl.pallas_call(
        finish_kernel,
        grid=(tokens // tile,),
        in_specs=[
            pl.BlockSpec((2, tile, part), lambda i: (0, i, 1)),
            pl.BlockSpec((2, tile, part), lambda i: (0, i, 0)),
            pl.BlockSpec((2, tile, part), lambda i: (0, i, 0)),
            *[pl.BlockSpec(memory_space=pl.ANY)] * len(outputs),
        ],
        out_specs=[pl.BlockSpec((tile, part), lambda i: (i, chunk))] * 2,
        out_shape=[shape, shape],
        input_output_aliases={3 + i: i for i in range(len(outputs))},
        compiler_params=pltpu.CompilerParams(vmem_limit_bytes=vmem_bytes),
        name="finish",
    )(keep, received, last, *outputs)


def across(block, stage):
    owners, places = lax.axis_size("kv"), lax.axis_size("seq")
    route = []
    for owner in range(owners):
        for place in range(places):
            flip = 1 + (place + stage) % CORES
            route.append((owner * places + place, (owner ^ flip) * places + place))
    return lax.ppermute(block, ("kv", "seq"), route)


def along(block, chips):
    size = lax.axis_size("seq")
    return lax.ppermute(block, "seq", [(i, (i + CORES * chips) % size) for i in range(size)])


def other_core(block):
    return lax.ppermute(block, "seq", [(i, i ^ 1) for i in range(lax.axis_size("seq"))])


def together(*trees):
    return lax.optimization_barrier(trees)


class Pieces:
    def __init__(self):
        self.arrays, self.near, self.far = [], {}, {}

    def add(self, table, members, array):
        for index, member in enumerate(members):
            table[member] = (len(self.arrays), index)
        self.arrays.append(array)

    def send(self, members, direction, chips):
        blocks = [
            self.arrays[which][index : index + 1]
            for which, index in (self.near[member] for member in members)
        ]
        block = jnp.concatenate(blocks) if len(blocks) > 1 else blocks[0]
        moved = [(chunk, (step + direction) % chips) for chunk, step in members]
        self.add(self.near, moved, along(block, direction))

    def exchange(self):
        waiting = {}
        for member, (which, index) in self.near.items():
            if member[1] and member not in self.far:
                waiting.setdefault(which, []).append((index, member))
        for which, members in waiting.items():
            members = [member for _, member in sorted(members)]
            self.add(self.far, members, other_core(self.arrays[which]))

    def taken(self, chunk, chips):
        members = [self.near[chunk, step] for step in range(1, chips)]
        others = [self.far[chunk, step] for step in range(1, chips)]
        return [piece for pair in zip(members, others) for piece in pair]


def body(
    queries, query_tangent, key_value, key_value_tangents, doc_lengths, out_weight, weight_tangent
):
    tokens, width = queries.shape
    head_dim = key_value.shape[2]
    heads = width // head_dim
    half = tokens // 2
    seq_index = lax.axis_index("seq")
    kv_index = lax.axis_index("kv")
    seq_size = lax.axis_size("seq")
    chips = seq_size // CORES

    owners = lax.axis_size("kv")
    core = seq_index % CORES
    flips = jnp.stack([1 + core, 3 + 0 * core, 2 - core, 0 * core])
    places_order = (kv_index ^ flips).astype(jnp.int32)
    mine = arrange(owners, weight_tangent, out_weight)
    pieces = Pieces()
    for chunk in range(CHUNKS):
        pieces.add(pieces.near, [(chunk, 0)], mine[chunk])
    pieces.send([(0, 0)], -1, chips)
    pieces.send([(0, 0)], 1, chips)
    other_tangent, other_value = other_core(weight_tangent), other_core(out_weight)

    key_value, key_value_tangents, _ = lax.optimization_barrier(
        (key_value, key_value_tangents, mine[0])
    )
    stacked = jnp.concatenate(
        [key_value[:, 0], key_value_tangents[:, 0], key_value[:, 1], key_value_tangents[:, 1]],
        axis=1,
    )
    prior = lax.ppermute(
        stacked[tokens - WINDOW :], "seq", [(i, i + 1) for i in range(seq_size - 1)]
    )

    doc_ends = jnp.cumsum(doc_lengths)
    doc_starts = doc_ends - doc_lengths
    position = seq_index * tokens + jnp.arange(tokens, dtype=jnp.int32)
    inside = (doc_starts[None, :] <= position[:, None]) & (position[:, None] < doc_ends[None, :])
    doc_first = jnp.sum(jnp.where(inside, doc_starts[None, :], 0), axis=1)
    lower = jnp.maximum(doc_first, position - WINDOW + 1)
    low = lower - (position // STRETCH * STRETCH - WINDOW)
    low = jnp.broadcast_to(low[:, None], (tokens, 128))

    step = jnp.arange(chips, dtype=jnp.int32)
    chip = seq_index // CORES
    owner = (chip - step + chips) % chips * CORES
    order = jnp.stack([owner + core, owner + 1 - core], axis=1).reshape(-1)
    whole_heads = order.shape[0] == heads

    def attend(part, context):
        heads_order = order if whole_heads else jnp.arange(heads, dtype=jnp.int32)
        pair = attention(part, heads_order, queries, query_tangent, context, low)
        if not whole_heads:
            pair = jnp.take(pair.reshape(half, 2, seq_size, -1), order, axis=2)
            pair = pair.reshape(half, 2 * width)
        return pair

    forward, backward = chips // 2, (chips - 1) // 2
    columns = out_weight.shape[1] // CHUNKS
    part = columns // owners

    def hop(chunk):
        first = [(chunk, 1)] if chunk < CHUNKS else []
        if chunk and first:
            pieces.send([(chunk, 0)], -1, chips)
        following = [(chunk + 1, 0)] if chunk + 1 < CHUNKS else []
        if first + following:
            pieces.send(first + following, 1, chips)
        for step in range(2, forward if first else 0):
            pieces.send([(chunk, step)], 1, chips)
        for step in range(1, backward if first else 0):
            pieces.send([(chunk, chips - step)], -1, chips)

    def add_stage(keep, received):
        return (keep[:, :, :part] + received[:, :, part:]).astype(jnp.bfloat16)

    pair_second = attend(1, stacked)
    pieces.arrays, pair_second, prior = together(pieces.arrays, pair_second, prior)
    pieces.exchange()
    hop(0)
    pair_first = attend(0, jnp.concatenate([prior, stacked[:half]], axis=0))

    pairs, send, sums = (pair_first, pair_second), (), ()
    raw = (weight_tangent, out_weight, other_tangent, other_value)
    kept, received, last, outputs = [], [], [], ()
    for chunk in range(CHUNKS):
        pieces.arrays, pairs, raw, send, sums = together(pieces.arrays, pairs, raw, send, sums)
        pieces.exchange()
        if chunk + 1 < CHUNKS:
            hop(chunk + 1)
        places = [(0, 0, 0), (0, 2, 0)] + [
            (1, 4 + place, index)
            for place, (_, index) in enumerate(pieces.taken(chunk, chips))
        ]
        arrays = [pieces.arrays[which] for which, _ in pieces.taken(chunk, chips)]
        if chunk >= 2:
            last[chunk - 2], pairs = together(last[chunk - 2], pairs)
        send, keep = project(chunk, places, places_order, pairs, (*raw, *arrays), columns)
        kept.append(keep)
        received.append(across(send, 0))
        if chunk:
            received[chunk - 1], send = together(received[chunk - 1], send)
            sums = add_stage(kept[chunk - 1], received[chunk - 1])
            last.append(across(sums, 1))
            if chunk >= 2:
                outputs = finish(
                    chunk - 2, outputs, kept[chunk - 2], received[chunk - 2], last[chunk - 2]
                )
    last.append(across(add_stage(kept[-1], received[-1]), 1))
    for chunk in range(max(CHUNKS - 2, 0), CHUNKS):
        outputs = finish(chunk, outputs, kept[chunk], received[chunk], last[chunk])
    return tuple(outputs)


def solution(mesh):
    in_specs = (
        P("seq", "kv"),
        P("seq", "kv"),
        P("seq", None, "kv"),
        P("seq", None, "kv"),
        P(),
        P(("kv", "seq"), None),
        P(("kv", "seq"), None),
    )
    out_specs = (P("seq", "kv"), P("seq", "kv"))
    return jax.shard_map(body, mesh=mesh, in_specs=in_specs, out_specs=out_specs, check_vma=False)
```

```python
import functools
import math

import jax
import jax.numpy as jnp
from jax import lax
from jax.experimental import pallas as pl
from jax.experimental.pallas import tpu as pltpu
from jax.sharding import PartitionSpec as P

STRETCH = 32
WINDOW = 224
CHUNKS = 4
SCHEDULED_GFLOPS = (5, 5, 1.5, 0.01)
TILE = 128
CORES = 2

masked_score = -1e30
vmem_bytes = 12 * 1024 * 1024


def arrange_kernel(owner_ref, tangent_ref, value_ref, whole_ref, *chunk_refs):
    owners = owner_ref.shape[0]
    columns = tangent_ref.shape[1] // owners
    part = columns // len(chunk_refs)
    for chunk, chunk_ref in enumerate(chunk_refs):
        for place in range(owners):
            start = pl.multiple_of(owner_ref[place] * columns + chunk * part, part)
            to = slice(place * part, (place + 1) * part)
            for mat, ref in enumerate((tangent_ref, value_ref)):
                block = ref[:, pl.ds(start, part)]
                whole_ref[chunk, mat, :, to] = block
                chunk_ref[0, mat, :, to] = block


def arrange(owners, tangent, value):
    rows, columns = value.shape
    shapes = [
        jax.ShapeDtypeStruct((count, 2, rows, columns // CHUNKS), value.dtype)
        for count in [CHUNKS] + [1] * CHUNKS
    ]
    return pl.pallas_call(
        arrange_kernel,
        in_specs=[pl.BlockSpec(memory_space=pltpu.SMEM)]
        + [pl.BlockSpec(memory_space=pltpu.VMEM)] * 2,
        out_specs=[pl.BlockSpec(memory_space=pltpu.VMEM)] * len(shapes),
        out_shape=shapes,
        compiler_params=pltpu.CompilerParams(vmem_limit_bytes=vmem_bytes),
        name="arrange",
    )(owners, tangent, value)


def attention_kernel(heads, head_dim, offset, order_ref, q_ref, qt_ref, ctx_ref, low_ref, out_ref):
    rows = q_ref.shape[0]
    span = WINDOW + STRETCH
    width = heads * head_dim
    score_scale = 1.0 / math.sqrt(head_dim)
    to_log2 = score_scale * math.log2(math.e)
    step = pl.program_id(0)
    transposed = (((1,), (1,)), ((), ()))
    column = lax.broadcasted_iota(jnp.int32, (STRETCH, span), 1)
    row = lax.broadcasted_iota(jnp.int32, (STRETCH, span), 0)
    causal = column <= row + WINDOW
    starts = [pl.multiple_of(order_ref[h] * head_dim, head_dim) for h in range(heads)]

    def window(part):
        return pl.ds(pl.multiple_of(offset + step * rows + part * STRETCH, STRETCH), span)

    def score(part):
        here = slice(part * STRETCH, (part + 1) * STRETCH)
        keys = ctx_ref[window(part), : 2 * head_dim]
        q = jnp.concatenate([q_ref[here, pl.ds(start, head_dim)] for start in starts], axis=0)
        qt = jnp.concatenate([qt_ref[here, pl.ds(start, head_dim)] for start in starts], axis=0)
        scores = lax.dot_general(
            q, keys[:, :head_dim], transposed, preferred_element_type=jnp.float32
        )
        tangent = lax.dot_general(
            jnp.concatenate([qt, q], axis=1), keys, transposed, preferred_element_type=jnp.float32
        )
        return scores.reshape(heads, STRETCH, span), tangent.reshape(heads, STRETCH, span)

    def weigh(part, scores, tangent):
        low = low_ref[part * STRETCH : (part + 1) * STRETCH, :]
        low = jnp.concatenate([low] * (span // low.shape[1]), axis=1)
        admitted = causal & (column >= low)
        scores = jnp.where(admitted[None], scores, masked_score)
        peak = jnp.max(scores, axis=-1, keepdims=True)
        exponent = jnp.exp2((scores - peak) * to_log2)
        inverse = 1.0 / jnp.sum(exponent, axis=-1, keepdims=True)
        mean = jnp.sum(exponent * tangent, axis=-1, keepdims=True) * inverse
        prob = exponent * inverse
        prob_low = prob.astype(jnp.bfloat16).reshape(heads * STRETCH, span)
        tan_low = (prob * ((tangent - mean) * score_scale)).astype(jnp.bfloat16)
        return prob_low, tan_low.reshape(heads * STRETCH, span)

    def gather_values(part, prob_low, tan_low):
        here = slice(part * STRETCH, (part + 1) * STRETCH)
        values = ctx_ref[window(part), 2 * head_dim :]
        both = jnp.dot(prob_low, values, preferred_element_type=jnp.float32)
        more = jnp.dot(tan_low, values[:, :head_dim], preferred_element_type=jnp.float32)
        out = both[:, :head_dim].astype(jnp.bfloat16)
        out_tan = (both[:, head_dim:] + more).astype(jnp.bfloat16)
        for h in range(heads):
            of = slice(h * STRETCH, (h + 1) * STRETCH)
            out_ref[here, h * head_dim : (h + 1) * head_dim] = out[of]
            out_ref[here, width + h * head_dim : width + (h + 1) * head_dim] = out_tan[of]

    parts = rows // STRETCH
    scored, weighed = score(0), None
    for part in range(parts):
        following = score(part + 1) if part + 1 < parts else None
        if weighed is not None:
            gather_values(part - 1, *weighed)
        weighed = weigh(part, *scored)
        scored = following
    gather_values(parts - 1, *weighed)


def attention(half, order, queries, query_tangent, context, low):
    tokens, width = queries.shape[0] // 2, queries.shape[1]
    head_dim = context.shape[1] // 4
    heads = width // head_dim
    elements = tokens * heads * (WINDOW + STRETCH)
    steps = tokens // TILE
    offset = context.shape[0] - tokens - WINDOW
    return pl.pallas_call(
        functools.partial(attention_kernel, heads, head_dim, offset),
        grid=(steps,),
        in_specs=[
            pl.BlockSpec(memory_space=pltpu.SMEM),
            pl.BlockSpec((TILE, width), lambda i: (half * steps + i, 0)),
            pl.BlockSpec((TILE, width), lambda i: (half * steps + i, 0)),
            pl.BlockSpec(context.shape, lambda i: (0, 0)),
            pl.BlockSpec((TILE, low.shape[1]), lambda i: (half * steps + i, 0)),
        ],
        out_specs=pl.BlockSpec((TILE, 2 * width), lambda i: (i, 0)),
        out_shape=jax.ShapeDtypeStruct((tokens, 2 * width), jnp.bfloat16),
        compiler_params=pltpu.CompilerParams(vmem_limit_bytes=vmem_bytes),
        cost_estimate=pl.CostEstimate(
            flops=elements, bytes_accessed=tokens, transcendentals=0
        ),
        name="attention",
    )(order, queries, query_tangent, context, low)


def project_kernel(indices, first_ref, second_ref, *refs):
    *piece_refs, send_ref, keep_ref, weight_ref, sems = refs
    step, steps = pl.program_id(0), pl.num_programs(0)
    width, columns = weight_ref.shape[1:]
    rows = width // len(indices)
    near = width // 2
    part = columns // 4

    @pl.when(step == 0)
    def _():
        copies = []
        for place, (index, ref) in enumerate(zip(indices, piece_refs)):
            target = weight_ref.at[:, pl.ds(place * rows, rows), :]
            copies.append(pltpu.make_async_copy(ref.at[index], target, sems.at[place]))
            copies[-1].start()
        for copy in copies:
            copy.wait()

    def run(pair_ref):
        dot = functools.partial(jnp.dot, preferred_element_type=jnp.float32)

        def products(mine, of):
            return dot(pair_ref[:, mine], weight_ref[1, of]), dot(
                pair_ref[:, mine], weight_ref[0, of]
            ) + dot(pair_ref[:, slice(width + mine.start, width + mine.stop)], weight_ref[1, of])

        here = products(slice(0, near), slice(0, near))
        there = products(slice(near, width), slice(near, width))
        for mat in range(2):
            for place, crossed in enumerate((2, 1, 0, 3)):
                to = slice(place * part, (place + 1) * part)
                total = here[mat][:, to] + there[mat][:, crossed * part : (crossed + 1) * part]
                ref = send_ref if place < 2 else keep_ref
                at = place % 2 * part
                ref[mat, :, at : at + part] = total.astype(ref.dtype)

    @pl.when(step < steps // 2)
    def _():
        run(first_ref)

    @pl.when(step >= steps // 2)
    def _():
        run(second_ref)


def project(gflops, pairs, pieces):
    tokens, width = pairs[0].shape
    tile = min(2 * TILE, tokens)
    steps = tokens // tile
    indices = [index for index, _ in pieces]
    arrays = [array for _, array in pieces]
    columns = arrays[0].shape[3]
    block = pl.BlockSpec((2, tile, columns // 2), lambda i: (0, i, 0))
    out = jax.ShapeDtypeStruct((2, 2 * tokens, columns // 2), jnp.bfloat16)
    return pl.pallas_call(
        functools.partial(project_kernel, indices),
        grid=(2 * steps,),
        in_specs=[
            pl.BlockSpec((tile, width), lambda i: (jnp.minimum(i, steps - 1), 0)),
            pl.BlockSpec((tile, width), lambda i: (jnp.maximum(i - steps, 0), 0)),
            *[pl.BlockSpec(memory_space=pl.ANY)] * len(arrays),
        ],
        out_specs=[block, block],
        out_shape=[out, out],
        scratch_shapes=[
            pltpu.VMEM((2, width // 2, columns), jnp.bfloat16),
            pltpu.SemaphoreType.DMA((len(arrays),)),
        ],
        compiler_params=pltpu.CompilerParams(vmem_limit_bytes=vmem_bytes),
        cost_estimate=pl.CostEstimate(
            flops=int(gflops * 1e9), bytes_accessed=tokens, transcendentals=0
        ),
        name="project",
    )(*pairs, *arrays)


def finish_kernel(keep_ref, received_ref, last_ref, *refs):
    for mat, ref in enumerate(refs[-2:]):
        total = keep_ref[mat].astype(jnp.float32) + received_ref[mat] + last_ref[mat]
        ref[...] = total.astype(ref.dtype)


def finish(chunk, outputs, keep, received, last):
    _, tokens, part = last.shape
    shape = jax.ShapeDtypeStruct((tokens, part * CHUNKS), jnp.bfloat16)
    tile = tokens // 2
    return pl.pallas_call(
        finish_kernel,
        grid=(tokens // tile,),
        in_specs=[
            pl.BlockSpec((2, tile, part), lambda i: (0, i, 1)),
            pl.BlockSpec((2, tile, part), lambda i: (0, i, 0)),
            pl.BlockSpec((2, tile, part), lambda i: (0, i, 0)),
            *[pl.BlockSpec(memory_space=pl.ANY)] * len(outputs),
        ],
        out_specs=[pl.BlockSpec((tile, part), lambda i: (i, chunk))] * 2,
        out_shape=[shape, shape],
        input_output_aliases={3 + i: i for i in range(len(outputs))},
        compiler_params=pltpu.CompilerParams(vmem_limit_bytes=vmem_bytes),
        name="finish",
    )(keep, received, last, *outputs)


def across(block, stage):
    owners, places = lax.axis_size("kv"), lax.axis_size("seq")
    route = []
    for owner in range(owners):
        for place in range(places):
            flip = 1 + (place + stage) % CORES
            route.append((owner * places + place, (owner ^ flip) * places + place))
    return lax.ppermute(block, ("kv", "seq"), route)


def along(block, chips):
    size = lax.axis_size("seq")
    return lax.ppermute(block, "seq", [(i, (i + CORES * chips) % size) for i in range(size)])


def other_core(block):
    return lax.ppermute(block, "seq", [(i, i ^ 1) for i in range(lax.axis_size("seq"))])


def together(*trees):
    return lax.optimization_barrier(trees)


class Gather:
    def __init__(self, mine, chips):
        self.near, self.far = {0: mine}, {}
        self.chips = chips
        self.forward, self.backward = chips // 2, (chips - 1) // 2

    def ahead(self):
        if self.forward:
            self.near[1] = along(self.near[0], 1)

    def behind(self):
        if self.backward:
            self.near[self.chips - 1] = along(self.near[0], -1)

    def farther(self):
        for step in range(2, self.forward + 1):
            self.near[step] = along(self.near[step - 1], 1)
        for step in range(2, self.backward + 1):
            self.near[self.chips - step] = along(self.near[self.chips - step + 1], -1)

    def exchange(self):
        for step in sorted(self.near):
            if step and step not in self.far:
                self.far[step] = other_core(self.near[step])

    def pieces(self, chunk, whole):
        near = [(0, self.near[step]) for step in range(self.chips)]
        far = [(0, self.far[step]) for step in range(1, self.chips)]
        return near + [(chunk, whole)] + far


def body(
    queries, query_tangent, key_value, key_value_tangents, doc_lengths, out_weight, weight_tangent
):
    tokens, width = queries.shape
    head_dim = key_value.shape[2]
    heads = width // head_dim
    half = tokens // 2
    seq_index = lax.axis_index("seq")
    kv_index = lax.axis_index("kv")
    seq_size = lax.axis_size("seq")
    chips = seq_size // CORES

    core = seq_index % CORES
    flips = jnp.stack([1 + core, 3 + 0 * core, 2 - core, 0 * core])
    whole, *mine = arrange((kv_index ^ flips).astype(jnp.int32), weight_tangent, out_weight)
    gathers = [Gather(block, chips) for block in mine]
    gathers[0].behind()
    gathers[0].ahead()
    whole = other_core(whole)

    key_value, key_value_tangents, _ = lax.optimization_barrier(
        (key_value, key_value_tangents, mine[0])
    )
    stacked = jnp.concatenate(
        [key_value[:, 0], key_value_tangents[:, 0], key_value[:, 1], key_value_tangents[:, 1]],
        axis=1,
    )
    prior = lax.ppermute(
        stacked[tokens - WINDOW :], "seq", [(i, i + 1) for i in range(seq_size - 1)]
    )

    doc_ends = jnp.cumsum(doc_lengths)
    doc_starts = doc_ends - doc_lengths
    position = seq_index * tokens + jnp.arange(tokens, dtype=jnp.int32)
    inside = (doc_starts[None, :] <= position[:, None]) & (position[:, None] < doc_ends[None, :])
    doc_first = jnp.sum(jnp.where(inside, doc_starts[None, :], 0), axis=1)
    lower = jnp.maximum(doc_first, position - WINDOW + 1)
    low = lower - (position // STRETCH * STRETCH - WINDOW)
    low = jnp.broadcast_to(low[:, None], (tokens, 128))

    step = jnp.arange(chips, dtype=jnp.int32)
    chip = seq_index // CORES
    owner = (chip - step + chips) % chips * CORES
    order = jnp.concatenate([owner + core, owner + 1 - core])
    whole_heads = order.shape[0] == heads

    def attend(part, context):
        heads_order = order if whole_heads else jnp.arange(heads, dtype=jnp.int32)
        pair = attention(part, heads_order, queries, query_tangent, context, low)
        if not whole_heads:
            pair = jnp.take(pair.reshape(half, 2, seq_size, -1), order, axis=2)
            pair = pair.reshape(half, 2 * width)
        return pair

    part = out_weight.shape[1] // CHUNKS // lax.axis_size("kv")

    def add_stage(keep, received):
        total = keep[:, :, :part].astype(jnp.float32) + received[:, :, part:]
        return total.astype(jnp.bfloat16)

    def settle(*others):
        states = [(gathering.near, gathering.far) for gathering in gathers]
        states, *others = together(states, *others)
        for gathering, (near, far) in zip(gathers, states):
            gathering.near, gathering.far = dict(near), dict(far)
        return others

    pair_second = attend(1, stacked)
    pair_second, prior = settle(pair_second, prior)
    gathers[0].exchange()
    gathers[0].farther()
    gathers[1].ahead()
    pair_first = attend(0, jnp.concatenate([prior, stacked[:half]], axis=0))

    pairs, send, sums = (pair_first, pair_second), (), ()
    kept, received, last, outputs = [], [], [], ()
    for chunk in range(CHUNKS):
        pairs, whole, send, sums = settle(pairs, whole, send, sums)
        gathers[chunk].exchange()
        if chunk + 1 < CHUNKS:
            gathers[chunk + 1].exchange()
            gathers[chunk + 1].behind()
            gathers[chunk + 1].farther()
        if chunk + 2 < CHUNKS:
            gathers[chunk + 2].ahead()
        if 2 <= chunk < CHUNKS - 1:
            last[chunk - 2], pairs = together(last[chunk - 2], pairs)
        send, keep = project(
            SCHEDULED_GFLOPS[chunk], pairs, gathers[chunk].pieces(chunk, whole)
        )
        kept.append(keep)
        received.append(across(send, 0))
        if chunk:
            received[chunk - 1], send = together(received[chunk - 1], send)
            sums = add_stage(kept[chunk - 1], received[chunk - 1])
            last.append(across(sums, 1))
            if chunk >= 2:
                outputs = finish(
                    chunk - 2, outputs, kept[chunk - 2], received[chunk - 2], last[chunk - 2]
                )
    last.append(across(add_stage(kept[-1], received[-1]), 1))
    for chunk in range(max(CHUNKS - 2, 0), CHUNKS):
        outputs = finish(chunk, outputs, kept[chunk], received[chunk], last[chunk])
    return tuple(outputs)


def solution(mesh):
    in_specs = (
        P("seq", "kv"),
        P("seq", "kv"),
        P("seq", None, "kv"),
        P("seq", None, "kv"),
        P(),
        P(("kv", "seq"), None),
        P(("kv", "seq"), None),
    )
    out_specs = (P("seq", "kv"), P("seq", "kv"))
    return jax.shard_map(body, mesh=mesh, in_specs=in_specs, out_specs=out_specs, check_vma=False)
```

```python
import functools
import math

import jax
import jax.numpy as jnp
from jax import lax
from jax.experimental import pallas as pl
from jax.experimental.pallas import tpu as pltpu
from jax.sharding import PartitionSpec as P

STRETCH = 32
WINDOW = 224
CHUNKS = 4
SCHEDULED_GFLOPS = (5, 4, 1.5, 0.01)
TILE = 128
CORES = 2

masked_score = -1e30
vmem_bytes = 12 * 1024 * 1024


def arrange_kernel(owner_ref, tangent_ref, value_ref, whole_ref, *chunk_refs):
    owners = owner_ref.shape[0]
    columns = tangent_ref.shape[1] // owners
    part = columns // len(chunk_refs)
    for chunk, chunk_ref in enumerate(chunk_refs):
        for place in range(owners):
            start = pl.multiple_of(owner_ref[place] * columns + chunk * part, part)
            to = slice(place * part, (place + 1) * part)
            for mat, ref in enumerate((tangent_ref, value_ref)):
                block = ref[:, pl.ds(start, part)]
                whole_ref[chunk, mat, :, to] = block
                chunk_ref[0, mat, :, to] = block


def arrange(owners, tangent, value):
    rows, columns = value.shape
    shapes = [
        jax.ShapeDtypeStruct((count, 2, rows, columns // CHUNKS), value.dtype)
        for count in [CHUNKS] + [1] * CHUNKS
    ]
    return pl.pallas_call(
        arrange_kernel,
        in_specs=[pl.BlockSpec(memory_space=pltpu.SMEM)]
        + [pl.BlockSpec(memory_space=pltpu.VMEM)] * 2,
        out_specs=[pl.BlockSpec(memory_space=pltpu.VMEM)] * len(shapes),
        out_shape=shapes,
        compiler_params=pltpu.CompilerParams(vmem_limit_bytes=vmem_bytes),
        name="arrange",
    )(owners, tangent, value)


def attention_kernel(heads, head_dim, offset, order_ref, q_ref, qt_ref, ctx_ref, low_ref, out_ref):
    rows = q_ref.shape[0]
    span = WINDOW + STRETCH
    width = heads * head_dim
    score_scale = 1.0 / math.sqrt(head_dim)
    to_log2 = score_scale * math.log2(math.e)
    step = pl.program_id(0)
    transposed = (((1,), (1,)), ((), ()))
    column = lax.broadcasted_iota(jnp.int32, (STRETCH, span), 1)
    row = lax.broadcasted_iota(jnp.int32, (STRETCH, span), 0)
    causal = column <= row + WINDOW
    starts = [pl.multiple_of(order_ref[h] * head_dim, head_dim) for h in range(heads)]

    def window(part):
        return pl.ds(pl.multiple_of(offset + step * rows + part * STRETCH, STRETCH), span)

    def score(part):
        here = slice(part * STRETCH, (part + 1) * STRETCH)
        keys = ctx_ref[window(part), : 2 * head_dim]
        q = jnp.concatenate([q_ref[here, pl.ds(start, head_dim)] for start in starts], axis=0)
        qt = jnp.concatenate([qt_ref[here, pl.ds(start, head_dim)] for start in starts], axis=0)
        scores = lax.dot_general(
            q, keys[:, :head_dim], transposed, preferred_element_type=jnp.float32
        )
        tangent = lax.dot_general(
            jnp.concatenate([qt, q], axis=1), keys, transposed, preferred_element_type=jnp.float32
        )
        return scores.reshape(heads, STRETCH, span), tangent.reshape(heads, STRETCH, span)

    def weigh(part, scores, tangent):
        low = low_ref[part * STRETCH : (part + 1) * STRETCH, :]
        low = jnp.concatenate([low] * (span // low.shape[1]), axis=1)
        admitted = causal & (column >= low)
        scores = jnp.where(admitted[None], scores, masked_score)
        peak = jnp.max(scores, axis=-1, keepdims=True)
        exponent = jnp.exp2((scores - peak) * to_log2)
        inverse = 1.0 / jnp.sum(exponent, axis=-1, keepdims=True)
        mean = jnp.sum(exponent * tangent, axis=-1, keepdims=True) * inverse
        prob = exponent * inverse
        prob_low = prob.astype(jnp.bfloat16).reshape(heads * STRETCH, span)
        tan_low = (prob * ((tangent - mean) * score_scale)).astype(jnp.bfloat16)
        return prob_low, tan_low.reshape(heads * STRETCH, span)

    def gather_values(part, prob_low, tan_low):
        here = slice(part * STRETCH, (part + 1) * STRETCH)
        values = ctx_ref[window(part), 2 * head_dim :]
        both = jnp.dot(prob_low, values, preferred_element_type=jnp.float32)
        more = jnp.dot(tan_low, values[:, :head_dim], preferred_element_type=jnp.float32)
        out = both[:, :head_dim].astype(jnp.bfloat16)
        out_tan = (both[:, head_dim:] + more).astype(jnp.bfloat16)
        for h in range(heads):
            of = slice(h * STRETCH, (h + 1) * STRETCH)
            out_ref[here, h * head_dim : (h + 1) * head_dim] = out[of]
            out_ref[here, width + h * head_dim : width + (h + 1) * head_dim] = out_tan[of]

    parts = rows // STRETCH
    scored, weighed = score(0), None
    for part in range(parts):
        following = score(part + 1) if part + 1 < parts else None
        if weighed is not None:
            gather_values(part - 1, *weighed)
        weighed = weigh(part, *scored)
        scored = following
    gather_values(parts - 1, *weighed)


def attention(half, order, queries, query_tangent, context, low):
    tokens, width = queries.shape[0] // 2, queries.shape[1]
    head_dim = context.shape[1] // 4
    heads = width // head_dim
    elements = tokens * heads * (WINDOW + STRETCH)
    steps = tokens // TILE
    offset = context.shape[0] - tokens - WINDOW
    return pl.pallas_call(
        functools.partial(attention_kernel, heads, head_dim, offset),
        grid=(steps,),
        in_specs=[
            pl.BlockSpec(memory_space=pltpu.SMEM),
            pl.BlockSpec((TILE, width), lambda i: (half * steps + i, 0)),
            pl.BlockSpec((TILE, width), lambda i: (half * steps + i, 0)),
            pl.BlockSpec(context.shape, lambda i: (0, 0)),
            pl.BlockSpec((TILE, low.shape[1]), lambda i: (half * steps + i, 0)),
        ],
        out_specs=pl.BlockSpec((TILE, 2 * width), lambda i: (i, 0)),
        out_shape=jax.ShapeDtypeStruct((tokens, 2 * width), jnp.bfloat16),
        compiler_params=pltpu.CompilerParams(vmem_limit_bytes=vmem_bytes),
        cost_estimate=pl.CostEstimate(
            flops=elements, bytes_accessed=tokens, transcendentals=0
        ),
        name="attention",
    )(order, queries, query_tangent, context, low)


def project_kernel(indices, first_ref, second_ref, *refs):
    *piece_refs, send_ref, keep_ref, weight_ref, sems = refs
    step, steps = pl.program_id(0), pl.num_programs(0)
    width, columns = weight_ref.shape[1:]
    rows = width // len(indices)
    near = width // 2
    part = columns // 4

    @pl.when(step == 0)
    def _():
        copies = []
        for place, (index, ref) in enumerate(zip(indices, piece_refs)):
            target = weight_ref.at[:, pl.ds(place * rows, rows), :]
            copies.append(pltpu.make_async_copy(ref.at[index], target, sems.at[place]))
            copies[-1].start()
        for copy in copies:
            copy.wait()

    def run(pair_ref):
        dot = functools.partial(jnp.dot, preferred_element_type=jnp.float32)

        def products(mine, of):
            return dot(pair_ref[:, mine], weight_ref[1, of]), dot(
                pair_ref[:, mine], weight_ref[0, of]
            ) + dot(pair_ref[:, slice(width + mine.start, width + mine.stop)], weight_ref[1, of])

        here = products(slice(0, near), slice(0, near))
        there = products(slice(near, width), slice(near, width))
        for mat in range(2):
            for place, crossed in enumerate((2, 1, 0, 3)):
                to = slice(place * part, (place + 1) * part)
                total = here[mat][:, to] + there[mat][:, crossed * part : (crossed + 1) * part]
                ref = send_ref if place < 2 else keep_ref
                at = place % 2 * part
                ref[mat, :, at : at + part] = total.astype(ref.dtype)

    @pl.when(step < steps // 2)
    def _():
        run(first_ref)

    @pl.when(step >= steps // 2)
    def _():
        run(second_ref)


def project(gflops, pairs, pieces):
    tokens, width = pairs[0].shape
    tile = min(2 * TILE, tokens)
    steps = tokens // tile
    indices = [index for index, _ in pieces]
    arrays = [array for _, array in pieces]
    columns = arrays[0].shape[3]
    block = pl.BlockSpec((2, tile, columns // 2), lambda i: (0, i, 0))
    out = jax.ShapeDtypeStruct((2, 2 * tokens, columns // 2), jnp.bfloat16)
    return pl.pallas_call(
        functools.partial(project_kernel, indices),
        grid=(2 * steps,),
        in_specs=[
            pl.BlockSpec((tile, width), lambda i: (jnp.minimum(i, steps - 1), 0)),
            pl.BlockSpec((tile, width), lambda i: (jnp.maximum(i - steps, 0), 0)),
            *[pl.BlockSpec(memory_space=pl.ANY)] * len(arrays),
        ],
        out_specs=[block, block],
        out_shape=[out, out],
        scratch_shapes=[
            pltpu.VMEM((2, width // 2, columns), jnp.bfloat16),
            pltpu.SemaphoreType.DMA((len(arrays),)),
        ],
        compiler_params=pltpu.CompilerParams(vmem_limit_bytes=vmem_bytes),
        cost_estimate=pl.CostEstimate(
            flops=int(gflops * 1e9), bytes_accessed=tokens, transcendentals=0
        ),
        name="project",
    )(*pairs, *arrays)


def finish_kernel(keep_ref, received_ref, last_ref, *refs):
    for mat, ref in enumerate(refs[-2:]):
        total = keep_ref[mat].astype(jnp.float32) + received_ref[mat] + last_ref[mat]
        ref[...] = total.astype(ref.dtype)


def finish(chunk, outputs, keep, received, last):
    _, tokens, part = last.shape
    shape = jax.ShapeDtypeStruct((tokens, part * CHUNKS), jnp.bfloat16)
    tile = tokens // 2
    return pl.pallas_call(
        finish_kernel,
        grid=(tokens // tile,),
        in_specs=[
            pl.BlockSpec((2, tile, part), lambda i: (0, i, 1)),
            pl.BlockSpec((2, tile, part), lambda i: (0, i, 0)),
            pl.BlockSpec((2, tile, part), lambda i: (0, i, 0)),
            *[pl.BlockSpec(memory_space=pl.ANY)] * len(outputs),
        ],
        out_specs=[pl.BlockSpec((tile, part), lambda i: (i, chunk))] * 2,
        out_shape=[shape, shape],
        input_output_aliases={3 + i: i for i in range(len(outputs))},
        compiler_params=pltpu.CompilerParams(vmem_limit_bytes=vmem_bytes),
        name="finish",
    )(keep, received, last, *outputs)


def across(block, stage):
    owners, places = lax.axis_size("kv"), lax.axis_size("seq")
    route = []
    for owner in range(owners):
        for place in range(places):
            flip = 1 + (place + stage) % CORES
            route.append((owner * places + place, (owner ^ flip) * places + place))
    return lax.ppermute(block, ("kv", "seq"), route)


def along(block, chips):
    size = lax.axis_size("seq")
    return lax.ppermute(block, "seq", [(i, (i + CORES * chips) % size) for i in range(size)])


def other_core(block):
    return lax.ppermute(block, "seq", [(i, i ^ 1) for i in range(lax.axis_size("seq"))])


def together(*trees):
    return lax.optimization_barrier(trees)


class Gather:
    def __init__(self, mine, chips):
        self.near, self.far = {0: mine}, {}
        self.chips = chips
        self.forward, self.backward = chips // 2, (chips - 1) // 2

    def ahead(self):
        if self.forward:
            self.near[1] = along(self.near[0], 1)

    def behind(self):
        if self.backward:
            self.near[self.chips - 1] = along(self.near[0], -1)

    def farther(self):
        for step in range(2, self.forward + 1):
            self.near[step] = along(self.near[step - 1], 1)
        for step in range(2, self.backward + 1):
            self.near[self.chips - step] = along(self.near[self.chips - step + 1], -1)

    def exchange(self):
        for step in sorted(self.near):
            if step and step not in self.far:
                self.far[step] = other_core(self.near[step])

    def pieces(self, chunk, whole):
        near = [(0, self.near[step]) for step in range(self.chips)]
        far = [(0, self.far[step]) for step in range(1, self.chips)]
        return near + [(chunk, whole)] + far


def body(
    queries, query_tangent, key_value, key_value_tangents, doc_lengths, out_weight, weight_tangent
):
    tokens, width = queries.shape
    head_dim = key_value.shape[2]
    heads = width // head_dim
    half = tokens // 2
    seq_index = lax.axis_index("seq")
    kv_index = lax.axis_index("kv")
    seq_size = lax.axis_size("seq")
    chips = seq_size // CORES

    core = seq_index % CORES
    flips = jnp.stack([1 + core, 3 + 0 * core, 2 - core, 0 * core])
    whole, *mine = arrange((kv_index ^ flips).astype(jnp.int32), weight_tangent, out_weight)
    gathers = [Gather(block, chips) for block in mine]
    gathers[0].behind()
    gathers[0].ahead()
    gathers[1].ahead()
    whole = other_core(whole)

    key_value, key_value_tangents, _ = lax.optimization_barrier(
        (key_value, key_value_tangents, mine[0])
    )
    stacked = jnp.concatenate(
        [key_value[:, 0], key_value_tangents[:, 0], key_value[:, 1], key_value_tangents[:, 1]],
        axis=1,
    )
    prior = lax.ppermute(
        stacked[tokens - WINDOW :], "seq", [(i, i + 1) for i in range(seq_size - 1)]
    )

    doc_ends = jnp.cumsum(doc_lengths)
    doc_starts = doc_ends - doc_lengths
    position = seq_index * tokens + jnp.arange(tokens, dtype=jnp.int32)
    inside = (doc_starts[None, :] <= position[:, None]) & (position[:, None] < doc_ends[None, :])
    doc_first = jnp.sum(jnp.where(inside, doc_starts[None, :], 0), axis=1)
    lower = jnp.maximum(doc_first, position - WINDOW + 1)
    low = lower - (position // STRETCH * STRETCH - WINDOW)
    low = jnp.broadcast_to(low[:, None], (tokens, 128))

    step = jnp.arange(chips, dtype=jnp.int32)
    chip = seq_index // CORES
    owner = (chip - step + chips) % chips * CORES
    order = jnp.concatenate([owner + core, owner + 1 - core])
    whole_heads = order.shape[0] == heads

    def attend(part, context):
        heads_order = order if whole_heads else jnp.arange(heads, dtype=jnp.int32)
        pair = attention(part, heads_order, queries, query_tangent, context, low)
        if not whole_heads:
            pair = jnp.take(pair.reshape(half, 2, seq_size, -1), order, axis=2)
            pair = pair.reshape(half, 2 * width)
        return pair

    part = out_weight.shape[1] // CHUNKS // lax.axis_size("kv")

    def add_stage(keep, received):
        total = keep[:, :, :part].astype(jnp.float32) + received[:, :, part:]
        return total.astype(jnp.bfloat16)

    def settle(*others):
        states = [(gathering.near, gathering.far) for gathering in gathers]
        states, *others = together(states, *others)
        for gathering, (near, far) in zip(gathers, states):
            gathering.near, gathering.far = dict(near), dict(far)
        return others

    pair_second = attend(1, stacked)
    pair_second, prior = settle(pair_second, prior)
    gathers[0].exchange()
    gathers[0].farther()
    gathers[2].ahead()
    pair_first = attend(0, jnp.concatenate([prior, stacked[:half]], axis=0))

    pairs, send, sums = (pair_first, pair_second), (), ()
    kept, received, last, outputs = [], [], [], ()
    for chunk in range(CHUNKS):
        pairs, whole, send, sums = settle(pairs, whole, send, sums)
        gathers[chunk].exchange()
        if chunk + 1 < CHUNKS:
            gathers[chunk + 1].exchange()
            gathers[chunk + 1].behind()
            gathers[chunk + 1].farther()
        if chunk + 3 < CHUNKS:
            gathers[chunk + 3].ahead()
        send, keep = project(
            SCHEDULED_GFLOPS[chunk], pairs, gathers[chunk].pieces(chunk, whole)
        )
        kept.append(keep)
        if chunk >= 2:
            last[chunk - 2], send = together(last[chunk - 2], send)
        received.append(across(send, 0))
        if chunk:
            received[chunk - 1], send = together(received[chunk - 1], send)
            sums = add_stage(kept[chunk - 1], received[chunk - 1])
            last.append(across(sums, 1))
            if chunk >= 2:
                outputs = finish(
                    chunk - 2, outputs, kept[chunk - 2], received[chunk - 2], last[chunk - 2]
                )
    last.append(across(add_stage(kept[-1], received[-1]), 1))
    for chunk in range(max(CHUNKS - 2, 0), CHUNKS):
        outputs = finish(chunk, outputs, kept[chunk], received[chunk], last[chunk])
    return tuple(outputs)


def solution(mesh):
    in_specs = (
        P("seq", "kv"),
        P("seq", "kv"),
        P("seq", None, "kv"),
        P("seq", None, "kv"),
        P(),
        P(("kv", "seq"), None),
        P(("kv", "seq"), None),
    )
    out_specs = (P("seq", "kv"), P("seq", "kv"))
    return jax.shard_map(body, mesh=mesh, in_specs=in_specs, out_specs=out_specs, check_vma=False)
```

```python
import functools
import math

import jax
import jax.numpy as jnp
from jax import lax
from jax.experimental import pallas as pl
from jax.experimental.pallas import tpu as pltpu
from jax.sharding import PartitionSpec as P

STRETCH = 32
WINDOW = 224
CHUNKS = 4
SCHEDULED_GFLOPS = (3, 2, 1.5, 0.01)
TILE = 128
CORES = 2

masked_score = -1e30
vmem_bytes = 12 * 1024 * 1024


def arrange_kernel(owner_ref, tangent_ref, value_ref, whole_ref, *chunk_refs):
    owners = owner_ref.shape[0]
    columns = tangent_ref.shape[1] // owners
    part = columns // len(chunk_refs)
    for chunk, chunk_ref in enumerate(chunk_refs):
        for place in range(owners):
            start = pl.multiple_of(owner_ref[place] * columns + chunk * part, part)
            to = slice(place * part, (place + 1) * part)
            for mat, ref in enumerate((tangent_ref, value_ref)):
                block = ref[:, pl.ds(start, part)]
                whole_ref[chunk, mat, :, to] = block
                chunk_ref[0, mat, :, to] = block


def arrange(owners, tangent, value):
    rows, columns = value.shape
    shapes = [
        jax.ShapeDtypeStruct((count, 2, rows, columns // CHUNKS), value.dtype)
        for count in [CHUNKS] + [1] * CHUNKS
    ]
    return pl.pallas_call(
        arrange_kernel,
        in_specs=[pl.BlockSpec(memory_space=pltpu.SMEM)]
        + [pl.BlockSpec(memory_space=pltpu.VMEM)] * 2,
        out_specs=[pl.BlockSpec(memory_space=pltpu.VMEM)] * len(shapes),
        out_shape=shapes,
        compiler_params=pltpu.CompilerParams(vmem_limit_bytes=vmem_bytes),
        name="arrange",
    )(owners, tangent, value)


def attention_kernel(heads, head_dim, offset, order_ref, q_ref, qt_ref, ctx_ref, low_ref, out_ref):
    rows = q_ref.shape[0]
    span = WINDOW + STRETCH
    width = heads * head_dim
    score_scale = 1.0 / math.sqrt(head_dim)
    to_log2 = score_scale * math.log2(math.e)
    step = pl.program_id(0)
    transposed = (((1,), (1,)), ((), ()))
    column = lax.broadcasted_iota(jnp.int32, (STRETCH, span), 1)
    row = lax.broadcasted_iota(jnp.int32, (STRETCH, span), 0)
    causal = column <= row + WINDOW
    starts = [pl.multiple_of(order_ref[h] * head_dim, head_dim) for h in range(heads)]

    def window(part):
        return pl.ds(pl.multiple_of(offset + step * rows + part * STRETCH, STRETCH), span)

    def score(part):
        here = slice(part * STRETCH, (part + 1) * STRETCH)
        keys = ctx_ref[window(part), : 2 * head_dim]
        q = jnp.concatenate([q_ref[here, pl.ds(start, head_dim)] for start in starts], axis=0)
        qt = jnp.concatenate([qt_ref[here, pl.ds(start, head_dim)] for start in starts], axis=0)
        scores = lax.dot_general(
            q, keys[:, :head_dim], transposed, preferred_element_type=jnp.float32
        )
        tangent = lax.dot_general(
            jnp.concatenate([qt, q], axis=1), keys, transposed, preferred_element_type=jnp.float32
        )
        return scores.reshape(heads, STRETCH, span), tangent.reshape(heads, STRETCH, span)

    def weigh(part, scores, tangent):
        low = low_ref[part * STRETCH : (part + 1) * STRETCH, :]
        low = jnp.concatenate([low] * (span // low.shape[1]), axis=1)
        admitted = causal & (column >= low)
        scores = jnp.where(admitted[None], scores, masked_score)
        peak = jnp.max(scores, axis=-1, keepdims=True)
        exponent = jnp.exp2((scores - peak) * to_log2)
        inverse = 1.0 / jnp.sum(exponent, axis=-1, keepdims=True)
        mean = jnp.sum(exponent * tangent, axis=-1, keepdims=True) * inverse
        prob = exponent * inverse
        prob_low = prob.astype(jnp.bfloat16).reshape(heads * STRETCH, span)
        tan_low = (prob * ((tangent - mean) * score_scale)).astype(jnp.bfloat16)
        return prob_low, tan_low.reshape(heads * STRETCH, span)

    def gather_values(part, prob_low, tan_low):
        here = slice(part * STRETCH, (part + 1) * STRETCH)
        values = ctx_ref[window(part), 2 * head_dim :]
        both = jnp.dot(prob_low, values, preferred_element_type=jnp.float32)
        more = jnp.dot(tan_low, values[:, :head_dim], preferred_element_type=jnp.float32)
        out = both[:, :head_dim].astype(jnp.bfloat16)
        out_tan = (both[:, head_dim:] + more).astype(jnp.bfloat16)
        for h in range(heads):
            of = slice(h * STRETCH, (h + 1) * STRETCH)
            out_ref[here, h * head_dim : (h + 1) * head_dim] = out[of]
            out_ref[here, width + h * head_dim : width + (h + 1) * head_dim] = out_tan[of]

    parts = rows // STRETCH
    scored, weighed = score(0), None
    for part in range(parts):
        following = score(part + 1) if part + 1 < parts else None
        if weighed is not None:
            gather_values(part - 1, *weighed)
        weighed = weigh(part, *scored)
        scored = following
    gather_values(parts - 1, *weighed)


def attention(half, order, queries, query_tangent, context, low):
    tokens, width = queries.shape[0] // 2, queries.shape[1]
    head_dim = context.shape[1] // 4
    heads = width // head_dim
    elements = tokens * heads * (WINDOW + STRETCH)
    steps = tokens // TILE
    offset = context.shape[0] - tokens - WINDOW
    return pl.pallas_call(
        functools.partial(attention_kernel, heads, head_dim, offset),
        grid=(steps,),
        in_specs=[
            pl.BlockSpec(memory_space=pltpu.SMEM),
            pl.BlockSpec((TILE, width), lambda i: (half * steps + i, 0)),
            pl.BlockSpec((TILE, width), lambda i: (half * steps + i, 0)),
            pl.BlockSpec(context.shape, lambda i: (0, 0)),
            pl.BlockSpec((TILE, low.shape[1]), lambda i: (half * steps + i, 0)),
        ],
        out_specs=pl.BlockSpec((TILE, 2 * width), lambda i: (i, 0)),
        out_shape=jax.ShapeDtypeStruct((tokens, 2 * width), jnp.bfloat16),
        compiler_params=pltpu.CompilerParams(vmem_limit_bytes=vmem_bytes),
        cost_estimate=pl.CostEstimate(
            flops=elements, bytes_accessed=tokens, transcendentals=0
        ),
        name="attention",
    )(order, queries, query_tangent, context, low)


def project_kernel(indices, first_ref, second_ref, *refs):
    *piece_refs, send_ref, keep_ref, weight_ref, sems = refs
    step, steps = pl.program_id(0), pl.num_programs(0)
    width, columns = weight_ref.shape[1:]
    rows = width // len(indices)
    near = width // 2
    part = columns // 4

    @pl.when(step == 0)
    def _():
        copies = []
        for place, (index, ref) in enumerate(zip(indices, piece_refs)):
            target = weight_ref.at[:, pl.ds(place * rows, rows), :]
            copies.append(pltpu.make_async_copy(ref.at[index], target, sems.at[place]))
            copies[-1].start()
        for copy in copies:
            copy.wait()

    def run(pair_ref):
        dot = functools.partial(jnp.dot, preferred_element_type=jnp.float32)

        def products(mine, of):
            return dot(pair_ref[:, mine], weight_ref[1, of]), dot(
                pair_ref[:, mine], weight_ref[0, of]
            ) + dot(pair_ref[:, slice(width + mine.start, width + mine.stop)], weight_ref[1, of])

        here = products(slice(0, near), slice(0, near))
        there = products(slice(near, width), slice(near, width))
        for mat in range(2):
            for place, crossed in enumerate((2, 1, 0, 3)):
                to = slice(place * part, (place + 1) * part)
                total = here[mat][:, to] + there[mat][:, crossed * part : (crossed + 1) * part]
                ref = send_ref if place < 2 else keep_ref
                at = place % 2 * part
                ref[mat, :, at : at + part] = total.astype(ref.dtype)

    @pl.when(step < steps // 2)
    def _():
        run(first_ref)

    @pl.when(step >= steps // 2)
    def _():
        run(second_ref)


def project(gflops, pairs, pieces):
    tokens, width = pairs[0].shape
    tile = min(2 * TILE, tokens)
    steps = tokens // tile
    indices = [index for index, _ in pieces]
    arrays = [array for _, array in pieces]
    columns = arrays[0].shape[3]
    block = pl.BlockSpec((2, tile, columns // 2), lambda i: (0, i, 0))
    out = jax.ShapeDtypeStruct((2, 2 * tokens, columns // 2), jnp.bfloat16)
    return pl.pallas_call(
        functools.partial(project_kernel, indices),
        grid=(2 * steps,),
        in_specs=[
            pl.BlockSpec((tile, width), lambda i: (jnp.minimum(i, steps - 1), 0)),
            pl.BlockSpec((tile, width), lambda i: (jnp.maximum(i - steps, 0), 0)),
            *[pl.BlockSpec(memory_space=pl.ANY)] * len(arrays),
        ],
        out_specs=[block, block],
        out_shape=[out, out],
        scratch_shapes=[
            pltpu.VMEM((2, width // 2, columns), jnp.bfloat16),
            pltpu.SemaphoreType.DMA((len(arrays),)),
        ],
        compiler_params=pltpu.CompilerParams(vmem_limit_bytes=vmem_bytes),
        cost_estimate=pl.CostEstimate(
            flops=int(gflops * 1e9), bytes_accessed=tokens, transcendentals=0
        ),
        name="project",
    )(*pairs, *arrays)


def finish_kernel(keep_ref, received_ref, last_ref, *refs):
    for mat, ref in enumerate(refs[-2:]):
        total = keep_ref[mat].astype(jnp.float32) + received_ref[mat] + last_ref[mat]
        ref[...] = total.astype(ref.dtype)


def finish(chunk, outputs, keep, received, last):
    _, tokens, part = last.shape
    shape = jax.ShapeDtypeStruct((tokens, part * CHUNKS), jnp.bfloat16)
    tile = tokens // 2
    return pl.pallas_call(
        finish_kernel,
        grid=(tokens // tile,),
        in_specs=[
            pl.BlockSpec((2, tile, part), lambda i: (0, i, 1)),
            pl.BlockSpec((2, tile, part), lambda i: (0, i, 0)),
            pl.BlockSpec((2, tile, part), lambda i: (0, i, 0)),
            *[pl.BlockSpec(memory_space=pl.ANY)] * len(outputs),
        ],
        out_specs=[pl.BlockSpec((tile, part), lambda i: (i, chunk))] * 2,
        out_shape=[shape, shape],
        input_output_aliases={3 + i: i for i in range(len(outputs))},
        compiler_params=pltpu.CompilerParams(vmem_limit_bytes=vmem_bytes),
        name="finish",
    )(keep, received, last, *outputs)


def across(block, stage):
    owners, places = lax.axis_size("kv"), lax.axis_size("seq")
    route = []
    for owner in range(owners):
        for place in range(places):
            flip = 1 + (place + stage) % CORES
            route.append((owner * places + place, (owner ^ flip) * places + place))
    return lax.ppermute(block, ("kv", "seq"), route)


def along(block, chips):
    size = lax.axis_size("seq")
    return lax.ppermute(block, "seq", [(i, (i + CORES * chips) % size) for i in range(size)])


def other_core(block):
    return lax.ppermute(block, "seq", [(i, i ^ 1) for i in range(lax.axis_size("seq"))])


def together(*trees):
    return lax.optimization_barrier(trees)


class Gather:
    def __init__(self, mine, chips):
        self.near, self.far = {0: mine}, {}
        self.chips = chips
        self.forward, self.backward = chips // 2, (chips - 1) // 2

    def ahead(self):
        if self.forward:
            self.near[1] = along(self.near[0], 1)

    def behind(self):
        if self.backward:
            self.near[self.chips - 1] = along(self.near[0], -1)

    def farther(self):
        for step in range(2, self.forward + 1):
            self.near[step] = along(self.near[step - 1], 1)
        for step in range(2, self.backward + 1):
            self.near[self.chips - step] = along(self.near[self.chips - step + 1], -1)

    def exchange(self, joint=True):
        steps = [step for step in sorted(self.near) if step and step not in self.far]
        if not joint:
            self.far.update({step: (0, other_core(self.near[step])) for step in steps})
        elif steps:
            blocks = [self.near[step] for step in steps]
            joined = jnp.concatenate(blocks) if len(blocks) > 1 else blocks[0]
            moved = other_core(joined)
            for index, step in enumerate(steps):
                self.far[step] = (index, moved)

    def pieces(self, chunk, whole):
        near = [(0, self.near[step]) for step in range(self.chips)]
        return near + [(chunk, whole)] + [self.far[step] for step in range(1, self.chips)]


def body(
    queries, query_tangent, key_value, key_value_tangents, doc_lengths, out_weight, weight_tangent
):
    tokens, width = queries.shape
    head_dim = key_value.shape[2]
    heads = width // head_dim
    half = tokens // 2
    seq_index = lax.axis_index("seq")
    kv_index = lax.axis_index("kv")
    seq_size = lax.axis_size("seq")
    chips = seq_size // CORES

    core = seq_index % CORES
    flips = jnp.stack([1 + core, 3 + 0 * core, 2 - core, 0 * core])
    whole, *mine = arrange((kv_index ^ flips).astype(jnp.int32), weight_tangent, out_weight)
    gathers = [Gather(block, chips) for block in mine]
    gathers[0].behind()
    gathers[0].ahead()
    gathers[1].ahead()
    whole = other_core(whole)

    key_value, key_value_tangents, _ = lax.optimization_barrier(
        (key_value, key_value_tangents, mine[0])
    )
    stacked = jnp.concatenate(
        [key_value[:, 0], key_value_tangents[:, 0], key_value[:, 1], key_value_tangents[:, 1]],
        axis=1,
    )
    prior = lax.ppermute(
        stacked[tokens - WINDOW :], "seq", [(i, i + 1) for i in range(seq_size - 1)]
    )

    doc_ends = jnp.cumsum(doc_lengths)
    doc_starts = doc_ends - doc_lengths
    position = seq_index * tokens + jnp.arange(tokens, dtype=jnp.int32)
    inside = (doc_starts[None, :] <= position[:, None]) & (position[:, None] < doc_ends[None, :])
    doc_first = jnp.sum(jnp.where(inside, doc_starts[None, :], 0), axis=1)
    lower = jnp.maximum(doc_first, position - WINDOW + 1)
    low = lower - (position // STRETCH * STRETCH - WINDOW)
    low = jnp.broadcast_to(low[:, None], (tokens, 128))

    step = jnp.arange(chips, dtype=jnp.int32)
    chip = seq_index // CORES
    owner = (chip - step + chips) % chips * CORES
    order = jnp.concatenate([owner + core, owner + 1 - core])
    whole_heads = order.shape[0] == heads

    def attend(part, context):
        heads_order = order if whole_heads else jnp.arange(heads, dtype=jnp.int32)
        pair = attention(part, heads_order, queries, query_tangent, context, low)
        if not whole_heads:
            pair = jnp.take(pair.reshape(half, 2, seq_size, -1), order, axis=2)
            pair = pair.reshape(half, 2 * width)
        return pair

    part = out_weight.shape[1] // CHUNKS // lax.axis_size("kv")

    def add_stage(keep, received):
        total = keep[:, :, :part].astype(jnp.float32) + received[:, :, part:]
        return total.astype(jnp.bfloat16)

    def settle(*others):
        states = [
            (gathering.near, {step: far[1] for step, far in gathering.far.items()})
            for gathering in gathers
        ]
        states, *others = together(states, *others)
        for gathering, (near, far) in zip(gathers, states):
            gathering.near = dict(near)
            gathering.far = {step: (gathering.far[step][0], far[step]) for step in far}
        return others

    pair_second = attend(1, stacked)
    pair_second, prior, whole = settle(pair_second, prior, whole)
    gathers[0].exchange()
    gathers[1].exchange()
    gathers[0].farther()
    gathers[2].ahead()
    pair_first = attend(0, jnp.concatenate([prior, stacked[:half]], axis=0))

    pairs, send, sums = (pair_first, pair_second), (), ()
    kept, received, last, outputs = [], [], [], ()
    for chunk in range(CHUNKS):
        pairs, whole, send, sums = settle(pairs, whole, send, sums)
        gathers[chunk].exchange(chunk < CHUNKS - 1)
        first = chunk + 1 + (chunk == 0)
        if chunk != 1 and first < CHUNKS:
            gathers[first].exchange()
        if chunk + 1 < CHUNKS:
            gathers[chunk + 1].behind()
            gathers[chunk + 1].farther()
        if chunk + 3 < CHUNKS:
            gathers[chunk + 3].ahead()
        send, keep = project(
            SCHEDULED_GFLOPS[chunk], pairs, gathers[chunk].pieces(chunk, whole)
        )
        kept.append(keep)
        if chunk >= 2:
            last[chunk - 2], send = together(last[chunk - 2], send)
        received.append(across(send, 0))
        if chunk:
            received[chunk - 1], send = together(received[chunk - 1], send)
            sums = add_stage(kept[chunk - 1], received[chunk - 1])
            last.append(across(sums, 1))
            if chunk >= 2:
                outputs = finish(
                    chunk - 2, outputs, kept[chunk - 2], received[chunk - 2], last[chunk - 2]
                )
    last.append(across(add_stage(kept[-1], received[-1]), 1))
    for chunk in range(max(CHUNKS - 2, 0), CHUNKS):
        outputs = finish(chunk, outputs, kept[chunk], received[chunk], last[chunk])
    return tuple(outputs)


def solution(mesh):
    in_specs = (
        P("seq", "kv"),
        P("seq", "kv"),
        P("seq", None, "kv"),
        P("seq", None, "kv"),
        P(),
        P(("kv", "seq"), None),
        P(("kv", "seq"), None),
    )
    out_specs = (P("seq", "kv"), P("seq", "kv"))
    return jax.shard_map(body, mesh=mesh, in_specs=in_specs, out_specs=out_specs, check_vma=False)
```

```python
import functools
import math

import jax
import jax.numpy as jnp
from jax import lax
from jax.experimental import pallas as pl
from jax.experimental.pallas import tpu as pltpu
from jax.sharding import PartitionSpec as P

STRETCH = 32
WINDOW = 224
CHUNKS = 4
SCHEDULED_GFLOPS = (3, 3, 1.5, 0.01)
TILE = 128
CORES = 2

masked_score = -1e30
vmem_bytes = 12 * 1024 * 1024


def arrange_kernel(owner_ref, tangent_ref, value_ref, whole_ref, *chunk_refs):
    owners = owner_ref.shape[0]
    columns = tangent_ref.shape[1] // owners
    part = columns // len(chunk_refs)
    for chunk, chunk_ref in enumerate(chunk_refs):
        for place in range(owners):
            start = pl.multiple_of(owner_ref[place] * columns + chunk * part, part)
            to = slice(place * part, (place + 1) * part)
            for mat, ref in enumerate((tangent_ref, value_ref)):
                block = ref[:, pl.ds(start, part)]
                whole_ref[chunk, mat, :, to] = block
                chunk_ref[0, mat, :, to] = block


def arrange(owners, tangent, value):
    rows, columns = value.shape
    shapes = [
        jax.ShapeDtypeStruct((count, 2, rows, columns // CHUNKS), value.dtype)
        for count in [CHUNKS] + [1] * CHUNKS
    ]
    return pl.pallas_call(
        arrange_kernel,
        in_specs=[pl.BlockSpec(memory_space=pltpu.SMEM)]
        + [pl.BlockSpec(memory_space=pltpu.VMEM)] * 2,
        out_specs=[pl.BlockSpec(memory_space=pltpu.VMEM)] * len(shapes),
        out_shape=shapes,
        compiler_params=pltpu.CompilerParams(vmem_limit_bytes=vmem_bytes),
        name="arrange",
    )(owners, tangent, value)


def attention_kernel(heads, head_dim, offset, order_ref, q_ref, qt_ref, ctx_ref, low_ref, out_ref):
    rows = q_ref.shape[0]
    span = WINDOW + STRETCH
    width = heads * head_dim
    score_scale = 1.0 / math.sqrt(head_dim)
    to_log2 = score_scale * math.log2(math.e)
    step = pl.program_id(0)
    transposed = (((1,), (1,)), ((), ()))
    column = lax.broadcasted_iota(jnp.int32, (STRETCH, span), 1)
    row = lax.broadcasted_iota(jnp.int32, (STRETCH, span), 0)
    causal = column <= row + WINDOW
    starts = [pl.multiple_of(order_ref[h] * head_dim, head_dim) for h in range(heads)]

    def window(part):
        return pl.ds(pl.multiple_of(offset + step * rows + part * STRETCH, STRETCH), span)

    def score(part):
        here = slice(part * STRETCH, (part + 1) * STRETCH)
        keys = ctx_ref[window(part), : 2 * head_dim]
        q = jnp.concatenate([q_ref[here, pl.ds(start, head_dim)] for start in starts], axis=0)
        qt = jnp.concatenate([qt_ref[here, pl.ds(start, head_dim)] for start in starts], axis=0)
        scores = lax.dot_general(
            q, keys[:, :head_dim], transposed, preferred_element_type=jnp.float32
        )
        tangent = lax.dot_general(
            jnp.concatenate([qt, q], axis=1), keys, transposed, preferred_element_type=jnp.float32
        )
        return scores.reshape(heads, STRETCH, span), tangent.reshape(heads, STRETCH, span)

    def weigh(part, scores, tangent):
        low = low_ref[part * STRETCH : (part + 1) * STRETCH, :]
        low = jnp.concatenate([low] * (span // low.shape[1]), axis=1)
        admitted = causal & (column >= low)
        scores = jnp.where(admitted[None], scores, masked_score)
        peak = jnp.max(scores, axis=-1, keepdims=True)
        exponent = jnp.exp2((scores - peak) * to_log2)
        inverse = 1.0 / jnp.sum(exponent, axis=-1, keepdims=True)
        mean = jnp.sum(exponent * tangent, axis=-1, keepdims=True) * inverse
        prob = exponent * inverse
        prob_low = prob.astype(jnp.bfloat16).reshape(heads * STRETCH, span)
        tan_low = (prob * ((tangent - mean) * score_scale)).astype(jnp.bfloat16)
        return prob_low, tan_low.reshape(heads * STRETCH, span)

    def gather_values(part, prob_low, tan_low):
        here = slice(part * STRETCH, (part + 1) * STRETCH)
        values = ctx_ref[window(part), 2 * head_dim :]
        both = jnp.dot(prob_low, values, preferred_element_type=jnp.float32)
        more = jnp.dot(tan_low, values[:, :head_dim], preferred_element_type=jnp.float32)
        out = both[:, :head_dim].astype(jnp.bfloat16)
        out_tan = (both[:, head_dim:] + more).astype(jnp.bfloat16)
        for h in range(heads):
            of = slice(h * STRETCH, (h + 1) * STRETCH)
            out_ref[here, h * head_dim : (h + 1) * head_dim] = out[of]
            out_ref[here, width + h * head_dim : width + (h + 1) * head_dim] = out_tan[of]

    parts = rows // STRETCH
    scored, weighed = score(0), None
    for part in range(parts):
        following = score(part + 1) if part + 1 < parts else None
        if weighed is not None:
            gather_values(part - 1, *weighed)
        weighed = weigh(part, *scored)
        scored = following
    gather_values(parts - 1, *weighed)


def attention(half, order, queries, query_tangent, context, low):
    tokens, width = queries.shape[0] // 2, queries.shape[1]
    head_dim = context.shape[1] // 4
    heads = width // head_dim
    elements = tokens * heads * (WINDOW + STRETCH)
    steps = tokens // TILE
    offset = context.shape[0] - tokens - WINDOW
    return pl.pallas_call(
        functools.partial(attention_kernel, heads, head_dim, offset),
        grid=(steps,),
        in_specs=[
            pl.BlockSpec(memory_space=pltpu.SMEM),
            pl.BlockSpec((TILE, width), lambda i: (half * steps + i, 0)),
            pl.BlockSpec((TILE, width), lambda i: (half * steps + i, 0)),
            pl.BlockSpec(context.shape, lambda i: (0, 0)),
            pl.BlockSpec((TILE, low.shape[1]), lambda i: (half * steps + i, 0)),
        ],
        out_specs=pl.BlockSpec((TILE, 2 * width), lambda i: (i, 0)),
        out_shape=jax.ShapeDtypeStruct((tokens, 2 * width), jnp.bfloat16),
        compiler_params=pltpu.CompilerParams(vmem_limit_bytes=vmem_bytes),
        cost_estimate=pl.CostEstimate(
            flops=elements, bytes_accessed=tokens, transcendentals=0
        ),
        name="attention",
    )(order, queries, query_tangent, context, low)


def project_kernel(indices, first_ref, second_ref, *refs):
    *piece_refs, send_ref, keep_ref, weight_ref, sems = refs
    step, steps = pl.program_id(0), pl.num_programs(0)
    width, columns = weight_ref.shape[1:]
    rows = width // len(indices)
    near = width // 2
    part = columns // 4

    @pl.when(step == 0)
    def _():
        copies = []
        for place, (index, ref) in enumerate(zip(indices, piece_refs)):
            target = weight_ref.at[:, pl.ds(place * rows, rows), :]
            copies.append(pltpu.make_async_copy(ref.at[index], target, sems.at[place]))
            copies[-1].start()
        for copy in copies:
            copy.wait()

    def run(pair_ref):
        dot = functools.partial(jnp.dot, preferred_element_type=jnp.float32)

        def products(mine, of):
            return dot(pair_ref[:, mine], weight_ref[1, of]), dot(
                pair_ref[:, mine], weight_ref[0, of]
            ) + dot(pair_ref[:, slice(width + mine.start, width + mine.stop)], weight_ref[1, of])

        here = products(slice(0, near), slice(0, near))
        there = products(slice(near, width), slice(near, width))
        for mat in range(2):
            for place, crossed in enumerate((2, 1, 0, 3)):
                to = slice(place * part, (place + 1) * part)
                total = here[mat][:, to] + there[mat][:, crossed * part : (crossed + 1) * part]
                ref = send_ref if place < 2 else keep_ref
                at = place % 2 * part
                ref[mat, :, at : at + part] = total.astype(ref.dtype)

    @pl.when(step < steps // 2)
    def _():
        run(first_ref)

    @pl.when(step >= steps // 2)
    def _():
        run(second_ref)


def project(gflops, pairs, pieces):
    tokens, width = pairs[0].shape
    tile = min(2 * TILE, tokens)
    steps = tokens // tile
    indices = [index for index, _ in pieces]
    arrays = [array for _, array in pieces]
    columns = arrays[0].shape[3]
    block = pl.BlockSpec((2, tile, columns // 2), lambda i: (0, i, 0))
    out = jax.ShapeDtypeStruct((2, 2 * tokens, columns // 2), jnp.bfloat16)
    return pl.pallas_call(
        functools.partial(project_kernel, indices),
        grid=(2 * steps,),
        in_specs=[
            pl.BlockSpec((tile, width), lambda i: (jnp.minimum(i, steps - 1), 0)),
            pl.BlockSpec((tile, width), lambda i: (jnp.maximum(i - steps, 0), 0)),
            *[pl.BlockSpec(memory_space=pl.ANY)] * len(arrays),
        ],
        out_specs=[block, block],
        out_shape=[out, out],
        scratch_shapes=[
            pltpu.VMEM((2, width // 2, columns), jnp.bfloat16),
            pltpu.SemaphoreType.DMA((len(arrays),)),
        ],
        compiler_params=pltpu.CompilerParams(vmem_limit_bytes=vmem_bytes),
        cost_estimate=pl.CostEstimate(
            flops=int(gflops * 1e9), bytes_accessed=tokens, transcendentals=0
        ),
        name="project",
    )(*pairs, *arrays)


def finish_kernel(keep_ref, received_ref, last_ref, *refs):
    for mat, ref in enumerate(refs[-2:]):
        total = keep_ref[mat].astype(jnp.float32) + received_ref[mat] + last_ref[mat]
        ref[...] = total.astype(ref.dtype)


def finish(chunk, outputs, keep, received, last):
    _, tokens, part = last.shape
    shape = jax.ShapeDtypeStruct((tokens, part * CHUNKS), jnp.bfloat16)
    tile = tokens // 2
    return pl.pallas_call(
        finish_kernel,
        grid=(tokens // tile,),
        in_specs=[
            pl.BlockSpec((2, tile, part), lambda i: (0, i, 1)),
            pl.BlockSpec((2, tile, part), lambda i: (0, i, 0)),
            pl.BlockSpec((2, tile, part), lambda i: (0, i, 0)),
            *[pl.BlockSpec(memory_space=pl.ANY)] * len(outputs),
        ],
        out_specs=[pl.BlockSpec((tile, part), lambda i: (i, chunk))] * 2,
        out_shape=[shape, shape],
        input_output_aliases={3 + i: i for i in range(len(outputs))},
        compiler_params=pltpu.CompilerParams(vmem_limit_bytes=vmem_bytes),
        name="finish",
    )(keep, received, last, *outputs)


def across(block, stage):
    owners, places = lax.axis_size("kv"), lax.axis_size("seq")
    route = []
    for owner in range(owners):
        for place in range(places):
            flip = 1 + (place + stage) % CORES
            route.append((owner * places + place, (owner ^ flip) * places + place))
    return lax.ppermute(block, ("kv", "seq"), route)


def along(block, chips):
    size = lax.axis_size("seq")
    return lax.ppermute(block, "seq", [(i, (i + CORES * chips) % size) for i in range(size)])


def other_core(block):
    return lax.ppermute(block, "seq", [(i, i ^ 1) for i in range(lax.axis_size("seq"))])


def together(*trees):
    return lax.optimization_barrier(trees)


class Gather:
    def __init__(self, mine, chips):
        self.near, self.far = {0: mine}, {}
        self.chips = chips
        self.forward, self.backward = chips // 2, (chips - 1) // 2

    def ahead(self):
        if self.forward:
            self.near[1] = along(self.near[0], 1)

    def behind(self):
        if self.backward:
            self.near[-1] = along(self.near[0], -1)

    def farther(self):
        for step in range(2, self.forward + 1):
            self.near[step] = along(self.near[step - 1], 1)
        for step in range(2, self.backward + 1):
            self.near[-step] = along(self.near[1 - step], -1)

    def exchange(self, joint=True):
        steps = [step for step in sorted(self.near) if step and step not in self.far]
        if not joint:
            self.far.update({step: (0, other_core(self.near[step])) for step in steps})
        elif steps:
            blocks = [self.near[step] for step in steps]
            joined = jnp.concatenate(blocks) if len(blocks) > 1 else blocks[0]
            moved = other_core(joined)
            for index, step in enumerate(steps):
                self.far[step] = (index, moved)

    def pieces(self, chunk, whole):
        steps = [*range(1, self.forward + 1), *range(-self.backward, 0)]
        near = [(0, self.near[step]) for step in [0, *steps]]
        return near + [(chunk, whole)] + [self.far[step] for step in steps]


def body(
    queries, query_tangent, key_value, key_value_tangents, doc_lengths, out_weight, weight_tangent
):
    tokens, width = queries.shape
    head_dim = key_value.shape[2]
    heads = width // head_dim
    half = tokens // 2
    seq_index = lax.axis_index("seq")
    kv_index = lax.axis_index("kv")
    seq_size = lax.axis_size("seq")
    chips = seq_size // CORES

    core = seq_index % CORES
    flips = jnp.stack([1 + core, 3 + 0 * core, 2 - core, 0 * core])
    whole, *mine = arrange((kv_index ^ flips).astype(jnp.int32), weight_tangent, out_weight)
    gathers = [Gather(block, chips) for block in mine]
    gathers[0].behind()
    gathers[0].ahead()
    gathers[1].ahead()
    whole = other_core(whole)

    key_value, key_value_tangents, _ = lax.optimization_barrier(
        (key_value, key_value_tangents, mine[0])
    )
    stacked = jnp.concatenate(
        [key_value[:, 0], key_value_tangents[:, 0], key_value[:, 1], key_value_tangents[:, 1]],
        axis=1,
    )
    prior = lax.ppermute(
        stacked[tokens - WINDOW :], "seq", [(i, i + 1) for i in range(seq_size - 1)]
    )

    doc_ends = jnp.cumsum(doc_lengths)
    doc_starts = doc_ends - doc_lengths
    position = seq_index * tokens + jnp.arange(tokens, dtype=jnp.int32)
    inside = (doc_starts[None, :] <= position[:, None]) & (position[:, None] < doc_ends[None, :])
    doc_first = jnp.sum(jnp.where(inside, doc_starts[None, :], 0), axis=1)
    lower = jnp.maximum(doc_first, position - WINDOW + 1)
    low = lower - (position // STRETCH * STRETCH - WINDOW)
    low = jnp.broadcast_to(low[:, None], (tokens, 128))

    step = jnp.arange(chips, dtype=jnp.int32)
    chip = seq_index // CORES
    owner = (chip - step + chips) % chips * CORES
    order = jnp.concatenate([owner + core, owner + 1 - core])
    whole_heads = order.shape[0] == heads

    def attend(part, context):
        heads_order = order if whole_heads else jnp.arange(heads, dtype=jnp.int32)
        pair = attention(part, heads_order, queries, query_tangent, context, low)
        if not whole_heads:
            pair = jnp.take(pair.reshape(half, 2, seq_size, -1), order, axis=2)
            pair = pair.reshape(half, 2 * width)
        return pair

    part = out_weight.shape[1] // CHUNKS // lax.axis_size("kv")

    def add_stage(keep, received):
        total = keep[:, :, :part].astype(jnp.float32) + received[:, :, part:]
        return total.astype(jnp.bfloat16)

    def settle(*others):
        states = [
            (gathering.near, {step: far[1] for step, far in gathering.far.items()})
            for gathering in gathers
        ]
        states, *others = together(states, *others)
        for gathering, (near, far) in zip(gathers, states):
            gathering.near = dict(near)
            gathering.far = {step: (gathering.far[step][0], far[step]) for step in far}
        return others

    pair_second = attend(1, stacked)
    pair_second, prior, whole = settle(pair_second, prior, whole)
    gathers[0].exchange(False)
    gathers[1].exchange()
    gathers[0].farther()
    gathers[2].ahead()
    pair_first = attend(0, jnp.concatenate([prior, stacked[:half]], axis=0))

    pairs, send, sums = (pair_first, pair_second), (), ()
    kept, received, last, outputs = [], [], [], ()
    for chunk in range(CHUNKS):
        pairs, whole, send, sums = settle(pairs, whole, send, sums)
        gathers[chunk].exchange(chunk < CHUNKS - 1)
        first = chunk + 1 + (chunk == 0)
        if chunk != 1 and first < CHUNKS:
            gathers[first].exchange()
        if chunk + 1 < CHUNKS:
            gathers[chunk + 1].behind()
            gathers[chunk + 1].farther()
        if 0 < chunk < CHUNKS - 2:
            gathers[chunk + 2].ahead()
        send, keep = project(
            SCHEDULED_GFLOPS[chunk], pairs, gathers[chunk].pieces(chunk, whole)
        )
        kept.append(keep)
        if chunk >= 2:
            last[chunk - 2], send = together(last[chunk - 2], send)
        received.append(across(send, 0))
        if chunk:
            received[chunk - 1], send = together(received[chunk - 1], send)
            sums = add_stage(kept[chunk - 1], received[chunk - 1])
            last.append(across(sums, 1))
            if chunk >= 2:
                outputs = finish(
                    chunk - 2, outputs, kept[chunk - 2], received[chunk - 2], last[chunk - 2]
                )
    last.append(across(add_stage(kept[-1], received[-1]), 1))
    for chunk in range(max(CHUNKS - 2, 0), CHUNKS):
        outputs = finish(chunk, outputs, kept[chunk], received[chunk], last[chunk])
    return tuple(outputs)


def solution(mesh):
    in_specs = (
        P("seq", "kv"),
        P("seq", "kv"),
        P("seq", None, "kv"),
        P("seq", None, "kv"),
        P(),
        P(("kv", "seq"), None),
        P(("kv", "seq"), None),
    )
    out_specs = (P("seq", "kv"), P("seq", "kv"))
    return jax.shard_map(body, mesh=mesh, in_specs=in_specs, out_specs=out_specs, check_vma=False)
```

```python
import functools
import math

import jax
import jax.numpy as jnp
from jax import lax
from jax.experimental import pallas as pl
from jax.experimental.pallas import tpu as pltpu
from jax.sharding import PartitionSpec as P

STRETCH = 32
WINDOW = 224
CHUNKS = 4
SCHEDULED_GFLOPS = (3, 3, 1.5, 0.01)
TILE = 128
CORES = 2

masked_score = -1e30
vmem_bytes = 12 * 1024 * 1024


def arrange_kernel(owner_ref, tangent_hbm, value_hbm, whole_ref, *refs):
    *chunk_refs, tangent_ref, value_ref, sems = refs
    sources = ((tangent_hbm, tangent_ref), (value_hbm, value_ref))
    copies = [
        pltpu.make_async_copy(source, target, sems.at[index])
        for index, (source, target) in enumerate(sources)
    ]
    for copy in copies:
        copy.start()
    for copy in copies:
        copy.wait()
    owners = owner_ref.shape[0]
    columns = tangent_ref.shape[1] // owners
    part = columns // len(chunk_refs)
    for chunk, chunk_ref in enumerate(chunk_refs):
        for place in range(owners):
            start = pl.multiple_of(owner_ref[place] * columns + chunk * part, part)
            to = slice(place * part, (place + 1) * part)
            for mat, ref in enumerate((tangent_ref, value_ref)):
                block = ref[:, pl.ds(start, part)]
                whole_ref[chunk, mat, :, to] = block
                chunk_ref[0, mat, :, to] = block


def arrange(owners, tangent, value):
    rows, columns = value.shape
    shapes = [
        jax.ShapeDtypeStruct((count, 2, rows, columns // CHUNKS), value.dtype)
        for count in [CHUNKS] + [1] * CHUNKS
    ]
    return pl.pallas_call(
        arrange_kernel,
        in_specs=[pl.BlockSpec(memory_space=pltpu.SMEM)]
        + [pl.BlockSpec(memory_space=pltpu.HBM)] * 2,
        out_specs=[pl.BlockSpec(memory_space=pltpu.VMEM)] * len(shapes),
        out_shape=shapes,
        scratch_shapes=[pltpu.VMEM(value.shape, value.dtype)] * 2
        + [pltpu.SemaphoreType.DMA((2,))],
        compiler_params=pltpu.CompilerParams(vmem_limit_bytes=vmem_bytes),
        name="arrange",
    )(owners, tangent, value)


def attention_kernel(heads, head_dim, offset, order_ref, q_ref, qt_ref, ctx_ref, low_ref, out_ref):
    rows = q_ref.shape[0]
    span = WINDOW + STRETCH
    width = heads * head_dim
    score_scale = 1.0 / math.sqrt(head_dim)
    to_log2 = score_scale * math.log2(math.e)
    step = pl.program_id(0)
    transposed = (((1,), (1,)), ((), ()))
    column = lax.broadcasted_iota(jnp.int32, (STRETCH, span), 1)
    row = lax.broadcasted_iota(jnp.int32, (STRETCH, span), 0)
    causal = column <= row + WINDOW
    starts = [pl.multiple_of(order_ref[h] * head_dim, head_dim) for h in range(heads)]

    def window(part):
        return pl.ds(pl.multiple_of(offset + step * rows + part * STRETCH, STRETCH), span)

    def score(part):
        here = slice(part * STRETCH, (part + 1) * STRETCH)
        keys = ctx_ref[window(part), : 2 * head_dim]
        q = jnp.concatenate([q_ref[here, pl.ds(start, head_dim)] for start in starts], axis=0)
        qt = jnp.concatenate([qt_ref[here, pl.ds(start, head_dim)] for start in starts], axis=0)
        scores = lax.dot_general(
            q, keys[:, :head_dim], transposed, preferred_element_type=jnp.float32
        )
        tangent = lax.dot_general(
            jnp.concatenate([qt, q], axis=1), keys, transposed, preferred_element_type=jnp.float32
        )
        return scores.reshape(heads, STRETCH, span), tangent.reshape(heads, STRETCH, span)

    def weigh(part, scores, tangent):
        low = low_ref[part * STRETCH : (part + 1) * STRETCH, :]
        low = jnp.concatenate([low] * (span // low.shape[1]), axis=1)
        admitted = causal & (column >= low)
        scores = jnp.where(admitted[None], scores, masked_score)
        peak = jnp.max(scores, axis=-1, keepdims=True)
        exponent = jnp.exp2((scores - peak) * to_log2)
        inverse = 1.0 / jnp.sum(exponent, axis=-1, keepdims=True)
        mean = jnp.sum(exponent * tangent, axis=-1, keepdims=True) * inverse
        prob = exponent * inverse
        prob_low = prob.astype(jnp.bfloat16).reshape(heads * STRETCH, span)
        tan_low = (prob * ((tangent - mean) * score_scale)).astype(jnp.bfloat16)
        return prob_low, tan_low.reshape(heads * STRETCH, span)

    def gather_values(part, prob_low, tan_low):
        here = slice(part * STRETCH, (part + 1) * STRETCH)
        values = ctx_ref[window(part), 2 * head_dim :]
        both = jnp.dot(prob_low, values, preferred_element_type=jnp.float32)
        more = jnp.dot(tan_low, values[:, :head_dim], preferred_element_type=jnp.float32)
        out = both[:, :head_dim].astype(jnp.bfloat16)
        out_tan = (both[:, head_dim:] + more).astype(jnp.bfloat16)
        for h in range(heads):
            of = slice(h * STRETCH, (h + 1) * STRETCH)
            out_ref[here, h * head_dim : (h + 1) * head_dim] = out[of]
            out_ref[here, width + h * head_dim : width + (h + 1) * head_dim] = out_tan[of]

    parts = rows // STRETCH
    scored, weighed = score(0), None
    for part in range(parts):
        following = score(part + 1) if part + 1 < parts else None
        if weighed is not None:
            gather_values(part - 1, *weighed)
        weighed = weigh(part, *scored)
        scored = following
    gather_values(parts - 1, *weighed)


def attention(half, order, queries, query_tangent, context, low):
    tokens, width = queries.shape[0] // 2, queries.shape[1]
    head_dim = context.shape[1] // 4
    heads = width // head_dim
    elements = tokens * heads * (WINDOW + STRETCH)
    steps = tokens // TILE
    offset = context.shape[0] - tokens - WINDOW
    return pl.pallas_call(
        functools.partial(attention_kernel, heads, head_dim, offset),
        grid=(steps,),
        in_specs=[
            pl.BlockSpec(memory_space=pltpu.SMEM),
            pl.BlockSpec((TILE, width), lambda i: (half * steps + i, 0)),
            pl.BlockSpec((TILE, width), lambda i: (half * steps + i, 0)),
            pl.BlockSpec(context.shape, lambda i: (0, 0)),
            pl.BlockSpec((TILE, low.shape[1]), lambda i: (half * steps + i, 0)),
        ],
        out_specs=pl.BlockSpec((TILE, 2 * width), lambda i: (i, 0)),
        out_shape=jax.ShapeDtypeStruct((tokens, 2 * width), jnp.bfloat16),
        compiler_params=pltpu.CompilerParams(vmem_limit_bytes=vmem_bytes),
        cost_estimate=pl.CostEstimate(
            flops=elements, bytes_accessed=tokens, transcendentals=0
        ),
        name="attention",
    )(order, queries, query_tangent, context, low)


def project_kernel(indices, first_ref, second_ref, *refs):
    *piece_refs, send_ref, keep_ref, weight_ref, sems = refs
    step, steps = pl.program_id(0), pl.num_programs(0)
    width, columns = weight_ref.shape[1:]
    rows = width // len(indices)
    near = width // 2
    part = columns // 4

    @pl.when(step == 0)
    def _():
        copies = []
        for place, (index, ref) in enumerate(zip(indices, piece_refs)):
            target = weight_ref.at[:, pl.ds(place * rows, rows), :]
            copies.append(pltpu.make_async_copy(ref.at[index], target, sems.at[place]))
            copies[-1].start()
        for copy in copies:
            copy.wait()

    def run(pair_ref):
        dot = functools.partial(jnp.dot, preferred_element_type=jnp.float32)

        def products(mine, of):
            return dot(pair_ref[:, mine], weight_ref[1, of]), dot(
                pair_ref[:, mine], weight_ref[0, of]
            ) + dot(pair_ref[:, slice(width + mine.start, width + mine.stop)], weight_ref[1, of])

        here = products(slice(0, near), slice(0, near))
        there = products(slice(near, width), slice(near, width))
        for mat in range(2):
            for place, crossed in enumerate((2, 1, 0, 3)):
                to = slice(place * part, (place + 1) * part)
                total = here[mat][:, to] + there[mat][:, crossed * part : (crossed + 1) * part]
                ref = send_ref if place < 2 else keep_ref
                at = place % 2 * part
                ref[mat, :, at : at + part] = total.astype(ref.dtype)

    @pl.when(step < steps // 2)
    def _():
        run(first_ref)

    @pl.when(step >= steps // 2)
    def _():
        run(second_ref)


def project(gflops, pairs, pieces):
    tokens, width = pairs[0].shape
    tile = min(2 * TILE, tokens)
    steps = tokens // tile
    indices = [index for index, _ in pieces]
    arrays = [array for _, array in pieces]
    columns = arrays[0].shape[3]
    block = pl.BlockSpec((2, tile, columns // 2), lambda i: (0, i, 0))
    out = jax.ShapeDtypeStruct((2, 2 * tokens, columns // 2), jnp.bfloat16)
    return pl.pallas_call(
        functools.partial(project_kernel, indices),
        grid=(2 * steps,),
        in_specs=[
            pl.BlockSpec((tile, width), lambda i: (jnp.minimum(i, steps - 1), 0)),
            pl.BlockSpec((tile, width), lambda i: (jnp.maximum(i - steps, 0), 0)),
            *[pl.BlockSpec(memory_space=pl.ANY)] * len(arrays),
        ],
        out_specs=[block, block],
        out_shape=[out, out],
        scratch_shapes=[
            pltpu.VMEM((2, width // 2, columns), jnp.bfloat16),
            pltpu.SemaphoreType.DMA((len(arrays),)),
        ],
        compiler_params=pltpu.CompilerParams(vmem_limit_bytes=vmem_bytes),
        cost_estimate=pl.CostEstimate(
            flops=int(gflops * 1e9), bytes_accessed=tokens, transcendentals=0
        ),
        name="project",
    )(*pairs, *arrays)


def finish_kernel(keep_ref, received_ref, last_ref, *refs):
    for mat, ref in enumerate(refs[-2:]):
        total = keep_ref[mat].astype(jnp.float32) + received_ref[mat] + last_ref[mat]
        ref[...] = total.astype(ref.dtype)


def finish(chunk, outputs, keep, received, last):
    _, tokens, part = last.shape
    shape = jax.ShapeDtypeStruct((tokens, part * CHUNKS), jnp.bfloat16)
    tile = tokens // 2
    return pl.pallas_call(
        finish_kernel,
        grid=(tokens // tile,),
        in_specs=[
            pl.BlockSpec((2, tile, part), lambda i: (0, i, 1)),
            pl.BlockSpec((2, tile, part), lambda i: (0, i, 0)),
            pl.BlockSpec((2, tile, part), lambda i: (0, i, 0)),
            *[pl.BlockSpec(memory_space=pl.ANY)] * len(outputs),
        ],
        out_specs=[pl.BlockSpec((tile, part), lambda i: (i, chunk))] * 2,
        out_shape=[shape, shape],
        input_output_aliases={3 + i: i for i in range(len(outputs))},
        compiler_params=pltpu.CompilerParams(vmem_limit_bytes=vmem_bytes),
        name="finish",
    )(keep, received, last, *outputs)


def across(block, stage):
    owners, places = lax.axis_size("kv"), lax.axis_size("seq")
    route = []
    for owner in range(owners):
        for place in range(places):
            flip = 1 + (place + stage) % CORES
            route.append((owner * places + place, (owner ^ flip) * places + place))
    return lax.ppermute(block, ("kv", "seq"), route)


def along(block, chips):
    size = lax.axis_size("seq")
    return lax.ppermute(block, "seq", [(i, (i + CORES * chips) % size) for i in range(size)])


def other_core(block):
    return lax.ppermute(block, "seq", [(i, i ^ 1) for i in range(lax.axis_size("seq"))])


def together(*trees):
    return lax.optimization_barrier(trees)


class Gather:
    def __init__(self, mine, chips):
        self.near, self.far = {0: mine}, {}
        self.chips = chips
        self.forward, self.backward = chips // 2, (chips - 1) // 2

    def ahead(self):
        if self.forward:
            self.near[1] = along(self.near[0], 1)

    def behind(self):
        if self.backward:
            self.near[-1] = along(self.near[0], -1)

    def farther_ahead(self):
        for step in range(2, self.forward + 1):
            self.near[step] = along(self.near[step - 1], 1)

    def farther_behind(self):
        for step in range(2, self.backward + 1):
            self.near[-step] = along(self.near[1 - step], -1)

    def exchange(self, joint=True):
        steps = [step for step in sorted(self.near) if step and step not in self.far]
        if not joint:
            self.far.update({step: (0, other_core(self.near[step])) for step in steps})
        elif steps:
            blocks = [self.near[step] for step in steps]
            joined = jnp.concatenate(blocks) if len(blocks) > 1 else blocks[0]
            moved = other_core(joined)
            for index, step in enumerate(steps):
                self.far[step] = (index, moved)

    def pieces(self, chunk, whole):
        steps = [*range(1, self.forward + 1), *range(-self.backward, 0)]
        near = [(0, self.near[step]) for step in [0, *steps]]
        return near + [(chunk, whole)] + [self.far[step] for step in steps]


def body(
    queries, query_tangent, key_value, key_value_tangents, doc_lengths, out_weight, weight_tangent
):
    tokens, width = queries.shape
    head_dim = key_value.shape[2]
    heads = width // head_dim
    half = tokens // 2
    seq_index = lax.axis_index("seq")
    kv_index = lax.axis_index("kv")
    seq_size = lax.axis_size("seq")
    chips = seq_size // CORES

    core = seq_index % CORES
    flips = jnp.stack([1 + core, 3 + 0 * core, 2 - core, 0 * core])
    whole, *mine = arrange((kv_index ^ flips).astype(jnp.int32), weight_tangent, out_weight)
    gathers = [Gather(block, chips) for block in mine]
    gathers[0].behind()
    gathers[0].ahead()
    gathers[1].ahead()
    whole = other_core(whole)

    key_value, key_value_tangents, _ = lax.optimization_barrier(
        (key_value, key_value_tangents, mine[0])
    )
    stacked = jnp.concatenate(
        [key_value[:, 0], key_value_tangents[:, 0], key_value[:, 1], key_value_tangents[:, 1]],
        axis=1,
    )
    prior = lax.ppermute(
        stacked[tokens - WINDOW :], "seq", [(i, i + 1) for i in range(seq_size - 1)]
    )

    doc_ends = jnp.cumsum(doc_lengths)
    doc_starts = doc_ends - doc_lengths
    position = seq_index * tokens + jnp.arange(tokens, dtype=jnp.int32)
    inside = (doc_starts[None, :] <= position[:, None]) & (position[:, None] < doc_ends[None, :])
    doc_first = jnp.sum(jnp.where(inside, doc_starts[None, :], 0), axis=1)
    lower = jnp.maximum(doc_first, position - WINDOW + 1)
    low = lower - (position // STRETCH * STRETCH - WINDOW)
    low = jnp.broadcast_to(low[:, None], (tokens, 128))

    step = jnp.arange(chips, dtype=jnp.int32)
    chip = seq_index // CORES
    owner = (chip - step + chips) % chips * CORES
    order = jnp.concatenate([owner + core, owner + 1 - core])
    whole_heads = order.shape[0] == heads

    def attend(part, context):
        heads_order = order if whole_heads else jnp.arange(heads, dtype=jnp.int32)
        pair = attention(part, heads_order, queries, query_tangent, context, low)
        if not whole_heads:
            pair = jnp.take(pair.reshape(half, 2, seq_size, -1), order, axis=2)
            pair = pair.reshape(half, 2 * width)
        return pair

    part = out_weight.shape[1] // CHUNKS // lax.axis_size("kv")

    def add_stage(keep, received):
        total = keep[:, :, :part].astype(jnp.float32) + received[:, :, part:]
        return total.astype(jnp.bfloat16)

    def settle(*others):
        states = [
            (gathering.near, {step: far[1] for step, far in gathering.far.items()})
            for gathering in gathers
        ]
        states, *others = together(states, *others)
        for gathering, (near, far) in zip(gathers, states):
            gathering.near = dict(near)
            gathering.far = {step: (gathering.far[step][0], far[step]) for step in far}
        return others

    pair_second = attend(1, stacked)
    pair_second, prior, whole = settle(pair_second, prior, whole)
    gathers[0].exchange(False)
    gathers[1].exchange()
    gathers[0].farther_ahead()
    gathers[0].farther_behind()
    gathers[2].ahead()
    pair_first = attend(0, jnp.concatenate([prior, stacked[:half]], axis=0))

    pairs, send, sums = (pair_first, pair_second), (), ()
    kept, received, last, outputs = [], [], [], ()
    for chunk in range(CHUNKS):
        pairs, whole, send, sums = settle(pairs, whole, send, sums)
        gathers[chunk].exchange(chunk < CHUNKS - 1)
        first = chunk + 1 + (chunk == 0)
        if chunk != 1 and first < CHUNKS:
            gathers[first].exchange()
        if chunk + 1 < CHUNKS:
            if chunk + 2 < CHUNKS:
                gathers[chunk + 1].behind()
                gathers[chunk + 1].farther_behind()
            gathers[chunk + 1].farther_ahead()
        if 0 < chunk < CHUNKS - 2:
            gathers[chunk + 2].ahead()
        send, keep = project(
            SCHEDULED_GFLOPS[chunk], pairs, gathers[chunk].pieces(chunk, whole)
        )
        kept.append(keep)
        if chunk == CHUNKS - 2:
            final = gathers[chunk + 1]
            final.near[0], send = together(final.near[0], send)
            final.behind()
            final.farther_behind()
        if chunk >= 2:
            last[chunk - 2], send = together(last[chunk - 2], send)
        received.append(across(send, 0))
        if chunk:
            received[chunk - 1], send = together(received[chunk - 1], send)
            sums = add_stage(kept[chunk - 1], received[chunk - 1])
            last.append(across(sums, 1))
            if chunk >= 2:
                outputs = finish(
                    chunk - 2, outputs, kept[chunk - 2], received[chunk - 2], last[chunk - 2]
                )
    last.append(across(add_stage(kept[-1], received[-1]), 1))
    for chunk in range(max(CHUNKS - 2, 0), CHUNKS):
        outputs = finish(chunk, outputs, kept[chunk], received[chunk], last[chunk])
    return tuple(outputs)


def solution(mesh):
    in_specs = (
        P("seq", "kv"),
        P("seq", "kv"),
        P("seq", None, "kv"),
        P("seq", None, "kv"),
        P(),
        P(("kv", "seq"), None),
        P(("kv", "seq"), None),
    )
    out_specs = (P("seq", "kv"), P("seq", "kv"))
    return jax.shard_map(body, mesh=mesh, in_specs=in_specs, out_specs=out_specs, check_vma=False)
```

```python
import functools
import math

import jax
import jax.numpy as jnp
from jax import lax
from jax.experimental import pallas as pl
from jax.experimental.pallas import tpu as pltpu
from jax.sharding import PartitionSpec as P

STRETCH = 32
WINDOW = 224
CHUNKS = 4
SCHEDULED_GFLOPS = (3, 3, 1.5, 0.01)
TILE = 128
CORES = 2

masked_score = -1e30
vmem_bytes = 12 * 1024 * 1024


def arrange_kernel(owner_ref, tangent_hbm, value_hbm, whole_ref, *refs):
    *chunk_refs, tangent_ref, value_ref, sems = refs
    sources = ((tangent_hbm, tangent_ref), (value_hbm, value_ref))
    copies = [
        pltpu.make_async_copy(source, target, sems.at[index])
        for index, (source, target) in enumerate(sources)
    ]
    for copy in copies:
        copy.start()
    for copy in copies:
        copy.wait()
    owners = owner_ref.shape[0]
    columns = tangent_ref.shape[1] // owners
    part = columns // len(chunk_refs)
    for chunk, chunk_ref in enumerate(chunk_refs):
        for place in range(owners):
            start = pl.multiple_of(owner_ref[place] * columns + chunk * part, part)
            to = slice(place * part, (place + 1) * part)
            for mat, ref in enumerate((tangent_ref, value_ref)):
                block = ref[:, pl.ds(start, part)]
                whole_ref[chunk, mat, :, to] = block
                chunk_ref[0, mat, :, to] = block


def arrange(owners, tangent, value):
    rows, columns = value.shape
    shapes = [
        jax.ShapeDtypeStruct((count, 2, rows, columns // CHUNKS), value.dtype)
        for count in [CHUNKS] + [1] * CHUNKS
    ]
    return pl.pallas_call(
        arrange_kernel,
        in_specs=[pl.BlockSpec(memory_space=pltpu.SMEM)]
        + [pl.BlockSpec(memory_space=pltpu.HBM)] * 2,
        out_specs=[pl.BlockSpec(memory_space=pltpu.VMEM)] * len(shapes),
        out_shape=shapes,
        scratch_shapes=[pltpu.VMEM(value.shape, value.dtype)] * 2
        + [pltpu.SemaphoreType.DMA((2,))],
        compiler_params=pltpu.CompilerParams(vmem_limit_bytes=5 * vmem_bytes),
        name="arrange",
    )(owners, tangent, value)


def attention_kernel(heads, head_dim, offset, order_ref, q_ref, qt_ref, ctx_ref, low_ref, out_ref):
    rows = q_ref.shape[0]
    span = WINDOW + STRETCH
    width = heads * head_dim
    score_scale = 1.0 / math.sqrt(head_dim)
    to_log2 = score_scale * math.log2(math.e)
    step = pl.program_id(0)
    transposed = (((1,), (1,)), ((), ()))
    column = lax.broadcasted_iota(jnp.int32, (STRETCH, span), 1)
    row = lax.broadcasted_iota(jnp.int32, (STRETCH, span), 0)
    causal = column <= row + WINDOW
    starts = [pl.multiple_of(order_ref[h] * head_dim, head_dim) for h in range(heads)]

    def window(part):
        return pl.ds(pl.multiple_of(offset + step * rows + part * STRETCH, STRETCH), span)

    def score(part):
        here = slice(part * STRETCH, (part + 1) * STRETCH)
        keys = ctx_ref[window(part), : 2 * head_dim]
        q = jnp.concatenate([q_ref[here, pl.ds(start, head_dim)] for start in starts], axis=0)
        qt = jnp.concatenate([qt_ref[here, pl.ds(start, head_dim)] for start in starts], axis=0)
        scores = lax.dot_general(
            q, keys[:, :head_dim], transposed, preferred_element_type=jnp.float32
        )
        tangent = lax.dot_general(
            jnp.concatenate([qt, q], axis=1), keys, transposed, preferred_element_type=jnp.float32
        )
        return scores.reshape(heads, STRETCH, span), tangent.reshape(heads, STRETCH, span)

    def weigh(part, scores, tangent):
        low = low_ref[part * STRETCH : (part + 1) * STRETCH, :]
        low = jnp.concatenate([low] * (span // low.shape[1]), axis=1)
        admitted = causal & (column >= low)
        scores = jnp.where(admitted[None], scores, masked_score)
        peak = jnp.max(scores, axis=-1, keepdims=True)
        exponent = jnp.exp2((scores - peak) * to_log2)
        inverse = 1.0 / jnp.sum(exponent, axis=-1, keepdims=True)
        mean = jnp.sum(exponent * tangent, axis=-1, keepdims=True) * inverse
        prob = exponent * inverse
        prob_low = prob.astype(jnp.bfloat16).reshape(heads * STRETCH, span)
        tan_low = (prob * ((tangent - mean) * score_scale)).astype(jnp.bfloat16)
        return prob_low, tan_low.reshape(heads * STRETCH, span)

    def gather_values(part, prob_low, tan_low):
        here = slice(part * STRETCH, (part + 1) * STRETCH)
        values = ctx_ref[window(part), 2 * head_dim :]
        both = jnp.dot(prob_low, values, preferred_element_type=jnp.float32)
        more = jnp.dot(tan_low, values[:, :head_dim], preferred_element_type=jnp.float32)
        out = both[:, :head_dim].astype(jnp.bfloat16)
        out_tan = (both[:, head_dim:] + more).astype(jnp.bfloat16)
        for h in range(heads):
            of = slice(h * STRETCH, (h + 1) * STRETCH)
            out_ref[here, h * head_dim : (h + 1) * head_dim] = out[of]
            out_ref[here, width + h * head_dim : width + (h + 1) * head_dim] = out_tan[of]

    parts = rows // STRETCH
    scored, weighed = score(0), None
    for part in range(parts):
        following = score(part + 1) if part + 1 < parts else None
        if weighed is not None:
            gather_values(part - 1, *weighed)
        weighed = weigh(part, *scored)
        scored = following
    gather_values(parts - 1, *weighed)


def attention(half, order, queries, query_tangent, context, low):
    tokens, width = queries.shape[0] // 2, queries.shape[1]
    head_dim = context.shape[1] // 4
    heads = width // head_dim
    elements = tokens * heads * (WINDOW + STRETCH)
    steps = tokens // TILE
    offset = context.shape[0] - tokens - WINDOW
    return pl.pallas_call(
        functools.partial(attention_kernel, heads, head_dim, offset),
        grid=(steps,),
        in_specs=[
            pl.BlockSpec(memory_space=pltpu.SMEM),
            pl.BlockSpec((TILE, width), lambda i: (half * steps + i, 0)),
            pl.BlockSpec((TILE, width), lambda i: (half * steps + i, 0)),
            pl.BlockSpec(context.shape, lambda i: (0, 0)),
            pl.BlockSpec((TILE, low.shape[1]), lambda i: (half * steps + i, 0)),
        ],
        out_specs=pl.BlockSpec((TILE, 2 * width), lambda i: (i, 0)),
        out_shape=jax.ShapeDtypeStruct((tokens, 2 * width), jnp.bfloat16),
        compiler_params=pltpu.CompilerParams(vmem_limit_bytes=vmem_bytes),
        cost_estimate=pl.CostEstimate(
            flops=elements, bytes_accessed=tokens, transcendentals=0
        ),
        name="attention",
    )(order, queries, query_tangent, context, low)


def project_kernel(indices, first_ref, second_ref, *refs):
    *piece_refs, send_ref, keep_ref, weight_ref, sems = refs
    step, steps = pl.program_id(0), pl.num_programs(0)
    width, columns = weight_ref.shape[1:]
    rows = width // len(indices)
    near = width // 2
    part = columns // 4

    @pl.when(step == 0)
    def _():
        copies = []
        for place, (index, ref) in enumerate(zip(indices, piece_refs)):
            target = weight_ref.at[:, pl.ds(place * rows, rows), :]
            copies.append(pltpu.make_async_copy(ref.at[index], target, sems.at[place]))
            copies[-1].start()
        for copy in copies:
            copy.wait()

    def run(pair_ref):
        dot = functools.partial(jnp.dot, preferred_element_type=jnp.float32)

        def products(mine, of):
            return dot(pair_ref[:, mine], weight_ref[1, of]), dot(
                pair_ref[:, mine], weight_ref[0, of]
            ) + dot(pair_ref[:, slice(width + mine.start, width + mine.stop)], weight_ref[1, of])

        here = products(slice(0, near), slice(0, near))
        there = products(slice(near, width), slice(near, width))
        for mat in range(2):
            for place, crossed in enumerate((2, 1, 0, 3)):
                to = slice(place * part, (place + 1) * part)
                total = here[mat][:, to] + there[mat][:, crossed * part : (crossed + 1) * part]
                ref = send_ref if place < 2 else keep_ref
                at = place % 2 * part
                ref[mat, :, at : at + part] = total.astype(ref.dtype)

    @pl.when(step < steps // 2)
    def _():
        run(first_ref)

    @pl.when(step >= steps // 2)
    def _():
        run(second_ref)


def project(gflops, pairs, pieces):
    tokens, width = pairs[0].shape
    tile = min(2 * TILE, tokens)
    steps = tokens // tile
    indices = [index for index, _ in pieces]
    arrays = [array for _, array in pieces]
    columns = arrays[0].shape[3]
    block = pl.BlockSpec((2, tile, columns // 2), lambda i: (0, i, 0))
    out = jax.ShapeDtypeStruct((2, 2 * tokens, columns // 2), jnp.bfloat16)
    return pl.pallas_call(
        functools.partial(project_kernel, indices),
        grid=(2 * steps,),
        in_specs=[
            pl.BlockSpec((tile, width), lambda i: (jnp.minimum(i, steps - 1), 0)),
            pl.BlockSpec((tile, width), lambda i: (jnp.maximum(i - steps, 0), 0)),
            *[pl.BlockSpec(memory_space=pl.ANY)] * len(arrays),
        ],
        out_specs=[block, block],
        out_shape=[out, out],
        scratch_shapes=[
            pltpu.VMEM((2, width // 2, columns), jnp.bfloat16),
            pltpu.SemaphoreType.DMA((len(arrays),)),
        ],
        compiler_params=pltpu.CompilerParams(vmem_limit_bytes=vmem_bytes),
        cost_estimate=pl.CostEstimate(
            flops=int(gflops * 1e9), bytes_accessed=tokens, transcendentals=0
        ),
        name="project",
    )(*pairs, *arrays)


def finish_kernel(keep_ref, received_ref, last_ref, *refs):
    for mat, ref in enumerate(refs[-2:]):
        total = keep_ref[mat].astype(jnp.float32) + received_ref[mat] + last_ref[mat]
        ref[...] = total.astype(ref.dtype)


def finish(chunk, outputs, keep, received, last):
    _, tokens, part = last.shape
    shape = jax.ShapeDtypeStruct((tokens, part * CHUNKS), jnp.bfloat16)
    tile = tokens // 2
    return pl.pallas_call(
        finish_kernel,
        grid=(tokens // tile,),
        in_specs=[
            pl.BlockSpec((2, tile, part), lambda i: (0, i, 1)),
            pl.BlockSpec((2, tile, part), lambda i: (0, i, 0)),
            pl.BlockSpec((2, tile, part), lambda i: (0, i, 0)),
            *[pl.BlockSpec(memory_space=pl.ANY)] * len(outputs),
        ],
        out_specs=[pl.BlockSpec((tile, part), lambda i: (i, chunk))] * 2,
        out_shape=[shape, shape],
        input_output_aliases={3 + i: i for i in range(len(outputs))},
        compiler_params=pltpu.CompilerParams(vmem_limit_bytes=vmem_bytes),
        name="finish",
    )(keep, received, last, *outputs)


def across(block, stage):
    owners, places = lax.axis_size("kv"), lax.axis_size("seq")
    route = []
    for owner in range(owners):
        for place in range(places):
            flip = 1 + (place + stage) % CORES
            route.append((owner * places + place, (owner ^ flip) * places + place))
    return lax.ppermute(block, ("kv", "seq"), route)


def along(block, chips):
    size = lax.axis_size("seq")
    return lax.ppermute(block, "seq", [(i, (i + CORES * chips) % size) for i in range(size)])


def other_core(block):
    return lax.ppermute(block, "seq", [(i, i ^ 1) for i in range(lax.axis_size("seq"))])


def together(*trees):
    return lax.optimization_barrier(trees)


class Gather:
    def __init__(self, mine, chips):
        self.near, self.far = {0: mine}, {}
        self.chips = chips
        self.forward, self.backward = chips // 2, (chips - 1) // 2

    def ahead(self):
        if self.forward:
            self.near[1] = along(self.near[0], 1)

    def behind(self):
        if self.backward:
            self.near[-1] = along(self.near[0], -1)

    def farther_ahead(self):
        for step in range(2, self.forward + 1):
            self.near[step] = along(self.near[step - 1], 1)

    def farther_behind(self):
        for step in range(2, self.backward + 1):
            self.near[-step] = along(self.near[1 - step], -1)

    def exchange(self, joint=True):
        steps = [step for step in sorted(self.near) if step and step not in self.far]
        if not joint:
            self.far.update({step: (0, other_core(self.near[step])) for step in steps})
        elif steps:
            blocks = [self.near[step] for step in steps]
            joined = jnp.concatenate(blocks) if len(blocks) > 1 else blocks[0]
            moved = other_core(joined)
            for index, step in enumerate(steps):
                self.far[step] = (index, moved)

    def pieces(self, chunk, whole):
        steps = [*range(1, self.forward + 1), *range(-self.backward, 0)]
        near = [(0, self.near[step]) for step in [0, *steps]]
        return near + [(chunk, whole)] + [self.far[step] for step in steps]


def body(
    queries, query_tangent, key_value, key_value_tangents, doc_lengths, out_weight, weight_tangent
):
    tokens, width = queries.shape
    head_dim = key_value.shape[2]
    heads = width // head_dim
    half = tokens // 2
    seq_index = lax.axis_index("seq")
    kv_index = lax.axis_index("kv")
    seq_size = lax.axis_size("seq")
    chips = seq_size // CORES

    core = seq_index % CORES
    flips = jnp.stack([1 + core, 3 + 0 * core, 2 - core, 0 * core])
    whole, *mine = arrange((kv_index ^ flips).astype(jnp.int32), weight_tangent, out_weight)
    gathers = [Gather(block, chips) for block in mine]
    gathers[0].behind()
    gathers[0].ahead()
    gathers[1].ahead()
    whole = other_core(whole)

    key_value, key_value_tangents, _ = lax.optimization_barrier(
        (key_value, key_value_tangents, mine[0])
    )
    stacked = jnp.concatenate(
        [key_value[:, 0], key_value_tangents[:, 0], key_value[:, 1], key_value_tangents[:, 1]],
        axis=1,
    )
    prior = lax.ppermute(
        stacked[tokens - WINDOW :], "seq", [(i, i + 1) for i in range(seq_size - 1)]
    )

    doc_ends = jnp.cumsum(doc_lengths)
    doc_starts = doc_ends - doc_lengths
    position = seq_index * tokens + jnp.arange(tokens, dtype=jnp.int32)
    inside = (doc_starts[None, :] <= position[:, None]) & (position[:, None] < doc_ends[None, :])
    doc_first = jnp.sum(jnp.where(inside, doc_starts[None, :], 0), axis=1)
    lower = jnp.maximum(doc_first, position - WINDOW + 1)
    low = lower - (position // STRETCH * STRETCH - WINDOW)
    low = jnp.broadcast_to(low[:, None], (tokens, 128))

    step = jnp.arange(chips, dtype=jnp.int32)
    chip = seq_index // CORES
    owner = (chip - step + chips) % chips * CORES
    order = jnp.concatenate([owner + core, owner + 1 - core])
    whole_heads = order.shape[0] == heads

    def attend(part, context):
        heads_order = order if whole_heads else jnp.arange(heads, dtype=jnp.int32)
        pair = attention(part, heads_order, queries, query_tangent, context, low)
        if not whole_heads:
            pair = jnp.take(pair.reshape(half, 2, seq_size, -1), order, axis=2)
            pair = pair.reshape(half, 2 * width)
        return pair

    part = out_weight.shape[1] // CHUNKS // lax.axis_size("kv")

    def add_stage(keep, received):
        total = keep[:, :, :part].astype(jnp.float32) + received[:, :, part:]
        return total.astype(jnp.bfloat16)

    def settle(*others):
        states = [
            (gathering.near, {step: far[1] for step, far in gathering.far.items()})
            for gathering in gathers
        ]
        states, *others = together(states, *others)
        for gathering, (near, far) in zip(gathers, states):
            gathering.near = dict(near)
            gathering.far = {step: (gathering.far[step][0], far[step]) for step in far}
        return others

    pair_second = attend(1, stacked)
    pair_second, prior, whole = settle(pair_second, prior, whole)
    gathers[0].exchange(False)
    gathers[1].exchange()
    gathers[0].farther_ahead()
    gathers[0].farther_behind()
    gathers[2].ahead()
    pair_first = attend(0, jnp.concatenate([prior, stacked[:half]], axis=0))

    pairs, send, sums = (pair_first, pair_second), (), ()
    kept, received, last, outputs = [], [], [], ()
    for chunk in range(CHUNKS):
        pairs, whole, send, sums = settle(pairs, whole, send, sums)
        gathers[chunk].exchange(chunk < CHUNKS - 1)
        first = chunk + 1 + (chunk == 0)
        if chunk != 1 and first < CHUNKS:
            gathers[first].exchange()
        if chunk + 1 < CHUNKS:
            if chunk + 2 < CHUNKS:
                gathers[chunk + 1].behind()
                gathers[chunk + 1].farther_behind()
            gathers[chunk + 1].farther_ahead()
        if 0 < chunk < CHUNKS - 2:
            gathers[chunk + 2].ahead()
        send, keep = project(
            SCHEDULED_GFLOPS[chunk], pairs, gathers[chunk].pieces(chunk, whole)
        )
        kept.append(keep)
        if chunk == CHUNKS - 2:
            final = gathers[chunk + 1]
            final.near[0], send = together(final.near[0], send)
            final.behind()
            final.farther_behind()
        if chunk >= 2:
            last[chunk - 2], send = together(last[chunk - 2], send)
        received.append(across(send, 0))
        if chunk:
            received[chunk - 1], send = together(received[chunk - 1], send)
            sums = add_stage(kept[chunk - 1], received[chunk - 1])
            last.append(across(sums, 1))
            if chunk >= 2:
                outputs = finish(
                    chunk - 2, outputs, kept[chunk - 2], received[chunk - 2], last[chunk - 2]
                )
    last.append(across(add_stage(kept[-1], received[-1]), 1))
    for chunk in range(max(CHUNKS - 2, 0), CHUNKS):
        outputs = finish(chunk, outputs, kept[chunk], received[chunk], last[chunk])
    return tuple(outputs)


def solution(mesh):
    in_specs = (
        P("seq", "kv"),
        P("seq", "kv"),
        P("seq", None, "kv"),
        P("seq", None, "kv"),
        P(),
        P(("kv", "seq"), None),
        P(("kv", "seq"), None),
    )
    out_specs = (P("seq", "kv"), P("seq", "kv"))
    return jax.shard_map(body, mesh=mesh, in_specs=in_specs, out_specs=out_specs, check_vma=False)
```

```python
import functools
import math

import jax
import jax.numpy as jnp
from jax import lax
from jax.experimental import pallas as pl
from jax.experimental.pallas import tpu as pltpu
from jax.sharding import PartitionSpec as P

STRETCH = 32
WINDOW = 224
CHUNKS = 4
SCHEDULED_GFLOPS = (3, 3, 1.5, 0.01)
TILE = 128
CORES = 2

masked_score = -1e30
vmem_bytes = 12 * 1024 * 1024


def arrange_kernel(owner_ref, tangent_ref, value_ref, whole_ref, *chunk_refs):
    owners = owner_ref.shape[0]
    columns = tangent_ref.shape[1] // owners
    part = columns // len(chunk_refs)
    for chunk, chunk_ref in enumerate(chunk_refs):
        for place in range(owners):
            start = pl.multiple_of(owner_ref[place] * columns + chunk * part, part)
            to = slice(place * part, (place + 1) * part)
            for mat, ref in enumerate((tangent_ref, value_ref)):
                block = ref[:, pl.ds(start, part)]
                whole_ref[chunk, mat, :, to] = block
                chunk_ref[0, mat, :, to] = block


def arrange(owners, tangent, value):
    rows, columns = value.shape
    shapes = [
        jax.ShapeDtypeStruct((count, 2, rows, columns // CHUNKS), value.dtype)
        for count in [CHUNKS] + [1] * CHUNKS
    ]
    return pl.pallas_call(
        arrange_kernel,
        in_specs=[pl.BlockSpec(memory_space=pltpu.SMEM)]
        + [pl.BlockSpec(memory_space=pltpu.VMEM)] * 2,
        out_specs=[pl.BlockSpec(memory_space=pltpu.VMEM)] * len(shapes),
        out_shape=shapes,
        compiler_params=pltpu.CompilerParams(vmem_limit_bytes=vmem_bytes),
        name="arrange",
    )(owners, tangent, value)


def attention_kernel(heads, head_dim, offset, order_ref, q_ref, qt_ref, ctx_ref, low_ref, out_ref):
    rows = q_ref.shape[0]
    span = WINDOW + STRETCH
    width = heads * head_dim
    score_scale = 1.0 / math.sqrt(head_dim)
    to_log2 = score_scale * math.log2(math.e)
    step = pl.program_id(0)
    transposed = (((1,), (1,)), ((), ()))
    column = lax.broadcasted_iota(jnp.int32, (STRETCH, span), 1)
    row = lax.broadcasted_iota(jnp.int32, (STRETCH, span), 0)
    causal = column <= row + WINDOW
    starts = [pl.multiple_of(order_ref[h] * head_dim, head_dim) for h in range(heads)]

    def window(part):
        return pl.ds(pl.multiple_of(offset + step * rows + part * STRETCH, STRETCH), span)

    def score(part):
        here = slice(part * STRETCH, (part + 1) * STRETCH)
        keys = ctx_ref[window(part), : 2 * head_dim]
        q = jnp.concatenate([q_ref[here, pl.ds(start, head_dim)] for start in starts], axis=0)
        qt = jnp.concatenate([qt_ref[here, pl.ds(start, head_dim)] for start in starts], axis=0)
        scores = lax.dot_general(
            q, keys[:, :head_dim], transposed, preferred_element_type=jnp.float32
        )
        tangent = lax.dot_general(
            jnp.concatenate([qt, q], axis=1), keys, transposed, preferred_element_type=jnp.float32
        )
        return scores.reshape(heads, STRETCH, span), tangent.reshape(heads, STRETCH, span)

    def weigh(part, scores, tangent):
        low = low_ref[part * STRETCH : (part + 1) * STRETCH, :]
        low = jnp.concatenate([low] * (span // low.shape[1]), axis=1)
        admitted = causal & (column >= low)
        scores = jnp.where(admitted[None], scores, masked_score)
        peak = jnp.max(scores, axis=-1, keepdims=True)
        exponent = jnp.exp2((scores - peak) * to_log2)
        inverse = 1.0 / jnp.sum(exponent, axis=-1, keepdims=True)
        mean = jnp.sum(exponent * tangent, axis=-1, keepdims=True) * inverse
        prob = exponent * inverse
        prob_low = prob.astype(jnp.bfloat16).reshape(heads * STRETCH, span)
        tan_low = (prob * ((tangent - mean) * score_scale)).astype(jnp.bfloat16)
        return prob_low, tan_low.reshape(heads * STRETCH, span)

    def gather_values(part, prob_low, tan_low):
        here = slice(part * STRETCH, (part + 1) * STRETCH)
        values = ctx_ref[window(part), 2 * head_dim :]
        both = jnp.dot(prob_low, values, preferred_element_type=jnp.float32)
        more = jnp.dot(tan_low, values[:, :head_dim], preferred_element_type=jnp.float32)
        out = both[:, :head_dim].astype(jnp.bfloat16)
        out_tan = (both[:, head_dim:] + more).astype(jnp.bfloat16)
        for h in range(heads):
            of = slice(h * STRETCH, (h + 1) * STRETCH)
            out_ref[here, h * head_dim : (h + 1) * head_dim] = out[of]
            out_ref[here, width + h * head_dim : width + (h + 1) * head_dim] = out_tan[of]

    parts = rows // STRETCH
    scored, weighed = score(0), None
    for part in range(parts):
        following = score(part + 1) if part + 1 < parts else None
        if weighed is not None:
            gather_values(part - 1, *weighed)
        weighed = weigh(part, *scored)
        scored = following
    gather_values(parts - 1, *weighed)


def attention(half, order, queries, query_tangent, context, low):
    tokens, width = queries.shape[0] // 2, queries.shape[1]
    head_dim = context.shape[1] // 4
    heads = width // head_dim
    elements = tokens * heads * (WINDOW + STRETCH)
    steps = tokens // TILE
    offset = context.shape[0] - tokens - WINDOW
    return pl.pallas_call(
        functools.partial(attention_kernel, heads, head_dim, offset),
        grid=(steps,),
        in_specs=[
            pl.BlockSpec(memory_space=pltpu.SMEM),
            pl.BlockSpec((TILE, width), lambda i: (half * steps + i, 0)),
            pl.BlockSpec((TILE, width), lambda i: (half * steps + i, 0)),
            pl.BlockSpec(context.shape, lambda i: (0, 0)),
            pl.BlockSpec((TILE, low.shape[1]), lambda i: (half * steps + i, 0)),
        ],
        out_specs=pl.BlockSpec((TILE, 2 * width), lambda i: (i, 0)),
        out_shape=jax.ShapeDtypeStruct((tokens, 2 * width), jnp.bfloat16),
        compiler_params=pltpu.CompilerParams(vmem_limit_bytes=vmem_bytes),
        cost_estimate=pl.CostEstimate(
            flops=elements, bytes_accessed=tokens, transcendentals=0
        ),
        name="attention",
    )(order, queries, query_tangent, context, low)


def project_kernel(indices, first_ref, second_ref, *refs):
    *piece_refs, send_ref, keep_ref, weight_ref, sems = refs
    step, steps = pl.program_id(0), pl.num_programs(0)
    width, columns = weight_ref.shape[1:]
    rows = width // len(indices)
    near = width // 2
    part = columns // 4

    @pl.when(step == 0)
    def _():
        copies = []
        for place, (index, ref) in enumerate(zip(indices, piece_refs)):
            target = weight_ref.at[:, pl.ds(place * rows, rows), :]
            copies.append(pltpu.make_async_copy(ref.at[index], target, sems.at[place]))
            copies[-1].start()
        for copy in copies:
            copy.wait()

    def run(pair_ref):
        dot = functools.partial(jnp.dot, preferred_element_type=jnp.float32)

        def products(mine, of):
            return dot(pair_ref[:, mine], weight_ref[1, of]), dot(
                pair_ref[:, mine], weight_ref[0, of]
            ) + dot(pair_ref[:, slice(width + mine.start, width + mine.stop)], weight_ref[1, of])

        here = products(slice(0, near), slice(0, near))
        there = products(slice(near, width), slice(near, width))
        for mat in range(2):
            for place, crossed in enumerate((2, 1, 0, 3)):
                to = slice(place * part, (place + 1) * part)
                total = here[mat][:, to] + there[mat][:, crossed * part : (crossed + 1) * part]
                ref = send_ref if place < 2 else keep_ref
                at = place % 2 * part
                ref[mat, :, at : at + part] = total.astype(ref.dtype)

    @pl.when(step < steps // 2)
    def _():
        run(first_ref)

    @pl.when(step >= steps // 2)
    def _():
        run(second_ref)


def project(gflops, pairs, pieces):
    tokens, width = pairs[0].shape
    tile = min(2 * TILE, tokens)
    steps = tokens // tile
    indices = [index for index, _ in pieces]
    arrays = [array for _, array in pieces]
    columns = arrays[0].shape[3]
    block = pl.BlockSpec((2, tile, columns // 2), lambda i: (0, i, 0))
    out = jax.ShapeDtypeStruct((2, 2 * tokens, columns // 2), jnp.bfloat16)
    return pl.pallas_call(
        functools.partial(project_kernel, indices),
        grid=(2 * steps,),
        in_specs=[
            pl.BlockSpec((tile, width), lambda i: (jnp.minimum(i, steps - 1), 0)),
            pl.BlockSpec((tile, width), lambda i: (jnp.maximum(i - steps, 0), 0)),
            *[pl.BlockSpec(memory_space=pl.ANY)] * len(arrays),
        ],
        out_specs=[block, block],
        out_shape=[out, out],
        scratch_shapes=[
            pltpu.VMEM((2, width // 2, columns), jnp.bfloat16),
            pltpu.SemaphoreType.DMA((len(arrays),)),
        ],
        compiler_params=pltpu.CompilerParams(vmem_limit_bytes=vmem_bytes),
        cost_estimate=pl.CostEstimate(
            flops=int(gflops * 1e9), bytes_accessed=tokens, transcendentals=0
        ),
        name="project",
    )(*pairs, *arrays)


def finish_kernel(keep_ref, received_ref, last_ref, *refs):
    for mat, ref in enumerate(refs[-2:]):
        total = keep_ref[mat].astype(jnp.float32) + received_ref[mat] + last_ref[mat]
        ref[...] = total.astype(ref.dtype)


def finish(chunk, outputs, keep, received, last):
    _, tokens, part = last.shape
    shape = jax.ShapeDtypeStruct((tokens, part * CHUNKS), jnp.bfloat16)
    tile = tokens // 2
    return pl.pallas_call(
        finish_kernel,
        grid=(tokens // tile,),
        in_specs=[
            pl.BlockSpec((2, tile, part), lambda i: (0, i, 1)),
            pl.BlockSpec((2, tile, part), lambda i: (0, i, 0)),
            pl.BlockSpec((2, tile, part), lambda i: (0, i, 0)),
            *[pl.BlockSpec(memory_space=pl.ANY)] * len(outputs),
        ],
        out_specs=[pl.BlockSpec((tile, part), lambda i: (i, chunk))] * 2,
        out_shape=[shape, shape],
        input_output_aliases={3 + i: i for i in range(len(outputs))},
        compiler_params=pltpu.CompilerParams(vmem_limit_bytes=vmem_bytes),
        name="finish",
    )(keep, received, last, *outputs)


def across(block, stage):
    owners, places = lax.axis_size("kv"), lax.axis_size("seq")
    route = []
    for owner in range(owners):
        for place in range(places):
            flip = 1 + (place + stage) % CORES
            route.append((owner * places + place, (owner ^ flip) * places + place))
    return lax.ppermute(block, ("kv", "seq"), route)


def along(block, chips):
    size = lax.axis_size("seq")
    return lax.ppermute(block, "seq", [(i, (i + CORES * chips) % size) for i in range(size)])


def other_core(block):
    return lax.ppermute(block, "seq", [(i, i ^ 1) for i in range(lax.axis_size("seq"))])


def together(*trees):
    return lax.optimization_barrier(trees)


class Gather:
    def __init__(self, mine, chips):
        self.near, self.far = {0: mine}, {}
        self.chips = chips
        self.forward, self.backward = chips // 2, (chips - 1) // 2

    def ahead(self):
        if self.forward:
            self.near[1] = along(self.near[0], 1)

    def behind(self):
        if self.backward:
            self.near[-1] = along(self.near[0], -1)

    def farther(self):
        for step in range(2, self.forward + 1):
            self.near[step] = along(self.near[step - 1], 1)
        for step in range(2, self.backward + 1):
            self.near[-step] = along(self.near[1 - step], -1)

    def exchange(self, joint=True):
        steps = [step for step in sorted(self.near) if step and step not in self.far]
        if not joint:
            self.far.update({step: (0, other_core(self.near[step])) for step in steps})
        elif steps:
            blocks = [self.near[step] for step in steps]
            joined = jnp.concatenate(blocks) if len(blocks) > 1 else blocks[0]
            moved = other_core(joined)
            for index, step in enumerate(steps):
                self.far[step] = (index, moved)

    def pieces(self, chunk, whole):
        steps = [*range(1, self.forward + 1), *range(-self.backward, 0)]
        near = [(0, self.near[step]) for step in [0, *steps]]
        return near + [(chunk, whole)] + [self.far[step] for step in steps]


def body(
    queries, query_tangent, key_value, key_value_tangents, doc_lengths, out_weight, weight_tangent
):
    tokens, width = queries.shape
    head_dim = key_value.shape[2]
    heads = width // head_dim
    half = tokens // 2
    seq_index = lax.axis_index("seq")
    kv_index = lax.axis_index("kv")
    seq_size = lax.axis_size("seq")
    chips = seq_size // CORES

    core = seq_index % CORES
    flips = jnp.stack([1 + core, 3 + 0 * core, 2 - core, 0 * core])
    whole, *mine = arrange((kv_index ^ flips).astype(jnp.int32), weight_tangent, out_weight)
    gathers = [Gather(block, chips) for block in mine]
    gathers[0].behind()
    gathers[0].ahead()
    gathers[1].ahead()
    whole = other_core(whole)

    key_value, key_value_tangents, _ = lax.optimization_barrier(
        (key_value, key_value_tangents, mine[0])
    )
    stacked = jnp.concatenate(
        [key_value[:, 0], key_value_tangents[:, 0], key_value[:, 1], key_value_tangents[:, 1]],
        axis=1,
    )
    prior = lax.ppermute(
        stacked[tokens - WINDOW :], "seq", [(i, i + 1) for i in range(seq_size - 1)]
    )

    doc_ends = jnp.cumsum(doc_lengths)
    doc_starts = doc_ends - doc_lengths
    position = seq_index * tokens + jnp.arange(tokens, dtype=jnp.int32)
    inside = (doc_starts[None, :] <= position[:, None]) & (position[:, None] < doc_ends[None, :])
    doc_first = jnp.sum(jnp.where(inside, doc_starts[None, :], 0), axis=1)
    lower = jnp.maximum(doc_first, position - WINDOW + 1)
    low = lower - (position // STRETCH * STRETCH - WINDOW)
    low = jnp.broadcast_to(low[:, None], (tokens, 128))

    step = jnp.arange(chips, dtype=jnp.int32)
    chip = seq_index // CORES
    owner = (chip - step + chips) % chips * CORES
    order = jnp.concatenate([owner + core, owner + 1 - core])
    whole_heads = order.shape[0] == heads

    def attend(part, context):
        heads_order = order if whole_heads else jnp.arange(heads, dtype=jnp.int32)
        pair = attention(part, heads_order, queries, query_tangent, context, low)
        if not whole_heads:
            pair = jnp.take(pair.reshape(half, 2, seq_size, -1), order, axis=2)
            pair = pair.reshape(half, 2 * width)
        return pair

    part = out_weight.shape[1] // CHUNKS // lax.axis_size("kv")

    def add_stage(keep, received):
        total = keep[:, :, :part].astype(jnp.float32) + received[:, :, part:]
        return total.astype(jnp.bfloat16)

    def settle(*others):
        states = [
            (gathering.near, {step: far[1] for step, far in gathering.far.items()})
            for gathering in gathers
        ]
        states, *others = together(states, *others)
        for gathering, (near, far) in zip(gathers, states):
            gathering.near = dict(near)
            gathering.far = {step: (gathering.far[step][0], far[step]) for step in far}
        return others

    pair_second = attend(1, stacked)
    pair_second, prior, whole = settle(pair_second, prior, whole)
    gathers[0].exchange(False)
    gathers[1].exchange()
    gathers[0].farther()
    gathers[2].ahead()
    pair_first = attend(0, jnp.concatenate([prior, stacked[:half]], axis=0))

    pairs, send, sums = (pair_first, pair_second), (), ()
    kept, received, last, outputs = [], [], [], ()
    for chunk in range(CHUNKS):
        pairs, whole, send, sums = settle(pairs, whole, send, sums)
        gathers[chunk].exchange(chunk < CHUNKS - 1)
        if chunk == 0 and CHUNKS > 2:
            gathers[2].exchange()
        if chunk + 1 < CHUNKS:
            gathers[chunk + 1].behind()
            gathers[chunk + 1].farther()
        if 0 < chunk < CHUNKS - 2:
            gathers[chunk + 2].ahead()
        send, keep = project(
            SCHEDULED_GFLOPS[chunk], pairs, gathers[chunk].pieces(chunk, whole)
        )
        kept.append(keep)
        if chunk >= 2:
            last[chunk - 2], send = together(last[chunk - 2], send)
        received.append(across(send, 0))
        if chunk:
            received[chunk - 1], send = together(received[chunk - 1], send)
            sums = add_stage(kept[chunk - 1], received[chunk - 1])
            last.append(across(sums, 1))
            if chunk >= 2:
                outputs = finish(
                    chunk - 2, outputs, kept[chunk - 2], received[chunk - 2], last[chunk - 2]
                )
    last.append(across(add_stage(kept[-1], received[-1]), 1))
    for chunk in range(max(CHUNKS - 2, 0), CHUNKS):
        outputs = finish(chunk, outputs, kept[chunk], received[chunk], last[chunk])
    return tuple(outputs)


def solution(mesh):
    in_specs = (
        P("seq", "kv"),
        P("seq", "kv"),
        P("seq", None, "kv"),
        P("seq", None, "kv"),
        P(),
        P(("kv", "seq"), None),
        P(("kv", "seq"), None),
    )
    out_specs = (P("seq", "kv"), P("seq", "kv"))
    return jax.shard_map(body, mesh=mesh, in_specs=in_specs, out_specs=out_specs, check_vma=False)
```

```python
import functools
import math

import jax
import jax.numpy as jnp
from jax import lax
from jax.experimental import pallas as pl
from jax.experimental.pallas import tpu as pltpu
from jax.sharding import PartitionSpec as P

STRETCH = 32
WINDOW = 224
CHUNKS = 4
SCHEDULED_GFLOPS = (3, 3, 1.5, 0.01)
TILE = 128
CORES = 2

masked_score = -1e30
vmem_bytes = 12 * 1024 * 1024


def arrange_kernel(owner_ref, tangent_ref, value_ref, whole_ref, *chunk_refs):
    owners = owner_ref.shape[0]
    columns = tangent_ref.shape[1] // owners
    part = columns // len(chunk_refs)
    for chunk, chunk_ref in enumerate(chunk_refs):
        for place in range(owners):
            start = pl.multiple_of(owner_ref[place] * columns + chunk * part, part)
            to = slice(place * part, (place + 1) * part)
            for mat, ref in enumerate((tangent_ref, value_ref)):
                block = ref[:, pl.ds(start, part)]
                whole_ref[chunk, mat, :, to] = block
                chunk_ref[0, mat, :, to] = block


def arrange(owners, tangent, value):
    rows, columns = value.shape
    shapes = [
        jax.ShapeDtypeStruct((count, 2, rows, columns // CHUNKS), value.dtype)
        for count in [CHUNKS] + [1] * CHUNKS
    ]
    return pl.pallas_call(
        arrange_kernel,
        in_specs=[pl.BlockSpec(memory_space=pltpu.SMEM)]
        + [pl.BlockSpec(memory_space=pltpu.VMEM)] * 2,
        out_specs=[pl.BlockSpec(memory_space=pltpu.VMEM)] * len(shapes),
        out_shape=shapes,
        compiler_params=pltpu.CompilerParams(vmem_limit_bytes=vmem_bytes),
        name="arrange",
    )(owners, tangent, value)


def attention_kernel(heads, head_dim, offset, order_ref, q_ref, qt_ref, ctx_ref, low_ref, out_ref):
    rows = q_ref.shape[0]
    span = WINDOW + STRETCH
    width = heads * head_dim
    score_scale = 1.0 / math.sqrt(head_dim)
    to_log2 = score_scale * math.log2(math.e)
    step = pl.program_id(0)
    transposed = (((1,), (1,)), ((), ()))
    column = lax.broadcasted_iota(jnp.int32, (STRETCH, span), 1)
    row = lax.broadcasted_iota(jnp.int32, (STRETCH, span), 0)
    causal = column <= row + WINDOW
    starts = [pl.multiple_of(order_ref[h] * head_dim, head_dim) for h in range(heads)]

    def window(part):
        return pl.ds(pl.multiple_of(offset + step * rows + part * STRETCH, STRETCH), span)

    def score(part):
        here = slice(part * STRETCH, (part + 1) * STRETCH)
        keys = ctx_ref[window(part), : 2 * head_dim]
        q = jnp.concatenate([q_ref[here, pl.ds(start, head_dim)] for start in starts], axis=0)
        qt = jnp.concatenate([qt_ref[here, pl.ds(start, head_dim)] for start in starts], axis=0)
        scores = lax.dot_general(
            q, keys[:, :head_dim], transposed, preferred_element_type=jnp.float32
        )
        tangent = lax.dot_general(
            jnp.concatenate([qt, q], axis=1), keys, transposed, preferred_element_type=jnp.float32
        )
        return scores.reshape(heads, STRETCH, span), tangent.reshape(heads, STRETCH, span)

    def weigh(part, scores, tangent):
        low = low_ref[part * STRETCH : (part + 1) * STRETCH, :]
        low = jnp.concatenate([low] * (span // low.shape[1]), axis=1)
        admitted = causal & (column >= low)
        scores = jnp.where(admitted[None], scores, masked_score)
        peak = jnp.max(scores, axis=-1, keepdims=True)
        exponent = jnp.exp2((scores - peak) * to_log2)
        inverse = 1.0 / jnp.sum(exponent, axis=-1, keepdims=True)
        mean = jnp.sum(exponent * tangent, axis=-1, keepdims=True) * inverse
        prob = exponent * inverse
        prob_low = prob.astype(jnp.bfloat16).reshape(heads * STRETCH, span)
        tan_low = (prob * ((tangent - mean) * score_scale)).astype(jnp.bfloat16)
        return prob_low, tan_low.reshape(heads * STRETCH, span)

    def gather_values(part, prob_low, tan_low):
        here = slice(part * STRETCH, (part + 1) * STRETCH)
        values = ctx_ref[window(part), 2 * head_dim :]
        both = jnp.dot(prob_low, values, preferred_element_type=jnp.float32)
        more = jnp.dot(tan_low, values[:, :head_dim], preferred_element_type=jnp.float32)
        out = both[:, :head_dim].astype(jnp.bfloat16)
        out_tan = (both[:, head_dim:] + more).astype(jnp.bfloat16)
        for h in range(heads):
            of = slice(h * STRETCH, (h + 1) * STRETCH)
            out_ref[here, h * head_dim : (h + 1) * head_dim] = out[of]
            out_ref[here, width + h * head_dim : width + (h + 1) * head_dim] = out_tan[of]

    parts = rows // STRETCH
    scored, weighed = score(0), None
    for part in range(parts):
        following = score(part + 1) if part + 1 < parts else None
        if weighed is not None:
            gather_values(part - 1, *weighed)
        weighed = weigh(part, *scored)
        scored = following
    gather_values(parts - 1, *weighed)


def attention(half, order, queries, query_tangent, context, low):
    tokens, width = queries.shape[0] // 2, queries.shape[1]
    head_dim = context.shape[1] // 4
    heads = width // head_dim
    elements = tokens * heads * (WINDOW + STRETCH)
    steps = tokens // TILE
    offset = context.shape[0] - tokens - WINDOW
    return pl.pallas_call(
        functools.partial(attention_kernel, heads, head_dim, offset),
        grid=(steps,),
        in_specs=[
            pl.BlockSpec(memory_space=pltpu.SMEM),
            pl.BlockSpec((TILE, width), lambda i: (half * steps + i, 0)),
            pl.BlockSpec((TILE, width), lambda i: (half * steps + i, 0)),
            pl.BlockSpec(context.shape, lambda i: (0, 0)),
            pl.BlockSpec((TILE, low.shape[1]), lambda i: (half * steps + i, 0)),
        ],
        out_specs=pl.BlockSpec((TILE, 2 * width), lambda i: (i, 0)),
        out_shape=jax.ShapeDtypeStruct((tokens, 2 * width), jnp.bfloat16),
        compiler_params=pltpu.CompilerParams(vmem_limit_bytes=vmem_bytes),
        cost_estimate=pl.CostEstimate(
            flops=elements, bytes_accessed=tokens, transcendentals=0
        ),
        name="attention",
    )(order, queries, query_tangent, context, low)


def project_kernel(indices, first_ref, second_ref, *refs):
    *piece_refs, send_ref, keep_ref, weight_ref, sems = refs
    step, steps = pl.program_id(0), pl.num_programs(0)
    width, columns = weight_ref.shape[1:]
    rows = width // len(indices)
    near = width // 2
    part = columns // 4

    @pl.when(step == 0)
    def _():
        copies = []
        for place, (index, ref) in enumerate(zip(indices, piece_refs)):
            target = weight_ref.at[:, pl.ds(place * rows, rows), :]
            copies.append(pltpu.make_async_copy(ref.at[index], target, sems.at[place]))
            copies[-1].start()
        for copy in copies:
            copy.wait()

    def run(pair_ref):
        dot = functools.partial(jnp.dot, preferred_element_type=jnp.float32)

        def products(mine, of):
            return dot(pair_ref[:, mine], weight_ref[1, of]), dot(
                pair_ref[:, mine], weight_ref[0, of]
            ) + dot(pair_ref[:, slice(width + mine.start, width + mine.stop)], weight_ref[1, of])

        here = products(slice(0, near), slice(0, near))
        there = products(slice(near, width), slice(near, width))
        for mat in range(2):
            for place, crossed in enumerate((2, 1, 0, 3)):
                to = slice(place * part, (place + 1) * part)
                total = here[mat][:, to] + there[mat][:, crossed * part : (crossed + 1) * part]
                ref = send_ref if place < 2 else keep_ref
                at = place % 2 * part
                ref[mat, :, at : at + part] = total.astype(ref.dtype)

    @pl.when(step < steps // 2)
    def _():
        run(first_ref)

    @pl.when(step >= steps // 2)
    def _():
        run(second_ref)


def project(gflops, pairs, pieces):
    tokens, width = pairs[0].shape
    tile = min(4 * TILE, tokens)
    steps = tokens // tile
    indices = [index for index, _ in pieces]
    arrays = [array for _, array in pieces]
    columns = arrays[0].shape[3]
    block = pl.BlockSpec((2, tile, columns // 2), lambda i: (0, i, 0))
    out = jax.ShapeDtypeStruct((2, 2 * tokens, columns // 2), jnp.bfloat16)
    return pl.pallas_call(
        functools.partial(project_kernel, indices),
        grid=(2 * steps,),
        in_specs=[
            pl.BlockSpec((tile, width), lambda i: (jnp.minimum(i, steps - 1), 0)),
            pl.BlockSpec((tile, width), lambda i: (jnp.maximum(i - steps, 0), 0)),
            *[pl.BlockSpec(memory_space=pl.ANY)] * len(arrays),
        ],
        out_specs=[block, block],
        out_shape=[out, out],
        scratch_shapes=[
            pltpu.VMEM((2, width // 2, columns), jnp.bfloat16),
            pltpu.SemaphoreType.DMA((len(arrays),)),
        ],
        compiler_params=pltpu.CompilerParams(vmem_limit_bytes=2 * vmem_bytes),
        cost_estimate=pl.CostEstimate(
            flops=int(gflops * 1e9), bytes_accessed=tokens, transcendentals=0
        ),
        name="project",
    )(*pairs, *arrays)


def finish_kernel(keep_ref, received_ref, last_ref, *refs):
    for mat, ref in enumerate(refs[-2:]):
        total = keep_ref[mat].astype(jnp.float32) + received_ref[mat] + last_ref[mat]
        ref[...] = total.astype(ref.dtype)


def finish(chunk, outputs, keep, received, last):
    _, tokens, part = last.shape
    shape = jax.ShapeDtypeStruct((tokens, part * CHUNKS), jnp.bfloat16)
    tile = tokens // 2
    return pl.pallas_call(
        finish_kernel,
        grid=(tokens // tile,),
        in_specs=[
            pl.BlockSpec((2, tile, part), lambda i: (0, i, 1)),
            pl.BlockSpec((2, tile, part), lambda i: (0, i, 0)),
            pl.BlockSpec((2, tile, part), lambda i: (0, i, 0)),
            *[pl.BlockSpec(memory_space=pl.ANY)] * len(outputs),
        ],
        out_specs=[pl.BlockSpec((tile, part), lambda i: (i, chunk))] * 2,
        out_shape=[shape, shape],
        input_output_aliases={3 + i: i for i in range(len(outputs))},
        compiler_params=pltpu.CompilerParams(vmem_limit_bytes=vmem_bytes),
        name="finish",
    )(keep, received, last, *outputs)


def across(block, stage):
    owners, places = lax.axis_size("kv"), lax.axis_size("seq")
    route = []
    for owner in range(owners):
        for place in range(places):
            flip = 1 + (place + stage) % CORES
            route.append((owner * places + place, (owner ^ flip) * places + place))
    return lax.ppermute(block, ("kv", "seq"), route)


def along(block, chips):
    size = lax.axis_size("seq")
    return lax.ppermute(block, "seq", [(i, (i + CORES * chips) % size) for i in range(size)])


def other_core(block):
    return lax.ppermute(block, "seq", [(i, i ^ 1) for i in range(lax.axis_size("seq"))])


def together(*trees):
    return lax.optimization_barrier(trees)


class Gather:
    def __init__(self, mine, chips):
        self.near, self.far = {0: mine}, {}
        self.chips = chips
        self.forward, self.backward = chips // 2, (chips - 1) // 2

    def ahead(self):
        if self.forward:
            self.near[1] = along(self.near[0], 1)

    def behind(self):
        if self.backward:
            self.near[-1] = along(self.near[0], -1)

    def farther(self):
        for step in range(2, self.forward + 1):
            self.near[step] = along(self.near[step - 1], 1)
        for step in range(2, self.backward + 1):
            self.near[-step] = along(self.near[1 - step], -1)

    def exchange(self, joint=True):
        steps = [step for step in sorted(self.near) if step and step not in self.far]
        if not joint:
            self.far.update({step: (0, other_core(self.near[step])) for step in steps})
        elif steps:
            blocks = [self.near[step] for step in steps]
            joined = jnp.concatenate(blocks) if len(blocks) > 1 else blocks[0]
            moved = other_core(joined)
            for index, step in enumerate(steps):
                self.far[step] = (index, moved)

    def pieces(self, chunk, whole):
        steps = [*range(1, self.forward + 1), *range(-self.backward, 0)]
        near = [(0, self.near[step]) for step in [0, *steps]]
        return near + [(chunk, whole)] + [self.far[step] for step in steps]


def body(
    queries, query_tangent, key_value, key_value_tangents, doc_lengths, out_weight, weight_tangent
):
    tokens, width = queries.shape
    head_dim = key_value.shape[2]
    heads = width // head_dim
    half = tokens // 2
    seq_index = lax.axis_index("seq")
    kv_index = lax.axis_index("kv")
    seq_size = lax.axis_size("seq")
    chips = seq_size // CORES

    core = seq_index % CORES
    flips = jnp.stack([1 + core, 3 + 0 * core, 2 - core, 0 * core])
    whole, *mine = arrange((kv_index ^ flips).astype(jnp.int32), weight_tangent, out_weight)
    gathers = [Gather(block, chips) for block in mine]
    gathers[0].behind()
    gathers[0].ahead()
    gathers[1].ahead()
    whole = other_core(whole)

    key_value, key_value_tangents, _ = lax.optimization_barrier(
        (key_value, key_value_tangents, mine[0])
    )
    stacked = jnp.concatenate(
        [key_value[:, 0], key_value_tangents[:, 0], key_value[:, 1], key_value_tangents[:, 1]],
        axis=1,
    )
    prior = lax.ppermute(
        stacked[tokens - WINDOW :], "seq", [(i, i + 1) for i in range(seq_size - 1)]
    )

    doc_ends = jnp.cumsum(doc_lengths)
    doc_starts = doc_ends - doc_lengths
    position = seq_index * tokens + jnp.arange(tokens, dtype=jnp.int32)
    inside = (doc_starts[None, :] <= position[:, None]) & (position[:, None] < doc_ends[None, :])
    doc_first = jnp.sum(jnp.where(inside, doc_starts[None, :], 0), axis=1)
    lower = jnp.maximum(doc_first, position - WINDOW + 1)
    low = lower - (position // STRETCH * STRETCH - WINDOW)
    low = jnp.broadcast_to(low[:, None], (tokens, 128))

    step = jnp.arange(chips, dtype=jnp.int32)
    chip = seq_index // CORES
    owner = (chip - step + chips) % chips * CORES
    order = jnp.concatenate([owner + core, owner + 1 - core])
    whole_heads = order.shape[0] == heads

    def attend(part, context):
        heads_order = order if whole_heads else jnp.arange(heads, dtype=jnp.int32)
        pair = attention(part, heads_order, queries, query_tangent, context, low)
        if not whole_heads:
            pair = jnp.take(pair.reshape(half, 2, seq_size, -1), order, axis=2)
            pair = pair.reshape(half, 2 * width)
        return pair

    part = out_weight.shape[1] // CHUNKS // lax.axis_size("kv")

    def add_stage(keep, received):
        total = keep[:, :, :part].astype(jnp.float32) + received[:, :, part:]
        return total.astype(jnp.bfloat16)

    def settle(*others):
        states = [
            (gathering.near, {step: far[1] for step, far in gathering.far.items()})
            for gathering in gathers
        ]
        states, *others = together(states, *others)
        for gathering, (near, far) in zip(gathers, states):
            gathering.near = dict(near)
            gathering.far = {step: (gathering.far[step][0], far[step]) for step in far}
        return others

    pair_second = attend(1, stacked)
    pair_second, prior, whole = settle(pair_second, prior, whole)
    gathers[0].exchange(False)
    gathers[1].exchange()
    gathers[0].farther()
    gathers[2].ahead()
    pair_first = attend(0, jnp.concatenate([prior, stacked[:half]], axis=0))

    pairs, send, sums = (pair_first, pair_second), (), ()
    kept, received, last, outputs = [], [], [], ()
    for chunk in range(CHUNKS):
        pairs, whole, send, sums = settle(pairs, whole, send, sums)
        gathers[chunk].exchange(chunk < CHUNKS - 1)
        if chunk == 0 and CHUNKS > 2:
            gathers[2].exchange()
        if chunk + 1 < CHUNKS:
            gathers[chunk + 1].behind()
            gathers[chunk + 1].farther()
        if 0 < chunk < CHUNKS - 2:
            gathers[chunk + 2].ahead()
        send, keep = project(
            SCHEDULED_GFLOPS[chunk], pairs, gathers[chunk].pieces(chunk, whole)
        )
        kept.append(keep)
        if chunk >= 2:
            last[chunk - 2], send = together(last[chunk - 2], send)
        received.append(across(send, 0))
        if chunk:
            received[chunk - 1], send = together(received[chunk - 1], send)
            sums = add_stage(kept[chunk - 1], received[chunk - 1])
            last.append(across(sums, 1))
            if chunk >= 2:
                outputs = finish(
                    chunk - 2, outputs, kept[chunk - 2], received[chunk - 2], last[chunk - 2]
                )
    last.append(across(add_stage(kept[-1], received[-1]), 1))
    for chunk in range(max(CHUNKS - 2, 0), CHUNKS):
        outputs = finish(chunk, outputs, kept[chunk], received[chunk], last[chunk])
    return tuple(outputs)


def solution(mesh):
    in_specs = (
        P("seq", "kv"),
        P("seq", "kv"),
        P("seq", None, "kv"),
        P("seq", None, "kv"),
        P(),
        P(("kv", "seq"), None),
        P(("kv", "seq"), None),
    )
    out_specs = (P("seq", "kv"), P("seq", "kv"))
    return jax.shard_map(body, mesh=mesh, in_specs=in_specs, out_specs=out_specs, check_vma=False)
```
